32 devices in a mesh: wave: 8 (over y, x, core), lev: 4 (over z).
Axes of the slice: x: 2, y: 2, z: 4, core: 2. Of those that a mesh axis runs over, the one named last changes fastest.
Arguments:
- spectral: bfloat16 [2, 4, 2, 8, 1280], P(None, 'lev', None, 'wave'), may hold values from -6 to 6
- legendre: bfloat16 [8, 2560, 1280], P('wave'), may hold values from -0.15625 to 0.15625
- wavenumber: int32 [8], replicated, may hold values from 0 to 1279, as said below
Outputs:
- tendency_spec: bfloat16 [2, 4, 2, 8, 1280], P(None, 'lev', None, 'wave')
The draws below stay inside these ranges and needn't reach their ends.
Inputs may be any that keep to these rules, and one draw needn't show every extreme that they name: `wavenumber`: distinct zonal wavenumbers; 0 and 1279 are always among them.
All inputs are finite; a program needn't handle non-finite values.
Results may differ from the reference program's by a relative error of at most 0.006.
Values may be sent and summed in bfloat16 or wider, within the bound.
No kernel may reach another device: no remote copies, remote signals or barrier semaphores. Data moves between devices by JAX's collectives and lax.ppermute only.
A program may use at most 128 MiB of HBM per device.

```python
import math
import jax
import jax.numpy as jnp
from jax import lax

TRUNC = 1279
NLAT = 2560
NN = 1280
LEVELS = 4
MW = 8
LS = 320
BC = 1284
N_WAVE = 8
N_LEV = 4


def draw_wavenumber(key, part):
    inner = jax.random.permutation(jax.random.fold_in(key, 11), TRUNC - 1).astype(jnp.int32) + 1
    picked = jnp.concatenate([jnp.array([0, TRUNC], dtype=jnp.int32), inner[:MW - 2]])
    return jax.random.permutation(jax.random.fold_in(key, 23), picked).astype(jnp.int32)


def steps_of(own_key, dims, cuts, smallest, top_value):
    factor_of = 1.0
    for position, blocks in cuts:
        steps = jax.random.uniform(jax.random.fold_in(jax.random.fold_in(own_key, 6), position), (blocks,), jnp.float32, smallest / len(cuts), top_value / len(cuts))
        factor_of = factor_of * jnp.repeat(jnp.exp(steps), dims[position] // blocks).reshape((-1,) + (1,) * (len(dims) - 1 - position))
    return factor_of


def gaussian(stream_key, extent, deviation, reach, cuts=(), kind=jnp.bfloat16):
    gain = steps_of(stream_key, extent, cuts, -0.22, 0.18) if cuts else 1.0
    values = jax.random.normal(stream_key, extent, jnp.float32) * deviation * gain
    return jnp.minimum(jnp.maximum(values, -reach), reach).astype(kind)


def setup_inputs(seed: int = 0) -> dict:
    splits = jax.random.split(jax.random.key(seed), 4)
    return {
        "spectral": gaussian(splits[0], (2, LEVELS, 2, MW, NN), 1.0, 6.0, ((1, 4), (3, 8))),
        "legendre": gaussian(splits[1], (MW, NLAT, NN), NN ** -0.5, 0.15625, ((0, 8),)),
        "wavenumber": draw_wavenumber(jax.random.fold_in(splits[3], 71), 0),
    }


def circle_tables(latitude, band_index, wavenumber, lat_total, band_total, band_cap, wave_total):
    circle_length = 20 + 4 * jnp.minimum(latitude, lat_total - 1 - latitude)
    band_width = (circle_length + band_total - 1) // band_total
    offsets = jnp.arange(band_cap, dtype=jnp.int32)
    longitude_index = band_index[None, :, None] * band_width[:, None, None] + offsets[None, None, :]
    inside = (offsets[None, None, :] < band_width[:, None, None]) & (longitude_index < circle_length[:, None, None])
    rows = latitude.shape[0]
    longitude_index = longitude_index.reshape(rows, -1)
    inside = inside.reshape(rows, -1)
    phase_index = wavenumber[None, None, :] * longitude_index[:, :, None] % circle_length[:, None, None]
    length_float = circle_length.astype(jnp.float32)
    angles = 2.0 * math.pi * phase_index.astype(jnp.float32) / length_float[:, None, None]
    shown = inside[:, :, None].astype(jnp.float32)
    trig_basis = jnp.stack([jnp.cos(angles) * shown, -jnp.sin(angles) * shown], axis=2)
    colatitude = (latitude.astype(jnp.float32) + 0.5) * (math.pi / lat_total)
    circle_weight = jnp.sin(colatitude) / jnp.sqrt(length_float)
    synth_table = (trig_basis / math.sqrt(wave_total)).astype(jnp.bfloat16)
    analysis_table = (trig_basis * circle_weight[:, None, None, None]).astype(jnp.bfloat16)
    return (synth_table, analysis_table, 2.0 * jnp.cos(colatitude))

def tendencies(grid_values, planetary):
    vorticity = grid_values[0]
    divergence = grid_values[1]
    absolute_vort = vorticity + planetary[None, :, None]
    column_div = lax.optimization_barrier(jnp.sum(divergence, axis=0)) / math.sqrt(divergence.shape[0])
    return jnp.stack([-absolute_vort * divergence, absolute_vort * vorticity - divergence * column_div[None]]).astype(jnp.bfloat16)

def reference(spectral, legendre, wavenumber):
    kept_degrees = jnp.arange(NN, dtype=jnp.int32)[None, :] <= (TRUNC - wavenumber)[:, None]
    masked_spec = jnp.where(kept_degrees, spectral, jnp.zeros_like(spectral))
    legendre_f32 = legendre.astype(jnp.float32)
    fourier = jnp.einsum('flrsn,sjn->flrsj', masked_spec.astype(jnp.float32), legendre_f32).astype(jnp.bfloat16)
    band_index = jnp.arange(N_LEV, dtype=jnp.int32)

    def one_set(set_index):
        latitude = set_index * LS + jnp.arange(LS, dtype=jnp.int32)
        synth_table, analysis_table, planetary = circle_tables(latitude, band_index, wavenumber, NLAT, N_LEV, BC, MW)
        block = lax.dynamic_slice_in_dim(fourier, set_index * LS, LS, 4).astype(jnp.float32)
        grid_values = jnp.einsum('flrsq,qprs->flqp', block, synth_table.astype(jnp.float32))
        tendency = tendencies(grid_values, planetary)
        return jnp.einsum('flqp,qprs->flrsq', tendency.astype(jnp.float32), analysis_table.astype(jnp.float32)).astype(jnp.bfloat16)
    set_blocks = lax.map(one_set, jnp.arange(N_WAVE, dtype=jnp.int32))
    tend_fourier = jnp.moveaxis(set_blocks, 0, 4).reshape(2, LEVELS, 2, MW, NLAT)
    analysed = jnp.einsum('flrsj,sjn->flrsn', tend_fourier.astype(jnp.float32), legendre_f32)
    return jnp.where(kept_degrees, analysed, jnp.zeros_like(analysed)).astype(jnp.bfloat16)
```

```python
import functools
import math

import jax
import jax.numpy as jnp
from jax import lax
from jax.experimental import pallas as pl
from jax.experimental.pallas import tpu as pltpu
from jax.sharding import PartitionSpec as P

SUB = 8
LANES = 128
QUARTERS = 4
FIRST = 5
NT = (((1,), (1,)), ((), ()))
NN = (((1,), (0,)), ((), ()))
F32 = jnp.float32
BF16 = jnp.bfloat16


def dot(a, b, dims):
    return lax.dot_general(a, b, dims, preferred_element_type=F32)


def iota(shape, dim):
    return lax.broadcasted_iota(jnp.int32, shape, dim)


def one_hot(mask):
    return jnp.where(mask, 1.0, 0.0).astype(BF16)


def cos_sin_turns(turns):
    quadrant = jnp.floor(turns * 4.0 + 0.5)
    u = (turns - quadrant * 0.25) * (2.0 * math.pi)
    u2 = u * u
    sine = u * (1.0 + u2 * (-1 / 6 + u2 * (1 / 120 + u2 * (-1 / 5040 + u2 * (1 / 362880)))))
    cosine = 1.0 + u2 * (-0.5 + u2 * (1 / 24 + u2 * (-1 / 720 + u2 * (1 / 40320))))
    quadrant = quadrant.astype(jnp.int32) & 3
    odd = (quadrant & 1) == 1
    c = jnp.where(odd, sine, cosine)
    s = jnp.where(odd, cosine, sine)
    c = jnp.where((quadrant == 1) | (quadrant == 2), -c, c)
    s = jnp.where(quadrant >= 2, -s, s)
    return c, s


def cos_sin_phase(wavenumber, point, circle):
    inverse = 1.0 / circle
    product = wavenumber * point
    whole = jnp.floor(product * inverse + 0.5)
    return cos_sin_turns((product - whole * circle) * inverse)


def quarter_turns(wavenumber, band):
    k = (wavenumber * band) & 3
    c = jnp.where(k == 0, 1.0, jnp.where(k == 2, -1.0, 0.0))
    s = jnp.where(k == 1, 1.0, jnp.where(k == 3, -1.0, 0.0))
    return c, s


def plain_part(group, south):
    return (group % 2 == 0) != south


def block_place(block, groups):
    south = block >= groups
    return (2 * groups - 1 - block if south else block), south


def reverse_matrix(n):
    return one_hot(iota((n, n), 0) + iota((n, n), 1) == n - 1)


def own_wavenumber(wn_ref):
    return wn_ref[lax.axis_index("wave")]


def forward_kernel(groups, wn_ref, spec_ref, leg_ref, out_ref, leg, staged, sems):
    block = leg.shape[1]
    copies = [
        pltpu.make_async_copy(leg_ref.at[0, pl.ds(k * block, block)], leg.at[k], sems.at[k])
        for k in range(2 * groups)
    ]
    for copy in copies:
        copy.start()
    degrees = leg.shape[2]
    kept = iota((1, degrees), 1) <= degrees - 1 - own_wavenumber(wn_ref)
    rows = [
        jnp.where(kept, spec_ref[f, 0, r].astype(F32), 0.0) for f in range(2) for r in range(2)
    ]
    spec = jnp.concatenate(rows + [jnp.zeros((SUB - 4, degrees), F32)], axis=0).astype(BF16)
    staged[...] = jnp.zeros_like(staged)
    for k, copy in enumerate(copies):
        group, south = block_place(k, groups)
        plain = plain_part(group, south)
        copy.wait()
        fourier = dot(spec, leg[k], NT)
        row = (group if plain else groups + group) * SUB
        staged[0 if plain else 1, row : row + SUB, :] = fourier
    identity = one_hot(iota((block, block), 0) == iota((block, block), 1))
    placed = dot(identity, staged[0].astype(BF16), NT) + dot(
        reverse_matrix(block), staged[1].astype(BF16), NT
    )
    out_ref[...] = placed.astype(BF16).reshape(out_ref.shape)


def backward_kernel(groups, wn_ref, leg_ref, got_ref, out_ref, leg, sems):
    block = leg.shape[1]
    copies = [
        pltpu.make_async_copy(leg_ref.at[0, pl.ds(k * block, block)], leg.at[k], sems.at[k])
        for k in range(2 * groups)
    ]
    for copy in copies:
        copy.start()
    degrees = leg.shape[2]
    got = got_ref[...].reshape(block, LANES)
    shape = (groups * SUB, LANES)
    row, lane = iota(shape, 0), iota(shape, 1)
    group, field, part = row // SUB, (row % SUB) // 2, row % 2
    source = group * SUB + part * 4 + field * 2
    used = row % SUB < 4
    odd = group % 2
    plain = dot(one_hot(used & (lane == source + odd)), got, NT).astype(BF16)
    turned = dot(one_hot(used & (lane == source + 1 - odd)), got, NT).astype(BF16)
    turned = dot(turned, reverse_matrix(block), NN).astype(BF16)
    total = jnp.zeros((SUB, degrees), F32)
    for k, copy in enumerate(copies):
        g, south = block_place(k, groups)
        rows = plain if plain_part(g, south) else turned
        copy.wait()
        total = total + dot(rows[g * SUB : (g + 1) * SUB], leg[k], NN)
    kept = iota((1, degrees), 1) <= degrees - 1 - own_wavenumber(wn_ref)
    total = jnp.where(kept, total, 0.0).astype(BF16)
    for f in range(2):
        for r in range(2):
            out_ref[f, 0, r] = total[f * 2 + r : f * 2 + r + 1]


def grid_kernel(groups, waves, levels, lats, step, wn_ref, got_ref, out_ref, coef, planet, total, kept):
    devices = waves * levels
    block = devices * SUB
    half = waves * SUB
    device = lax.axis_index("lev") * waves + lax.axis_index("wave")
    numbers = [wn_ref[s] for s in range(waves)]

    got = got_ref[...].reshape(block, LANES)
    shape = (groups * 4 * SUB, LANES)
    row, lane = iota(shape, 0), iota(shape, 1)
    group, pair, south = row // (4 * SUB), (row // SUB) % 4, row % 2
    turned = (group + south) % 2
    source = turned * (groups * SUB) + group * SUB + pair
    fourier = dot(one_hot(lane == source), got, NT)

    def slot_number(lanes):
        value = jnp.zeros(lanes.shape, jnp.int32)
        for s in range(waves):
            value = jnp.where(lanes == s, numbers[s], value)
        return value

    shape = (SUB, block)
    band, slot = iota(shape, 0) // 2, (iota(shape, 1) // SUB) % waves
    turn_c, turn_s = quarter_turns(slot_number(slot), band)
    shape = (SUB, LANES)
    row, lane = iota(shape, 0), iota(shape, 1)
    back_c, back_s = quarter_turns(slot_number((lane // SUB) % waves), row // 2)
    back_s = jnp.where(lane < half, back_s, -back_s)
    first = lane < half
    which = lane % SUB

    kept[...] = jnp.zeros_like(kept)
    for g in range(groups):
        for f in range(2):
            base = (g * 4 + f * 2) * SUB
            real, imag = fourier[base : base + SUB], fourier[base + SUB : base + 2 * SUB]
            turned_r = real * turn_c - imag * turn_s
            turned_i = real * turn_s + imag * turn_c
            for l in range(levels):
                cut = slice((l // 2) * LANES, (l // 2 + 1) * LANES)
                a, b = turned_r[:, cut], turned_i[:, cut]
                if l % 2 == 0:
                    b = pltpu.roll(b, half, 1)
                else:
                    a = pltpu.roll(a, half, 1)
                both = jnp.where(first, a, b)
                for q in range(0, SUB, 2):
                    place = ((f * levels + l) * SUB + q) * SUB
                    two = jnp.concatenate(
                        [jnp.where(which == q + k, both, 0.0) for k in range(2)], axis=0
                    )
                    coef[place : place + 2 * SUB, :] = two.astype(BF16)

        def latitude(index):
            order = device * SUB + index
            return g * block + (order if g % 2 == 0 else block - 1 - order)

        lat = latitude(iota((SUB, LANES), 0)).astype(F32)
        quarter = lat + FIRST
        circle = QUARTERS * quarter
        weight = cos_sin_turns((lat + 0.5) * (0.5 / lats))[1] / jnp.sqrt(circle)
        row = iota((SUB * SUB, step), 0)
        lat_row = latitude(row // SUB).astype(F32)
        planetary = 2.0 * cos_sin_turns((lat_row + 0.5) * (0.5 / lats))[0]
        planet[...] = jnp.where(row % 2 == 0, planetary, -planetary)

        point = iota((SUB, step), 1)
        wide = jnp.concatenate([circle] * (step // LANES), axis=1)
        start = [cos_sin_phase(numbers[s].astype(F32), point.astype(F32), wide) for s in range(waves)]
        c0 = jnp.concatenate([c for c, _ in start], axis=0)
        n0 = jnp.concatenate([-s for _, s in start], axis=0)
        turn = [cos_sin_phase((numbers[s] * step).astype(F32), 1.0, circle) for s in range(waves)]
        tc = jnp.concatenate([jnp.concatenate([c for c, _ in turn], axis=0)] * (step // LANES), axis=1)
        ts = jnp.concatenate([jnp.concatenate([s for _, s in turn], axis=0)] * (step // LANES), axis=1)
        weights = jnp.concatenate([jnp.concatenate([weight] * (2 * waves), axis=0)] * (step // LANES), axis=1)
        limit = jnp.concatenate([jnp.concatenate([quarter] * (2 * waves), axis=0)] * (step // LANES), axis=1)
        limit = limit.astype(jnp.int32)
        points = iota((2 * half, step), 1)

        total[...] = jnp.zeros_like(total)
        longest = jnp.maximum(latitude(0), latitude(SUB - 1)) + FIRST
        count = (longest + step - 1) // step

        def one_step(i, carry):
            c, n = carry
            basis = jnp.concatenate([c, n], axis=0)
            synth = (basis * (1.0 / math.sqrt(waves))).astype(BF16)
            analysis = jnp.where(points + i * step < limit, basis * weights, 0.0).astype(BF16)
            values = dot(coef[...], synth, NN)
            rows = levels * SUB * SUB
            vort = values[:rows].reshape(levels, SUB * SUB, step)
            div = values[rows:].reshape(levels, SUB * SUB, step)
            column = div[0]
            for l in range(1, levels):
                column = column + div[l]
            column = column * (1.0 / math.sqrt(levels))
            absolute = vort + planet[...][None]
            tend = jnp.concatenate(
                [
                    (-absolute * div).reshape(rows, step).astype(BF16),
                    (absolute * vort - div * column[None]).reshape(rows, step).astype(BF16),
                ],
                axis=0,
            )
            total[...] += dot(tend, analysis, NT)
            return c * tc + n * ts, n * tc - c * ts

        lax.fori_loop(0, count, one_step, (c0, n0))

        sums = []
        for f in range(2):
            for l in range(levels):
                base = (f * levels + l) * SUB * SUB
                value = jnp.zeros((SUB, LANES), F32)
                for q in range(SUB):
                    value = jnp.where(which == q, total[base + q * SUB : base + (q + 1) * SUB, :], value)
                value = value * back_c + pltpu.roll(value, half, 1) * back_s
                value = value + pltpu.roll(value, 4, 0)
                sums.append(value + pltpu.roll(value, 2, 0))
        lined = []
        for l in range(levels):
            both = jnp.where(row_mod4(row_index()) < 2, sums[l], sums[levels + l])
            lined.append(jnp.where(row_index() < 4, both, pltpu.roll(both, half, 1)))
        for p in range(levels // 2):
            kept[p, g * SUB : (g + 1) * SUB, :] = jnp.where(
                first, lined[2 * p], pltpu.roll(lined[2 * p + 1], half, 1)
            )
    for p in range(levels // 2):
        moved = jnp.transpose(kept[p]).astype(BF16)
        out_ref[p * 2 * waves : (p + 1) * 2 * waves] = moved.reshape(2 * waves, SUB, LANES)


def row_index():
    return iota((SUB, LANES), 0)


def row_mod4(row):
    return row % 4


def fast_body(groups, waves, levels, step, spectral, legendre, wavenumber):
    lats, degrees = legendre.shape[1:]
    devices = waves * levels
    block = devices * SUB
    smem = pl.BlockSpec(memory_space=pltpu.SMEM)
    vmem = pl.BlockSpec(memory_space=pltpu.VMEM)
    anywhere = pl.BlockSpec(memory_space=pl.ANY)
    params = pltpu.CompilerParams(vmem_limit_bytes=32 * 1024 * 1024)
    parcel = jax.ShapeDtypeStruct((devices, SUB, LANES), BF16)
    leg_scratch = [
        pltpu.VMEM((2 * groups, block, degrees), BF16),
    ]
    sent = pl.pallas_call(
        functools.partial(forward_kernel, groups),
        out_shape=parcel,
        in_specs=[smem, vmem, anywhere],
        out_specs=vmem,
        scratch_shapes=leg_scratch
        + [pltpu.VMEM((2, LANES, block), F32), pltpu.SemaphoreType.DMA((2 * groups,))],
        compiler_params=params,
        name="forward",
    )(wavenumber, spectral, legendre)
    got = lax.all_to_all(sent, ("lev", "wave"), 0, 0, tiled=True)
    rows = 2 * levels * SUB * SUB
    tend = pl.pallas_call(
        functools.partial(grid_kernel, groups, waves, levels, lats, step),
        out_shape=parcel,
        in_specs=[smem, vmem],
        out_specs=vmem,
        scratch_shapes=[
            pltpu.VMEM((rows, LANES), BF16),
            pltpu.VMEM((SUB * SUB, step), F32),
            pltpu.VMEM((rows, LANES), F32),
            pltpu.VMEM((levels // 2, LANES, LANES), F32),
        ],
        compiler_params=params,
        name="grid",
    )(wavenumber, got)
    back = lax.all_to_all(tend, ("lev", "wave"), 0, 0, tiled=True)
    return pl.pallas_call(
        functools.partial(backward_kernel, groups),
        out_shape=jax.ShapeDtypeStruct(spectral.shape, BF16),
        in_specs=[smem, anywhere, vmem],
        out_specs=vmem,
        scratch_shapes=leg_scratch + [pltpu.SemaphoreType.DMA((2 * groups,))],
        compiler_params=params,
        name="backward",
    )(wavenumber, legendre, back)


def body(spectral, legendre, wavenumber):
    waves, levels = lax.axis_size("wave"), lax.axis_size("lev")
    lats = legendre.shape[1]
    group_lats = waves * levels * SUB
    groups = lats // (2 * group_lats)
    fits = (
        2 * groups * group_lats == lats
        and wavenumber.shape[0] == waves
        and spectral.shape[1] == 1
        and 2 * waves * SUB == LANES
        and levels % 2 == 0
        and 2 * groups * SUB <= LANES
        and group_lats % LANES == 0
    )
    if fits:
        return fast_body(groups, waves, levels, LANES, spectral, legendre, wavenumber)
    return general_body(spectral, legendre, wavenumber)


def circle_tables(latitude, band_index, wavenumber, lat_total, band_total, band_cap, wave_total):
    circle_length = 20 + 4 * jnp.minimum(latitude, lat_total - 1 - latitude)
    band_width = (circle_length + band_total - 1) // band_total
    offsets = jnp.arange(band_cap, dtype=jnp.int32)
    longitude_index = band_index[None, :, None] * band_width[:, None, None] + offsets[None, None, :]
    inside = (offsets[None, None, :] < band_width[:, None, None]) & (
        longitude_index < circle_length[:, None, None]
    )
    rows = latitude.shape[0]
    longitude_index = longitude_index.reshape(rows, -1)
    inside = inside.reshape(rows, -1)
    phase_index = (
        wavenumber[None, None, :] * longitude_index[:, :, None] % circle_length[:, None, None]
    )
    length_float = circle_length.astype(jnp.float32)
    angles = 2.0 * math.pi * phase_index.astype(jnp.float32) / length_float[:, None, None]
    shown = inside[:, :, None].astype(jnp.float32)
    trig_basis = jnp.stack([jnp.cos(angles) * shown, -jnp.sin(angles) * shown], axis=2)
    colatitude = (latitude.astype(jnp.float32) + 0.5) * (math.pi / lat_total)
    circle_weight = jnp.sin(colatitude) / jnp.sqrt(length_float)
    synth_table = (trig_basis / math.sqrt(wave_total)).astype(jnp.bfloat16)
    analysis_table = (trig_basis * circle_weight[:, None, None, None]).astype(jnp.bfloat16)
    return (synth_table, analysis_table, 2.0 * jnp.cos(colatitude))


def tendencies(grid_values, planetary):
    vorticity = grid_values[0]
    divergence = grid_values[1]
    absolute_vort = vorticity + planetary[None, :, None]
    column_div = jnp.sum(divergence, axis=0) / math.sqrt(divergence.shape[0])
    return jnp.stack(
        [-absolute_vort * divergence, absolute_vort * vorticity - divergence * column_div[None]]
    ).astype(jnp.bfloat16)


def general_body(spectral, legendre, wavenumber):
    wave_count = lax.axis_size("wave")
    lev_count = lax.axis_size("lev")
    wave_index = lax.axis_index("wave")
    lev_index = lax.axis_index("lev")
    lat_total = legendre.shape[1]
    degree_count = legendre.shape[2]
    set_span = lat_total // wave_count
    wave_total = wavenumber.shape[0]
    own_wave = lax.dynamic_slice_in_dim(wavenumber, wave_index, 1, 0)
    kept_degrees = (
        jnp.arange(degree_count, dtype=jnp.int32)[None, :] <= (degree_count - 1 - own_wave)[:, None]
    )
    masked_spec = jnp.where(kept_degrees, spectral, jnp.zeros_like(spectral))
    fourier = jnp.einsum(
        "flrsn,sjn->flrsj", masked_spec, legendre, preferred_element_type=jnp.float32
    ).astype(jnp.bfloat16)
    circle_max = 20 + 4 * (lat_total // 2 - 1)
    band_cap = (circle_max + lev_count - 1) // lev_count
    latitude = wave_index * set_span + jnp.arange(set_span, dtype=jnp.int32)
    band_index = jnp.reshape(lev_index, (1,))
    synth_table, analysis_table, planetary = circle_tables(
        latitude, band_index, wavenumber, lat_total, lev_count, band_cap, wave_total
    )
    set_fourier = lax.all_to_all(fourier, "wave", split_axis=4, concat_axis=3, tiled=True)
    grid_values = jnp.einsum(
        "flrsq,qprs->flqp",
        lax.all_gather(set_fourier, "lev", axis=1, tiled=True),
        synth_table,
        preferred_element_type=jnp.float32,
    )
    tendency = tendencies(grid_values, planetary)
    summed = lax.psum_scatter(
        jnp.einsum(
            "flqp,qprs->lfrsq", tendency, analysis_table, preferred_element_type=jnp.float32
        ),
        "lev",
        scatter_dimension=0,
        tiled=True,
    )
    returned = lax.all_to_all(
        summed.astype(jnp.bfloat16), "wave", split_axis=3, concat_axis=4, tiled=True
    )
    analysed = jnp.einsum(
        "lfrsj,sjn->flrsn", returned, legendre, preferred_element_type=jnp.float32
    )
    return jnp.where(kept_degrees, analysed, jnp.zeros_like(analysed)).astype(jnp.bfloat16)


def solution(mesh):
    in_specs = (P(None, "lev", None, "wave", None), P("wave", None, None), P())
    out_specs = P(None, "lev", None, "wave", None)
    return jax.shard_map(body, mesh=mesh, in_specs=in_specs, out_specs=out_specs, check_vma=False)
```

```python
import functools
import math

import jax
import jax.numpy as jnp
from jax import lax
from jax.experimental import pallas as pl
from jax.experimental.pallas import tpu as pltpu
from jax.sharding import PartitionSpec as P

SUB = 8
LANES = 128
QUARTERS = 4
FIRST = 5
NT = (((1,), (1,)), ((), ()))
NN = (((1,), (0,)), ((), ()))
F32 = jnp.float32
BF16 = jnp.bfloat16


def dot(a, b, dims):
    return lax.dot_general(a, b, dims, preferred_element_type=F32)


def iota(shape, dim):
    return lax.broadcasted_iota(jnp.int32, shape, dim)


def one_hot(mask):
    return jnp.where(mask, 1.0, 0.0).astype(BF16)


def cos_sin_turns(turns):
    quadrant = jnp.floor(turns * 4.0 + 0.5)
    u = (turns - quadrant * 0.25) * (2.0 * math.pi)
    u2 = u * u
    sine = u * (1.0 + u2 * (-1 / 6 + u2 * (1 / 120 + u2 * (-1 / 5040 + u2 * (1 / 362880)))))
    cosine = 1.0 + u2 * (-0.5 + u2 * (1 / 24 + u2 * (-1 / 720 + u2 * (1 / 40320))))
    quadrant = quadrant.astype(jnp.int32) & 3
    odd = (quadrant & 1) == 1
    c = jnp.where(odd, sine, cosine)
    s = jnp.where(odd, cosine, sine)
    c = jnp.where((quadrant == 1) | (quadrant == 2), -c, c)
    s = jnp.where(quadrant >= 2, -s, s)
    return c, s


def cos_sin_phase(wavenumber, point, circle):
    inverse = 1.0 / circle
    product = wavenumber * point
    whole = jnp.floor(product * inverse + 0.5)
    return cos_sin_turns((product - whole * circle) * inverse)


def quarter_turns(wavenumber, band):
    k = (wavenumber * band) & 3
    c = jnp.where(k == 0, 1.0, jnp.where(k == 2, -1.0, 0.0))
    s = jnp.where(k == 1, 1.0, jnp.where(k == 3, -1.0, 0.0))
    return c, s


def plain_part(group, south):
    return (group % 2 == 0) != south


def block_place(block, groups):
    south = block >= groups
    return (2 * groups - 1 - block if south else block), south


def reverse_matrix(n):
    return one_hot(iota((n, n), 0) + iota((n, n), 1) == n - 1)


def forward_kernel(groups, wn_hbm, spec_hbm, leg_hbm, out_ref, leg, kept_ref, wn, spec, sems):
    block = leg.shape[1]
    first = [
        pltpu.make_async_copy(wn_hbm, wn, sems.at[2 * groups]),
        pltpu.make_async_copy(spec_hbm, spec, sems.at[2 * groups + 1]),
    ]
    copies = [
        pltpu.make_async_copy(leg_hbm.at[0, pl.ds(k * block, block)], leg.at[k], sems.at[k])
        for k in range(2 * groups)
    ]
    for copy in first + copies:
        copy.start()
    for copy in first:
        copy.wait()
    degrees = leg.shape[2]
    kept = iota((SUB, degrees), 1) <= degrees - 1 - wn[lax.axis_index("wave")]
    kept_ref[...] = jnp.where(kept, 1.0, 0.0)
    rows = [spec[f, 0, 0].astype(F32) for f in range(2)]
    rows = jnp.concatenate(rows + [jnp.zeros((SUB - 4, degrees), F32)], axis=0)
    rows = jnp.where(kept, rows, 0.0)
    columns = jnp.transpose(jnp.concatenate([rows] * (LANES // SUB), axis=0)).astype(BF16)
    slot = iota((block, LANES), 1) // SUB
    plain = jnp.zeros((block, LANES), F32)
    turned = jnp.zeros((block, LANES), F32)
    for k, copy in enumerate(copies):
        group, south = block_place(k, groups)
        copy.wait()
        fourier = dot(leg[k], columns, NN)
        if plain_part(group, south):
            plain = jnp.where(slot == group, fourier, plain)
        else:
            turned = jnp.where(slot == groups + group, fourier, turned)
    placed = plain + dot(reverse_matrix(block), turned.astype(BF16), NN)
    out_ref[...] = placed.astype(BF16).reshape(out_ref.shape)


def backward_kernel(groups, kept_ref, leg, got_ref, out_ref):
    block, degrees = leg.shape[1:]
    got = got_ref[...].reshape(block, LANES)
    shape = (groups * SUB, LANES)
    row, lane = iota(shape, 0), iota(shape, 1)
    group, field, part = row // SUB, (row % SUB) // 2, row % 2
    source = group * SUB + part * 4 + field * 2
    used = row % SUB < 4
    odd = group % 2
    plain = dot(one_hot(used & (lane == source + odd)), got, NT).astype(BF16)
    turned = dot(one_hot(used & (lane == source + 1 - odd)), got, NT).astype(BF16)
    turned = dot(turned, reverse_matrix(block), NN).astype(BF16)
    total = jnp.zeros((SUB, degrees), F32)
    for k in range(2 * groups):
        g, south = block_place(k, groups)
        rows = plain if plain_part(g, south) else turned
        total = total + dot(rows[g * SUB : (g + 1) * SUB], leg[k], NN)
    total = (total * kept_ref[...]).astype(BF16)
    for f in range(2):
        out_ref[f, 0, 0] = total[f * 2 : f * 2 + 2]


def grid_kernel(groups, waves, levels, lats, step, wn_ref, got_ref, out_ref, coef, planet, total, kept):
    devices = waves * levels
    block = devices * SUB
    half = waves * SUB
    device = lax.axis_index("lev") * waves + lax.axis_index("wave")
    numbers = [wn_ref[s] for s in range(waves)]

    got = got_ref[...].reshape(block, LANES)
    shape = (groups * 4 * SUB, LANES)
    row, lane = iota(shape, 0), iota(shape, 1)
    group, pair, south = row // (4 * SUB), (row // SUB) % 4, row % 2
    turned = (group + south) % 2
    source = turned * (groups * SUB) + group * SUB + pair
    fourier = dot(one_hot(lane == source), got, NT)

    def slot_number(lanes):
        value = jnp.zeros(lanes.shape, jnp.int32)
        for s in range(waves):
            value = jnp.where(lanes == s, numbers[s], value)
        return value

    shape = (SUB, block)
    band, slot = iota(shape, 0) // 2, (iota(shape, 1) // SUB) % waves
    turn_c, turn_s = quarter_turns(slot_number(slot), band)
    shape = (SUB, LANES)
    row, lane = iota(shape, 0), iota(shape, 1)
    back_c, back_s = quarter_turns(slot_number((lane // SUB) % waves), row // 2)
    back_s = jnp.where(lane < half, back_s, -back_s)
    first = lane < half
    which = lane % SUB

    kept[...] = jnp.zeros_like(kept)
    for g in range(groups):
        for f in range(2):
            base = (g * 4 + f * 2) * SUB
            real, imag = fourier[base : base + SUB], fourier[base + SUB : base + 2 * SUB]
            turned_r = real * turn_c - imag * turn_s
            turned_i = real * turn_s + imag * turn_c
            for l in range(levels):
                cut = slice((l // 2) * LANES, (l // 2 + 1) * LANES)
                a, b = turned_r[:, cut], turned_i[:, cut]
                if l % 2 == 0:
                    b = pltpu.roll(b, half, 1)
                else:
                    a = pltpu.roll(a, half, 1)
                both = jnp.where(first, a, b)
                for q in range(0, SUB, 2):
                    place = ((f * levels + l) * SUB + q) * SUB
                    two = jnp.concatenate(
                        [jnp.where(which == q + k, both, 0.0) for k in range(2)], axis=0
                    )
                    coef[place : place + 2 * SUB, :] = two.astype(BF16)

        def latitude(index):
            order = device * SUB + index
            return g * block + (order if g % 2 == 0 else block - 1 - order)

        lat = latitude(iota((SUB, LANES), 0)).astype(F32)
        quarter = lat + FIRST
        circle = QUARTERS * quarter
        weight = cos_sin_turns((lat + 0.5) * (0.5 / lats))[1] / jnp.sqrt(circle)
        row = iota((SUB * SUB, step), 0)
        lat_row = latitude(row // SUB).astype(F32)
        planetary = 2.0 * cos_sin_turns((lat_row + 0.5) * (0.5 / lats))[0]
        planet[...] = jnp.where(row % 2 == 0, planetary, -planetary)

        point = iota((SUB, step), 1)
        wide = jnp.concatenate([circle] * (step // LANES), axis=1)
        start = [cos_sin_phase(numbers[s].astype(F32), point.astype(F32), wide) for s in range(waves)]
        c0 = jnp.concatenate([c for c, _ in start], axis=0)
        n0 = jnp.concatenate([-s for _, s in start], axis=0)
        turn = [cos_sin_phase((numbers[s] * step).astype(F32), 1.0, circle) for s in range(waves)]
        tc = jnp.concatenate([jnp.concatenate([c for c, _ in turn], axis=0)] * (step // LANES), axis=1)
        ts = jnp.concatenate([jnp.concatenate([s for _, s in turn], axis=0)] * (step // LANES), axis=1)
        weights = jnp.concatenate([jnp.concatenate([weight] * (2 * waves), axis=0)] * (step // LANES), axis=1)
        limit = jnp.concatenate([jnp.concatenate([quarter] * (2 * waves), axis=0)] * (step // LANES), axis=1)
        limit = limit.astype(jnp.int32)
        points = iota((2 * half, step), 1)

        total[...] = jnp.zeros_like(total)
        longest = jnp.maximum(latitude(0), latitude(SUB - 1)) + FIRST
        count = (longest + step - 1) // step

        def one_step(i, carry):
            c, n = carry
            basis = jnp.concatenate([c, n], axis=0)
            synth = (basis * (1.0 / math.sqrt(waves))).astype(BF16)
            analysis = jnp.where(points + i * step < limit, basis * weights, 0.0).astype(BF16)
            values = dot(coef[...], synth, NN)
            rows = levels * SUB * SUB
            vort = values[:rows].reshape(levels, SUB * SUB, step)
            div = values[rows:].reshape(levels, SUB * SUB, step)
            column = div[0]
            for l in range(1, levels):
                column = column + div[l]
            column = column * (1.0 / math.sqrt(levels))
            absolute = vort + planet[...][None]
            tend = jnp.concatenate(
                [
                    (-absolute * div).reshape(rows, step).astype(BF16),
                    (absolute * vort - div * column[None]).reshape(rows, step).astype(BF16),
                ],
                axis=0,
            )
            total[...] += dot(tend, analysis, NT)
            return c * tc + n * ts, n * tc - c * ts

        lax.fori_loop(0, count, one_step, (c0, n0))

        sums = []
        for f in range(2):
            for l in range(levels):
                base = (f * levels + l) * SUB * SUB
                value = jnp.zeros((SUB, LANES), F32)
                for q in range(SUB):
                    value = jnp.where(which == q, total[base + q * SUB : base + (q + 1) * SUB, :], value)
                value = value * back_c + pltpu.roll(value, half, 1) * back_s
                value = value + pltpu.roll(value, 4, 0)
                sums.append(value + pltpu.roll(value, 2, 0))
        lined = []
        for l in range(levels):
            both = jnp.where(row_mod4(row_index()) < 2, sums[l], sums[levels + l])
            lined.append(jnp.where(row_index() < 4, both, pltpu.roll(both, half, 1)))
        for p in range(levels // 2):
            kept[p, g * SUB : (g + 1) * SUB, :] = jnp.where(
                first, lined[2 * p], pltpu.roll(lined[2 * p + 1], half, 1)
            )
    for p in range(levels // 2):
        moved = jnp.transpose(kept[p]).astype(BF16)
        out_ref[p * 2 * waves : (p + 1) * 2 * waves] = moved.reshape(2 * waves, SUB, LANES)


def row_index():
    return iota((SUB, LANES), 0)


def row_mod4(row):
    return row % 4


def fast_body(groups, waves, levels, step, spectral, legendre, wavenumber):
    lats, degrees = legendre.shape[1:]
    devices = waves * levels
    block = devices * SUB
    smem = pl.BlockSpec(memory_space=pltpu.SMEM)
    vmem = pl.BlockSpec(memory_space=pltpu.VMEM)
    hbm = pl.BlockSpec(memory_space=pltpu.HBM)
    params = pltpu.CompilerParams(vmem_limit_bytes=40 * 1024 * 1024)
    parcel = jax.ShapeDtypeStruct((devices, SUB, LANES), BF16)
    spectral = jnp.transpose(spectral, (0, 1, 3, 2, 4))
    sent, leg, kept = pl.pallas_call(
        functools.partial(forward_kernel, groups),
        out_shape=[
            parcel,
            jax.ShapeDtypeStruct((2 * groups, block, degrees), BF16),
            jax.ShapeDtypeStruct((SUB, degrees), F32),
        ],
        in_specs=[hbm, hbm, hbm],
        out_specs=[vmem] * 3,
        scratch_shapes=[
            pltpu.SMEM(wavenumber.shape, jnp.int32),
            pltpu.VMEM(spectral.shape, BF16),
            pltpu.SemaphoreType.DMA((2 * groups + 2,)),
        ],
        compiler_params=params,
        name="forward",
    )(*(pltpu.with_memory_space_constraint(x, pltpu.HBM) for x in (wavenumber, spectral, legendre)))
    got = lax.all_to_all(sent, ("lev", "wave"), 0, 0, tiled=True)
    rows = 2 * levels * SUB * SUB
    tend = pl.pallas_call(
        functools.partial(grid_kernel, groups, waves, levels, lats, step),
        out_shape=parcel,
        in_specs=[smem, vmem],
        out_specs=vmem,
        scratch_shapes=[
            pltpu.VMEM((rows, LANES), BF16),
            pltpu.VMEM((SUB * SUB, step), F32),
            pltpu.VMEM((rows, LANES), F32),
            pltpu.VMEM((levels // 2, LANES, LANES), F32),
        ],
        compiler_params=params,
        name="grid",
    )(wavenumber, got)
    back = lax.all_to_all(tend, ("lev", "wave"), 0, 0, tiled=True)
    out = pl.pallas_call(
        functools.partial(backward_kernel, groups),
        out_shape=jax.ShapeDtypeStruct(spectral.shape, BF16),
        in_specs=[vmem, vmem, vmem],
        out_specs=vmem,
        compiler_params=params,
        name="backward",
    )(kept, leg, back)
    return jnp.transpose(out, (0, 1, 3, 2, 4))


def body(spectral, legendre, wavenumber):
    waves, levels = lax.axis_size("wave"), lax.axis_size("lev")
    lats = legendre.shape[1]
    group_lats = waves * levels * SUB
    groups = lats // (2 * group_lats)
    fits = (
        2 * groups * group_lats == lats
        and wavenumber.shape[0] == waves
        and spectral.shape[1] == 1
        and 2 * waves * SUB == LANES
        and levels % 2 == 0
        and 2 * groups * SUB <= LANES
        and group_lats % LANES == 0
    )
    if fits:
        return fast_body(groups, waves, levels, 2 * LANES, spectral, legendre, wavenumber)
    return general_body(spectral, legendre, wavenumber)


def circle_tables(latitude, band_index, wavenumber, lat_total, band_total, band_cap, wave_total):
    circle_length = 20 + 4 * jnp.minimum(latitude, lat_total - 1 - latitude)
    band_width = (circle_length + band_total - 1) // band_total
    offsets = jnp.arange(band_cap, dtype=jnp.int32)
    longitude_index = band_index[None, :, None] * band_width[:, None, None] + offsets[None, None, :]
    inside = (offsets[None, None, :] < band_width[:, None, None]) & (
        longitude_index < circle_length[:, None, None]
    )
    rows = latitude.shape[0]
    longitude_index = longitude_index.reshape(rows, -1)
    inside = inside.reshape(rows, -1)
    phase_index = (
        wavenumber[None, None, :] * longitude_index[:, :, None] % circle_length[:, None, None]
    )
    length_float = circle_length.astype(jnp.float32)
    angles = 2.0 * math.pi * phase_index.astype(jnp.float32) / length_float[:, None, None]
    shown = inside[:, :, None].astype(jnp.float32)
    trig_basis = jnp.stack([jnp.cos(angles) * shown, -jnp.sin(angles) * shown], axis=2)
    colatitude = (latitude.astype(jnp.float32) + 0.5) * (math.pi / lat_total)
    circle_weight = jnp.sin(colatitude) / jnp.sqrt(length_float)
    synth_table = (trig_basis / math.sqrt(wave_total)).astype(jnp.bfloat16)
    analysis_table = (trig_basis * circle_weight[:, None, None, None]).astype(jnp.bfloat16)
    return (synth_table, analysis_table, 2.0 * jnp.cos(colatitude))


def tendencies(grid_values, planetary):
    vorticity = grid_values[0]
    divergence = grid_values[1]
    absolute_vort = vorticity + planetary[None, :, None]
    column_div = jnp.sum(divergence, axis=0) / math.sqrt(divergence.shape[0])
    return jnp.stack(
        [-absolute_vort * divergence, absolute_vort * vorticity - divergence * column_div[None]]
    ).astype(jnp.bfloat16)


def general_body(spectral, legendre, wavenumber):
    wave_count = lax.axis_size("wave")
    lev_count = lax.axis_size("lev")
    wave_index = lax.axis_index("wave")
    lev_index = lax.axis_index("lev")
    lat_total = legendre.shape[1]
    degree_count = legendre.shape[2]
    set_span = lat_total // wave_count
    wave_total = wavenumber.shape[0]
    own_wave = lax.dynamic_slice_in_dim(wavenumber, wave_index, 1, 0)
    kept_degrees = (
        jnp.arange(degree_count, dtype=jnp.int32)[None, :] <= (degree_count - 1 - own_wave)[:, None]
    )
    masked_spec = jnp.where(kept_degrees, spectral, jnp.zeros_like(spectral))
    fourier = jnp.einsum(
        "flrsn,sjn->flrsj", masked_spec, legendre, preferred_element_type=jnp.float32
    ).astype(jnp.bfloat16)
    circle_max = 20 + 4 * (lat_total // 2 - 1)
    band_cap = (circle_max + lev_count - 1) // lev_count
    latitude = wave_index * set_span + jnp.arange(set_span, dtype=jnp.int32)
    band_index = jnp.reshape(lev_index, (1,))
    synth_table, analysis_table, planetary = circle_tables(
        latitude, band_index, wavenumber, lat_total, lev_count, band_cap, wave_total
    )
    set_fourier = lax.all_to_all(fourier, "wave", split_axis=4, concat_axis=3, tiled=True)
    grid_values = jnp.einsum(
        "flrsq,qprs->flqp",
        lax.all_gather(set_fourier, "lev", axis=1, tiled=True),
        synth_table,
        preferred_element_type=jnp.float32,
    )
    tendency = tendencies(grid_values, planetary)
    summed = lax.psum_scatter(
        jnp.einsum(
            "flqp,qprs->lfrsq", tendency, analysis_table, preferred_element_type=jnp.float32
        ),
        "lev",
        scatter_dimension=0,
        tiled=True,
    )
    returned = lax.all_to_all(
        summed.astype(jnp.bfloat16), "wave", split_axis=3, concat_axis=4, tiled=True
    )
    analysed = jnp.einsum(
        "lfrsj,sjn->flrsn", returned, legendre, preferred_element_type=jnp.float32
    )
    return jnp.where(kept_degrees, analysed, jnp.zeros_like(analysed)).astype(jnp.bfloat16)


def solution(mesh):
    in_specs = (P(None, "lev", None, "wave", None), P("wave", None, None), P())
    out_specs = P(None, "lev", None, "wave", None)
    return jax.shard_map(body, mesh=mesh, in_specs=in_specs, out_specs=out_specs, check_vma=False)
```

```python
import functools
import math

import jax
import jax.numpy as jnp
from jax import lax
from jax.experimental import pallas as pl
from jax.experimental.pallas import tpu as pltpu
from jax.sharding import PartitionSpec as P

SUB = 8
LANES = 128
QUARTERS = 4
FIRST = 5
NT = (((1,), (1,)), ((), ()))
NN = (((1,), (0,)), ((), ()))
F32 = jnp.float32
BF16 = jnp.bfloat16


def dot(a, b, dims):
    return lax.dot_general(a, b, dims, preferred_element_type=F32)


def iota(shape, dim):
    return lax.broadcasted_iota(jnp.int32, shape, dim)


def one_hot(mask):
    return jnp.where(mask, 1.0, 0.0).astype(BF16)


def cos_sin_turns(turns):
    quadrant = jnp.floor(turns * 4.0 + 0.5)
    u = (turns - quadrant * 0.25) * (2.0 * math.pi)
    u2 = u * u
    sine = u * (1.0 + u2 * (-1 / 6 + u2 * (1 / 120 + u2 * (-1 / 5040 + u2 * (1 / 362880)))))
    cosine = 1.0 + u2 * (-0.5 + u2 * (1 / 24 + u2 * (-1 / 720 + u2 * (1 / 40320))))
    quadrant = quadrant.astype(jnp.int32) & 3
    odd = (quadrant & 1) == 1
    c = jnp.where(odd, sine, cosine)
    s = jnp.where(odd, cosine, sine)
    c = jnp.where((quadrant == 1) | (quadrant == 2), -c, c)
    s = jnp.where(quadrant >= 2, -s, s)
    return c, s


def cos_sin_phase(wavenumber, point, circle):
    inverse = 1.0 / circle
    product = wavenumber * point
    whole = jnp.floor(product * inverse + 0.5)
    return cos_sin_turns((product - whole * circle) * inverse)


def quarter_turns(wavenumber, band):
    k = (wavenumber * band) & 3
    c = jnp.where(k == 0, 1.0, jnp.where(k == 2, -1.0, 0.0))
    s = jnp.where(k == 1, 1.0, jnp.where(k == 3, -1.0, 0.0))
    return c, s


def plain_part(group, south):
    return (group % 2 == 0) != south


def block_place(block, groups):
    south = block >= groups
    return (2 * groups - 1 - block if south else block), south


def reverse_matrix(n):
    return one_hot(iota((n, n), 0) + iota((n, n), 1) == n - 1)


def forward_kernel(groups, wn_hbm, spec_hbm, leg_hbm, out_ref, kept_ref, leg, wn, spec, sems):
    block = leg.shape[1]
    first = [
        pltpu.make_async_copy(wn_hbm, wn, sems.at[2 * groups]),
        pltpu.make_async_copy(spec_hbm, spec, sems.at[2 * groups + 1]),
    ]
    copies = [
        pltpu.make_async_copy(
            leg_hbm.at[0, pl.ds(k * block, 2 * block)].reshape(2, block, leg.shape[2]),
            leg.at[pl.ds(k, 2)],
            sems.at[k],
        )
        for k in range(0, 2 * groups, 2)
    ]
    for copy in first + copies:
        copy.start()
    for copy in first:
        copy.wait()
    degrees = leg.shape[2]
    kept = iota((SUB, degrees), 1) <= degrees - 1 - wn[lax.axis_index("wave")]
    kept_ref[...] = jnp.where(kept, 1.0, 0.0)
    rows = [spec[f, 0, 0].astype(F32) for f in range(2)]
    rows = jnp.concatenate(rows + [jnp.zeros((SUB - 4, degrees), F32)], axis=0)
    rows = jnp.where(kept, rows, 0.0)
    rows = rows.astype(BF16)
    pieces = [[], []]
    for k in range(2 * groups):
        group, south = block_place(k, groups)
        if k % 2 == 0:
            copies[k // 2].wait()
        pieces[0 if plain_part(group, south) else 1].append((group, dot(rows, leg[k], NT)))
    pieces = [[v for _, v in sorted(p, key=lambda x: x[0])] for p in pieces]
    blank = jnp.zeros((SUB, block), F32)
    n = LANES // SUB
    plain = jnp.concatenate(pieces[0] + [blank] * (n - groups), axis=0)
    turned = jnp.concatenate([blank] * groups + pieces[1] + [blank] * (n - 2 * groups), axis=0)
    placed = jnp.transpose(plain) + dot(reverse_matrix(block), turned.astype(BF16), NT)
    out_ref[...] = placed.astype(BF16).reshape(out_ref.shape)


def backward_kernel(groups, kept_ref, leg, got_ref, out_ref):
    degrees = leg.shape[2]
    block = leg.shape[1] // (2 * groups)
    got = got_ref[...].reshape(block, LANES)
    shape = (groups * SUB, LANES)
    row, lane = iota(shape, 0), iota(shape, 1)
    group, field, part = row // SUB, (row % SUB) // 2, row % 2
    source = group * SUB + part * 4 + field * 2
    used = row % SUB < 4
    odd = group % 2
    plain = dot(one_hot(used & (lane == source + odd)), got, NT).astype(BF16)
    turned = dot(one_hot(used & (lane == source + 1 - odd)), got, NT).astype(BF16)
    turned = dot(turned, reverse_matrix(block), NN).astype(BF16)
    total = jnp.zeros((SUB, degrees), F32)
    for k in range(2 * groups):
        g, south = block_place(k, groups)
        rows = plain if plain_part(g, south) else turned
        total = total + dot(
            rows[g * SUB : (g + 1) * SUB], leg[0, k * block : (k + 1) * block, :], NN
        )
    total = (total * kept_ref[...]).astype(BF16)
    for f in range(2):
        out_ref[f, 0, 0] = total[f * 2 : f * 2 + 2]


def chunk_counts(groups, block, step):
    return [-(-(FIRST + block * (g + 1) - 1) // step) for g in range(groups)]


def latitude(group, block, order):
    return group * block + (order if group % 2 == 0 else block - 1 - order)


def this_device(waves):
    return lax.axis_index("lev") * waves + lax.axis_index("wave")


def tables_kernel(
    groups, waves, levels, lats, step, wn_hbm, synth, analysis, planet, turns, backs, wn, sem
):
    copy = pltpu.make_async_copy(wn_hbm, wn, sem)
    copy.start()
    block = waves * levels * SUB
    half = waves * SUB
    device = this_device(waves)
    copy.wait()
    numbers = [wn[s] for s in range(waves)]

    def slot_number(lanes):
        value = jnp.zeros(lanes.shape, jnp.int32)
        for s in range(waves):
            value = jnp.where(lanes == s, numbers[s], value)
        return value

    shape = (SUB, block)
    turns[0], turns[1] = quarter_turns(
        slot_number((iota(shape, 1) // SUB) % waves), iota(shape, 0) // 2
    )
    shape = (SUB, LANES)
    lane = iota(shape, 1)
    back_c, back_s = quarter_turns(slot_number((lane // SUB) % waves), iota(shape, 0) // 2)
    backs[0], backs[1] = back_c, jnp.where(lane < half, back_s, -back_s)

    def wide(x):
        return jnp.concatenate([x] * (step // LANES), axis=1)

    slot = 0
    for g, count in enumerate(chunk_counts(groups, block, step)):
        lat = latitude(g, block, device * SUB + iota((SUB, LANES), 0)).astype(F32)
        quarter = lat + FIRST
        circle = QUARTERS * quarter
        weight = cos_sin_turns((lat + 0.5) * (0.5 / lats))[1] / jnp.sqrt(circle)
        row = iota((SUB * SUB, LANES), 0)
        lat_row = latitude(g, block, device * SUB + row // SUB).astype(F32)
        planetary = 2.0 * cos_sin_turns((lat_row + 0.5) * (0.5 / lats))[0]
        planet[g] = wide(jnp.where(row % 2 == 0, planetary, -planetary))

        point = iota((SUB, step), 1)
        start = [
            cos_sin_phase(numbers[s].astype(F32), point.astype(F32), wide(circle))
            for s in range(waves)
        ]
        turn = [cos_sin_phase((numbers[s] * step).astype(F32), 1.0, circle) for s in range(waves)]
        quarter, weight = wide(quarter).astype(jnp.int32), wide(weight)
        for s in range(0, waves, 2):
            pair = [start[s], start[s + 1]]
            for a in range(count):
                shown = point + a * step < quarter
                rows = pl.ds(s * SUB, 2 * SUB), pl.ds(half + s * SUB, 2 * SUB)
                for part, at in enumerate(rows):
                    basis = [-v[1] if part else v[0] for v in pair]
                    synth[slot + a, at, :] = jnp.concatenate(
                        [v * (1.0 / math.sqrt(waves)) for v in basis], axis=0
                    ).astype(BF16)
                    analysis[slot + a, at, :] = jnp.concatenate(
                        [jnp.where(shown, v * weight, 0.0) for v in basis], axis=0
                    ).astype(BF16)
                if a + 1 < count:
                    pair = [
                        (
                            c * wide(turn[s + k][0]) - n * wide(turn[s + k][1]),
                            n * wide(turn[s + k][0]) + c * wide(turn[s + k][1]),
                        )
                        for k, (c, n) in enumerate(pair)
                    ]
        slot += count
    analysis[slot] = jnp.zeros(analysis.shape[1:], BF16)


def grid_kernel(
    groups, waves, levels, step, synth, analysis, planet, turns, backs, got_ref, leg_hbm, out_ref, leg,
    coef, grid_a, grid_b, tend_a, tend_b, total, kept, sem,
):
    ahead = pltpu.make_async_copy(leg_hbm, leg, sem)
    ahead.start()
    block = waves * levels * SUB
    half = waves * SUB
    device = this_device(waves)
    row, lane = iota((SUB, LANES), 0), iota((SUB, LANES), 1)
    first = lane < half
    which = lane % SUB

    got = got_ref[...].reshape(block, LANES)
    shape = (groups * 4 * SUB, LANES)
    row_of, lane_of = iota(shape, 0), iota(shape, 1)
    group, pair, south = row_of // (4 * SUB), (row_of // SUB) % 4, row_of % 2
    source = (group + south) % 2 * (groups * SUB) + group * SUB + pair
    fourier = dot(one_hot(lane_of == source), got, NT)
    turn_c, turn_s = turns[0], turns[1]

    for g in range(groups):
        for f in range(2):
            base = (g * 4 + f * 2) * SUB
            real, imag = fourier[base : base + SUB], fourier[base + SUB : base + 2 * SUB]
            turned_r = real * turn_c - imag * turn_s
            turned_i = real * turn_s + imag * turn_c
            for l in range(levels):
                cut = slice((l // 2) * LANES, (l // 2 + 1) * LANES)
                a, b = turned_r[:, cut], turned_i[:, cut]
                if l % 2 == 0:
                    b = pltpu.roll(b, half, 1)
                else:
                    a = pltpu.roll(a, half, 1)
                both = jnp.where(first, a, b)
                for q in range(0, SUB, 2):
                    place = ((f * levels + l) * SUB + q) * SUB
                    two = jnp.concatenate(
                        [jnp.where(which == q + k, both, 0.0) for k in range(2)], axis=0
                    )
                    coef[g, place : place + 2 * SUB, :] = two.astype(BF16)

    most = chunk_counts(groups, block, step)
    ends, skips = [], []
    end = 0
    for g in range(groups):
        order = device * SUB
        longest = FIRST + jnp.maximum(
            latitude(g, block, order), latitude(g, block, order + SUB - 1)
        )
        count = (longest + step - 1) // step
        end = end + count
        ends.append(end)
        skips.append(most[g] - count)

    def place_of(i):
        group, slot = jnp.int32(0), i
        for g in range(groups - 1):
            past = i >= ends[g]
            group = group + jnp.where(past, 1, 0)
            slot = slot + jnp.where(past, skips[g], 0)
        return group, slot

    total[...] = jnp.zeros_like(total)
    for ref in (grid_a, grid_b, tend_a, tend_b):
        ref[...] = jnp.zeros_like(ref)
    rows = levels * SUB * SUB

    def stage(i, values, older, tend, oldest):
        group, slot = place_of(jnp.minimum(i, end - 1))
        values[...] = dot(coef[group], synth[slot], NN)

        group, _ = place_of(jnp.clip(i - 1, 0, end - 1))
        for r in range(0, SUB * SUB, 2 * SUB):
            at = [pl.ds(l * SUB * SUB + r, 2 * SUB) for l in range(levels)]
            below = [pl.ds(rows + l * SUB * SUB + r, 2 * SUB) for l in range(levels)]
            div = [older[b, :] for b in below]
            column = div[0]
            for l in range(1, levels):
                column = column + div[l]
            column = column * (1.0 / math.sqrt(levels))
            turning = planet[group, pl.ds(r, 2 * SUB), :]
            for l in range(levels):
                vort = older[at[l], :]
                absolute = vort + turning
                tend[at[l], :] = (-absolute * div[l]).astype(BF16)
                tend[below[l], :] = (absolute * vort - div[l] * column).astype(BF16)

        inside = (i >= 2) & (i - 2 < end)
        group, slot = place_of(jnp.clip(i - 2, 0, end - 1))
        slot = jnp.where(inside, slot, sum(most))
        total[group] += dot(oldest[...], analysis[slot], NT)

    @pl.loop(0, (end + 3) // 2)
    def _(pair):
        stage(2 * pair, grid_a, grid_b, tend_b, tend_a)
        stage(2 * pair + 1, grid_b, grid_a, tend_a, tend_b)

    back_c, back_s = backs[0], backs[1]
    kept[...] = jnp.zeros_like(kept)
    for g in range(groups):
        sums = []
        for f in range(2):
            for l in range(levels):
                base = (f * levels + l) * SUB * SUB
                value = jnp.zeros((SUB, LANES), F32)
                for q in range(SUB):
                    part = total[g, base + q * SUB : base + (q + 1) * SUB, :]
                    value = jnp.where(which == q, part, value)
                value = value * back_c + pltpu.roll(value, half, 1) * back_s
                value = value + pltpu.roll(value, 4, 0)
                sums.append(value + pltpu.roll(value, 2, 0))
        lined = []
        for l in range(levels):
            both = jnp.where(row % 4 < 2, sums[l], sums[levels + l])
            lined.append(jnp.where(row < 4, both, pltpu.roll(both, half, 1)))
        for p in range(levels // 2):
            kept[p, g * SUB : (g + 1) * SUB, :] = jnp.where(
                first, lined[2 * p], pltpu.roll(lined[2 * p + 1], half, 1)
            )
    for p in range(levels // 2):
        moved = jnp.transpose(kept[p]).astype(BF16)
        out_ref[p * 2 * waves : (p + 1) * 2 * waves] = moved.reshape(2 * waves, SUB, LANES)
    ahead.wait()


def fast_body(groups, waves, levels, step, spectral, legendre, wavenumber):
    lats, degrees = legendre.shape[1:]
    devices = waves * levels
    block = devices * SUB
    vmem = pl.BlockSpec(memory_space=pltpu.VMEM)
    hbm = pl.BlockSpec(memory_space=pltpu.HBM)
    params = pltpu.CompilerParams(vmem_limit_bytes=24 * 1024 * 1024)
    parcel = jax.ShapeDtypeStruct((devices, SUB, LANES), BF16)
    spectral = jnp.transpose(spectral, (0, 1, 3, 2, 4))
    sent, kept = pl.pallas_call(
        functools.partial(forward_kernel, groups),
        out_shape=[
            parcel,
            jax.ShapeDtypeStruct((SUB, degrees), F32),
        ],
        in_specs=[hbm, hbm, hbm],
        out_specs=[vmem] * 2,
        scratch_shapes=[
            pltpu.VMEM((2 * groups, block, degrees), BF16),
            pltpu.SMEM(wavenumber.shape, jnp.int32),
            pltpu.VMEM(spectral.shape, BF16),
            pltpu.SemaphoreType.DMA((2 * groups + 2,)),
        ],
        compiler_params=params,
        name="forward",
    )(*(pltpu.with_memory_space_constraint(x, pltpu.HBM) for x in (wavenumber, spectral, legendre)))
    got = lax.all_to_all(sent, ("lev", "wave"), 0, 0, tiled=True)
    rows = 2 * levels * SUB * SUB
    slots = sum(chunk_counts(groups, block, step))
    tables = pl.pallas_call(
        functools.partial(tables_kernel, groups, waves, levels, lats, step),
        out_shape=[
            jax.ShapeDtypeStruct((slots, LANES, step), BF16),
            jax.ShapeDtypeStruct((slots + 1, LANES, step), BF16),
            jax.ShapeDtypeStruct((groups, SUB * SUB, step), F32),
            jax.ShapeDtypeStruct((2, SUB, block), F32),
            jax.ShapeDtypeStruct((2, SUB, LANES), F32),
        ],
        in_specs=[hbm],
        out_specs=[vmem] * 5,
        scratch_shapes=[pltpu.SMEM(wavenumber.shape, jnp.int32), pltpu.SemaphoreType.DMA],
        compiler_params=params,
        name="tables",
    )(pltpu.with_memory_space_constraint(wavenumber, pltpu.HBM))
    tend, leg = pl.pallas_call(
        functools.partial(grid_kernel, groups, waves, levels, step),
        out_shape=[parcel, jax.ShapeDtypeStruct(legendre.shape, BF16)],
        in_specs=[vmem] * 6 + [hbm],
        out_specs=[vmem] * 2,
        scratch_shapes=[
            pltpu.VMEM((groups, rows, LANES), BF16),
            pltpu.VMEM((rows, step), F32),
            pltpu.VMEM((rows, step), F32),
            pltpu.VMEM((rows, step), BF16),
            pltpu.VMEM((rows, step), BF16),
            pltpu.VMEM((groups, rows, LANES), F32),
            pltpu.VMEM((levels // 2, LANES, LANES), F32),
            pltpu.SemaphoreType.DMA,
        ],
        compiler_params=params,
        name="grid",
    )(*tables, got, pltpu.with_memory_space_constraint(legendre, pltpu.HBM))
    back = lax.all_to_all(tend, ("lev", "wave"), 0, 0, tiled=True)
    out = pl.pallas_call(
        functools.partial(backward_kernel, groups),
        out_shape=jax.ShapeDtypeStruct(spectral.shape, BF16),
        in_specs=[vmem, vmem, vmem],
        out_specs=vmem,
        compiler_params=params,
        name="backward",
    )(kept, leg, back)
    return jnp.transpose(out, (0, 1, 3, 2, 4))


def body(spectral, legendre, wavenumber):
    waves, levels = lax.axis_size("wave"), lax.axis_size("lev")
    lats = legendre.shape[1]
    group_lats = waves * levels * SUB
    groups = lats // (2 * group_lats)
    fits = (
        2 * groups * group_lats == lats
        and wavenumber.shape[0] == waves
        and spectral.shape[1] == 1
        and 2 * waves * SUB == LANES
        and levels % 2 == 0
        and 2 * groups * SUB <= LANES
        and group_lats % LANES == 0
    )
    if fits:
        return fast_body(groups, waves, levels, 2 * LANES, spectral, legendre, wavenumber)
    return general_body(spectral, legendre, wavenumber)


def circle_tables(latitude, band_index, wavenumber, lat_total, band_total, band_cap, wave_total):
    circle_length = 20 + 4 * jnp.minimum(latitude, lat_total - 1 - latitude)
    band_width = (circle_length + band_total - 1) // band_total
    offsets = jnp.arange(band_cap, dtype=jnp.int32)
    longitude_index = band_index[None, :, None] * band_width[:, None, None] + offsets[None, None, :]
    inside = (offsets[None, None, :] < band_width[:, None, None]) & (
        longitude_index < circle_length[:, None, None]
    )
    rows = latitude.shape[0]
    longitude_index = longitude_index.reshape(rows, -1)
    inside = inside.reshape(rows, -1)
    phase_index = (
        wavenumber[None, None, :] * longitude_index[:, :, None] % circle_length[:, None, None]
    )
    length_float = circle_length.astype(jnp.float32)
    angles = 2.0 * math.pi * phase_index.astype(jnp.float32) / length_float[:, None, None]
    shown = inside[:, :, None].astype(jnp.float32)
    trig_basis = jnp.stack([jnp.cos(angles) * shown, -jnp.sin(angles) * shown], axis=2)
    colatitude = (latitude.astype(jnp.float32) + 0.5) * (math.pi / lat_total)
    circle_weight = jnp.sin(colatitude) / jnp.sqrt(length_float)
    synth_table = (trig_basis / math.sqrt(wave_total)).astype(jnp.bfloat16)
    analysis_table = (trig_basis * circle_weight[:, None, None, None]).astype(jnp.bfloat16)
    return (synth_table, analysis_table, 2.0 * jnp.cos(colatitude))


def tendencies(grid_values, planetary):
    vorticity = grid_values[0]
    divergence = grid_values[1]
    absolute_vort = vorticity + planetary[None, :, None]
    column_div = jnp.sum(divergence, axis=0) / math.sqrt(divergence.shape[0])
    return jnp.stack(
        [-absolute_vort * divergence, absolute_vort * vorticity - divergence * column_div[None]]
    ).astype(jnp.bfloat16)


def general_body(spectral, legendre, wavenumber):
    wave_count = lax.axis_size("wave")
    lev_count = lax.axis_size("lev")
    wave_index = lax.axis_index("wave")
    lev_index = lax.axis_index("lev")
    lat_total = legendre.shape[1]
    degree_count = legendre.shape[2]
    set_span = lat_total // wave_count
    wave_total = wavenumber.shape[0]
    own_wave = lax.dynamic_slice_in_dim(wavenumber, wave_index, 1, 0)
    kept_degrees = (
        jnp.arange(degree_count, dtype=jnp.int32)[None, :] <= (degree_count - 1 - own_wave)[:, None]
    )
    masked_spec = jnp.where(kept_degrees, spectral, jnp.zeros_like(spectral))
    fourier = jnp.einsum(
        "flrsn,sjn->flrsj", masked_spec, legendre, preferred_element_type=jnp.float32
    ).astype(jnp.bfloat16)
    circle_max = 20 + 4 * (lat_total // 2 - 1)
    band_cap = (circle_max + lev_count - 1) // lev_count
    latitude = wave_index * set_span + jnp.arange(set_span, dtype=jnp.int32)
    band_index = jnp.reshape(lev_index, (1,))
    synth_table, analysis_table, planetary = circle_tables(
        latitude, band_index, wavenumber, lat_total, lev_count, band_cap, wave_total
    )
    set_fourier = lax.all_to_all(fourier, "wave", split_axis=4, concat_axis=3, tiled=True)
    grid_values = jnp.einsum(
        "flrsq,qprs->flqp",
        lax.all_gather(set_fourier, "lev", axis=1, tiled=True),
        synth_table,
        preferred_element_type=jnp.float32,
    )
    tendency = tendencies(grid_values, planetary)
    summed = lax.psum_scatter(
        jnp.einsum(
            "flqp,qprs->lfrsq", tendency, analysis_table, preferred_element_type=jnp.float32
        ),
        "lev",
        scatter_dimension=0,
        tiled=True,
    )
    returned = lax.all_to_all(
        summed.astype(jnp.bfloat16), "wave", split_axis=3, concat_axis=4, tiled=True
    )
    analysed = jnp.einsum(
        "lfrsj,sjn->flrsn", returned, legendre, preferred_element_type=jnp.float32
    )
    return jnp.where(kept_degrees, analysed, jnp.zeros_like(analysed)).astype(jnp.bfloat16)


def solution(mesh):
    in_specs = (P(None, "lev", None, "wave", None), P("wave", None, None), P())
    out_specs = P(None, "lev", None, "wave", None)
    return jax.shard_map(body, mesh=mesh, in_specs=in_specs, out_specs=out_specs, check_vma=False)
```

```python
import functools
import math

import jax
import jax.numpy as jnp
from jax import lax
from jax.experimental import pallas as pl
from jax.experimental.pallas import tpu as pltpu
from jax.sharding import PartitionSpec as P

SUB = 8
LANES = 128
QUARTERS = 4
FIRST = 5
NT = (((1,), (1,)), ((), ()))
NN = (((1,), (0,)), ((), ()))
F32 = jnp.float32
BF16 = jnp.bfloat16


def dot(a, b, dims):
    return lax.dot_general(a, b, dims, preferred_element_type=F32)


def iota(shape, dim):
    return lax.broadcasted_iota(jnp.int32, shape, dim)


def one_hot(mask):
    return jnp.where(mask, 1.0, 0.0).astype(BF16)


def cos_sin_turns(turns):
    quadrant = jnp.floor(turns * 4.0 + 0.5)
    u = (turns - quadrant * 0.25) * (2.0 * math.pi)
    u2 = u * u
    sine = u * (1.0 + u2 * (-1 / 6 + u2 * (1 / 120 + u2 * (-1 / 5040 + u2 * (1 / 362880)))))
    cosine = 1.0 + u2 * (-0.5 + u2 * (1 / 24 + u2 * (-1 / 720 + u2 * (1 / 40320))))
    quadrant = quadrant.astype(jnp.int32) & 3
    odd = (quadrant & 1) == 1
    c = jnp.where(odd, sine, cosine)
    s = jnp.where(odd, cosine, sine)
    c = jnp.where((quadrant == 1) | (quadrant == 2), -c, c)
    s = jnp.where(quadrant >= 2, -s, s)
    return c, s


def cos_sin_phase(wavenumber, point, circle):
    inverse = 1.0 / circle
    product = wavenumber * point
    whole = jnp.floor(product * inverse + 0.5)
    return cos_sin_turns((product - whole * circle) * inverse)


def quarter_turns(wavenumber, band):
    k = (wavenumber * band) & 3
    c = jnp.where(k == 0, 1.0, jnp.where(k == 2, -1.0, 0.0))
    s = jnp.where(k == 1, 1.0, jnp.where(k == 3, -1.0, 0.0))
    return c, s


def plain_part(group, south):
    return (group % 2 == 0) != south


def block_place(block, groups):
    south = block >= groups
    return (2 * groups - 1 - block if south else block), south


def reverse_matrix(n):
    return one_hot(iota((n, n), 0) + iota((n, n), 1) == n - 1)


def forward_kernel(groups, wn_hbm, spec_hbm, leg_hbm, out_ref, kept_ref, leg, wn, spec, sems):
    block = leg.shape[1]
    first = [
        pltpu.make_async_copy(wn_hbm, wn, sems.at[2 * groups]),
        pltpu.make_async_copy(spec_hbm, spec, sems.at[2 * groups + 1]),
    ]
    copies = [
        pltpu.make_async_copy(
            leg_hbm.at[0, pl.ds(k * block, 2 * block)].reshape(2, block, leg.shape[2]),
            leg.at[pl.ds(k, 2)],
            sems.at[k],
        )
        for k in range(0, 2 * groups, 2)
    ]
    for copy in first + copies:
        copy.start()
    for copy in first:
        copy.wait()
    degrees = leg.shape[2]
    kept = iota((SUB, degrees), 1) <= degrees - 1 - wn[lax.axis_index("wave")]
    kept_ref[...] = jnp.where(kept, 1.0, 0.0)
    rows = [spec[f, 0, 0].astype(F32) for f in range(2)]
    rows = jnp.concatenate(rows + [jnp.zeros((SUB - 4, degrees), F32)], axis=0)
    rows = jnp.where(kept, rows, 0.0)
    rows = rows.astype(BF16)
    pieces = [[], []]
    for k in range(2 * groups):
        group, south = block_place(k, groups)
        if k % 2 == 0:
            copies[k // 2].wait()
        pieces[0 if plain_part(group, south) else 1].append((group, dot(rows, leg[k], NT)))
    pieces = [[v for _, v in sorted(p, key=lambda x: x[0])] for p in pieces]
    blank = jnp.zeros((SUB, block), F32)
    n = LANES // SUB
    plain = jnp.concatenate(pieces[0] + [blank] * (n - groups), axis=0)
    turned = jnp.concatenate([blank] * groups + pieces[1] + [blank] * (n - 2 * groups), axis=0)
    placed = jnp.transpose(plain) + dot(reverse_matrix(block), turned.astype(BF16), NT)
    out_ref[...] = placed.astype(BF16).reshape(out_ref.shape)


def backward_kernel(groups, kept_ref, leg, got_ref, out_ref):
    degrees = leg.shape[2]
    block = leg.shape[1] // (2 * groups)
    got = got_ref[...].reshape(block, LANES)
    shape = (groups * SUB, LANES)
    row, lane = iota(shape, 0), iota(shape, 1)
    group, field, part = row // SUB, (row % SUB) // 2, row % 2
    source = group * SUB + part * 4 + field * 2
    used = row % SUB < 4
    odd = group % 2
    plain = dot(one_hot(used & (lane == source + odd)), got, NT).astype(BF16)
    turned = dot(one_hot(used & (lane == source + 1 - odd)), got, NT).astype(BF16)
    turned = dot(turned, reverse_matrix(block), NN).astype(BF16)
    total = jnp.zeros((SUB, degrees), F32)
    for k in range(2 * groups):
        g, south = block_place(k, groups)
        rows = plain if plain_part(g, south) else turned
        total = total + dot(
            rows[g * SUB : (g + 1) * SUB], leg[0, k * block : (k + 1) * block, :], NN
        )
    total = (total * kept_ref[...]).astype(BF16)
    for f in range(2):
        out_ref[f, 0, 0] = total[f * 2 : f * 2 + 2]


def chunk_counts(groups, block, step):
    return [-(-(FIRST + block * (g + 1) - 1) // step) for g in range(groups)]


def latitude(group, block, order):
    return group * block + (order if group % 2 == 0 else block - 1 - order)


def step_counts(groups, block, step, device, largest):
    counts = []
    for g in range(groups):
        ends = [latitude(g, block, device * SUB + q) for q in (0, SUB - 1)]
        counts.append((FIRST + largest(*ends) + step - 1) // step)
    return counts


def this_device(waves):
    return lax.axis_index("lev") * waves + lax.axis_index("wave")


def tables_kernel(
    groups, waves, levels, lats, step, wn_hbm, synth, analysis, planet, turns, backs, wn, sem
):
    copy = pltpu.make_async_copy(wn_hbm, wn, sem)
    copy.start()
    block = waves * levels * SUB
    half = waves * SUB
    device = this_device(waves)
    copy.wait()
    numbers = [wn[s] for s in range(waves)]

    def slot_number(lanes):
        value = jnp.zeros(lanes.shape, jnp.int32)
        for s in range(waves):
            value = jnp.where(lanes == s, numbers[s], value)
        return value

    shape = (SUB, block)
    turns[0], turns[1] = quarter_turns(
        slot_number((iota(shape, 1) // SUB) % waves), iota(shape, 0) // 2
    )
    shape = (SUB, LANES)
    lane = iota(shape, 1)
    back_c, back_s = quarter_turns(slot_number((lane // SUB) % waves), iota(shape, 0) // 2)
    backs[0], backs[1] = back_c, jnp.where(lane < half, back_s, -back_s)

    def wide(x):
        return jnp.concatenate([x] * (step // LANES), axis=1)

    slot = 0
    for g, count in enumerate(chunk_counts(groups, block, step)):
        lat = latitude(g, block, device * SUB + iota((SUB, LANES), 0)).astype(F32)
        quarter = lat + FIRST
        circle = QUARTERS * quarter
        weight = cos_sin_turns((lat + 0.5) * (0.5 / lats))[1] / jnp.sqrt(circle)
        row = iota((SUB * SUB, LANES), 0)
        lat_row = latitude(g, block, device * SUB + row // SUB).astype(F32)
        planetary = 2.0 * cos_sin_turns((lat_row + 0.5) * (0.5 / lats))[0]
        planet[g] = wide(jnp.where(row % 2 == 0, planetary, -planetary))

        point = iota((SUB, step), 1)
        start = [
            cos_sin_phase(numbers[s].astype(F32), point.astype(F32), wide(circle))
            for s in range(waves)
        ]
        turn = [cos_sin_phase((numbers[s] * step).astype(F32), 1.0, circle) for s in range(waves)]
        quarter, weight = wide(quarter).astype(jnp.int32), wide(weight)
        for s in range(0, waves, 2):
            pair = [start[s], start[s + 1]]
            for a in range(count):
                shown = point + a * step < quarter
                rows = pl.ds(s * SUB, 2 * SUB), pl.ds(half + s * SUB, 2 * SUB)
                for part, at in enumerate(rows):
                    basis = [-v[1] if part else v[0] for v in pair]
                    synth[slot + a, at, :] = jnp.concatenate(
                        [v * (1.0 / math.sqrt(waves)) for v in basis], axis=0
                    ).astype(BF16)
                    analysis[slot + a, at, :] = jnp.concatenate(
                        [jnp.where(shown, v * weight, 0.0) for v in basis], axis=0
                    ).astype(BF16)
                if a + 1 < count:
                    pair = [
                        (
                            c * wide(turn[s + k][0]) - n * wide(turn[s + k][1]),
                            n * wide(turn[s + k][0]) + c * wide(turn[s + k][1]),
                        )
                        for k, (c, n) in enumerate(pair)
                    ]
        slot += count
    analysis[slot] = jnp.zeros(analysis.shape[1:], BF16)


def grid_kernel(
    groups, waves, levels, step, synth, analysis, planet, turns, backs, got_ref, leg_hbm, out_ref, leg,
    coef, grid_a, grid_b, tend_a, tend_b, total, kept, sem,
):
    ahead = pltpu.make_async_copy(leg_hbm, leg, sem)
    ahead.start()
    block = waves * levels * SUB
    half = waves * SUB
    device = this_device(waves)
    row, lane = iota((SUB, LANES), 0), iota((SUB, LANES), 1)
    first = lane < half
    which = lane % SUB

    got = got_ref[...].reshape(block, LANES)
    shape = (groups * 4 * SUB, LANES)
    row_of, lane_of = iota(shape, 0), iota(shape, 1)
    group, pair, south = row_of // (4 * SUB), (row_of // SUB) % 4, row_of % 2
    source = (group + south) % 2 * (groups * SUB) + group * SUB + pair
    fourier = dot(one_hot(lane_of == source), got, NT)
    turn_c, turn_s = turns[0], turns[1]

    for g in range(groups):
        for f in range(2):
            base = (g * 4 + f * 2) * SUB
            real, imag = fourier[base : base + SUB], fourier[base + SUB : base + 2 * SUB]
            turned_r = real * turn_c - imag * turn_s
            turned_i = real * turn_s + imag * turn_c
            for l in range(levels):
                cut = slice((l // 2) * LANES, (l // 2 + 1) * LANES)
                a, b = turned_r[:, cut], turned_i[:, cut]
                if l % 2 == 0:
                    b = pltpu.roll(b, half, 1)
                else:
                    a = pltpu.roll(a, half, 1)
                both = jnp.where(first, a, b)
                for q in range(0, SUB, 2):
                    place = ((f * levels + l) * SUB + q) * SUB
                    two = jnp.concatenate(
                        [jnp.where(which == q + k, both, 0.0) for k in range(2)], axis=0
                    )
                    coef[g, place : place + 2 * SUB, :] = two.astype(BF16)

    most = chunk_counts(groups, block, step)
    ends, skips = [], []
    end = 0
    for g, count in enumerate(step_counts(groups, block, step, device, jnp.maximum)):
        end = end + count
        ends.append(end)
        skips.append(most[g] - count)
    devices = waves * levels
    steps = max(sum(step_counts(groups, block, step, d, max)) for d in range(devices))

    def place_of(i):
        group, slot = jnp.int32(0), i
        for g in range(groups - 1):
            past = i >= ends[g]
            group = group + jnp.where(past, 1, 0)
            slot = slot + jnp.where(past, skips[g], 0)
        return group, slot

    total[...] = jnp.zeros_like(total)
    rows = levels * SUB * SUB

    def synthesis(i, values):
        group, slot = place_of(jnp.minimum(i, end - 1))
        values[...] = dot(coef[group], synth[slot], NN)

    def tendencies_of(i, values, tend):
        group, _ = place_of(jnp.minimum(i, end - 1))
        for r in range(0, SUB * SUB, 2 * SUB):
            at = [pl.ds(l * SUB * SUB + r, 2 * SUB) for l in range(levels)]
            below = [pl.ds(rows + l * SUB * SUB + r, 2 * SUB) for l in range(levels)]
            div = [values[b, :] for b in below]
            column = div[0]
            for l in range(1, levels):
                column = column + div[l]
            column = column * (1.0 / math.sqrt(levels))
            turning = planet[group, pl.ds(r, 2 * SUB), :]
            for l in range(levels):
                vort = values[at[l], :]
                absolute = vort + turning
                tend[at[l], :] = (-absolute * div[l]).astype(BF16)
                tend[below[l], :] = (absolute * vort - div[l] * column).astype(BF16)

    def analysis_of(i, tend):
        group, slot = place_of(jnp.minimum(i, end - 1))
        slot = jnp.where(i < end, slot, sum(most))
        total[group] += dot(tend[...], analysis[slot], NT)

    grids, tends = (grid_a, grid_b), (tend_a, tend_b)

    @pl.loop(0, jnp.minimum(end, 1))
    def _(_):
        for i in range(steps + 2):
            if i < steps:
                synthesis(i, grids[i % 2])
            if 1 <= i <= steps:
                tendencies_of(i - 1, grids[(i - 1) % 2], tends[(i - 1) % 2])
            if i >= 2:
                analysis_of(i - 2, tends[i % 2])

    back_c, back_s = backs[0], backs[1]
    kept[...] = jnp.zeros_like(kept)
    for g in range(groups):
        sums = []
        for f in range(2):
            for l in range(levels):
                base = (f * levels + l) * SUB * SUB
                value = jnp.zeros((SUB, LANES), F32)
                for q in range(SUB):
                    part = total[g, base + q * SUB : base + (q + 1) * SUB, :]
                    value = jnp.where(which == q, part, value)
                value = value * back_c + pltpu.roll(value, half, 1) * back_s
                value = value + pltpu.roll(value, 4, 0)
                sums.append(value + pltpu.roll(value, 2, 0))
        lined = []
        for l in range(levels):
            both = jnp.where(row % 4 < 2, sums[l], sums[levels + l])
            lined.append(jnp.where(row < 4, both, pltpu.roll(both, half, 1)))
        for p in range(levels // 2):
            kept[p, g * SUB : (g + 1) * SUB, :] = jnp.where(
                first, lined[2 * p], pltpu.roll(lined[2 * p + 1], half, 1)
            )
    for p in range(levels // 2):
        moved = jnp.transpose(kept[p]).astype(BF16)
        out_ref[p * 2 * waves : (p + 1) * 2 * waves] = moved.reshape(2 * waves, SUB, LANES)
    ahead.wait()


def fast_body(groups, waves, levels, step, spectral, legendre, wavenumber):
    lats, degrees = legendre.shape[1:]
    devices = waves * levels
    block = devices * SUB
    vmem = pl.BlockSpec(memory_space=pltpu.VMEM)
    hbm = pl.BlockSpec(memory_space=pltpu.HBM)
    params = pltpu.CompilerParams(vmem_limit_bytes=24 * 1024 * 1024)
    parcel = jax.ShapeDtypeStruct((devices, SUB, LANES), BF16)
    spectral = jnp.transpose(spectral, (0, 1, 3, 2, 4))
    sent, kept = pl.pallas_call(
        functools.partial(forward_kernel, groups),
        out_shape=[
            parcel,
            jax.ShapeDtypeStruct((SUB, degrees), F32),
        ],
        in_specs=[hbm, hbm, hbm],
        out_specs=[vmem] * 2,
        scratch_shapes=[
            pltpu.VMEM((2 * groups, block, degrees), BF16),
            pltpu.SMEM(wavenumber.shape, jnp.int32),
            pltpu.VMEM(spectral.shape, BF16),
            pltpu.SemaphoreType.DMA((2 * groups + 2,)),
        ],
        compiler_params=params,
        name="forward",
    )(*(pltpu.with_memory_space_constraint(x, pltpu.HBM) for x in (wavenumber, spectral, legendre)))
    got = lax.all_to_all(sent, ("lev", "wave"), 0, 0, tiled=True)
    rows = 2 * levels * SUB * SUB
    slots = sum(chunk_counts(groups, block, step))
    tables = pl.pallas_call(
        functools.partial(tables_kernel, groups, waves, levels, lats, step),
        out_shape=[
            jax.ShapeDtypeStruct((slots, LANES, step), BF16),
            jax.ShapeDtypeStruct((slots + 1, LANES, step), BF16),
            jax.ShapeDtypeStruct((groups, SUB * SUB, step), F32),
            jax.ShapeDtypeStruct((2, SUB, block), F32),
            jax.ShapeDtypeStruct((2, SUB, LANES), F32),
        ],
        in_specs=[hbm],
        out_specs=[vmem] * 5,
        scratch_shapes=[pltpu.SMEM(wavenumber.shape, jnp.int32), pltpu.SemaphoreType.DMA],
        compiler_params=params,
        name="tables",
    )(pltpu.with_memory_space_constraint(wavenumber, pltpu.HBM))
    tend, leg = pl.pallas_call(
        functools.partial(grid_kernel, groups, waves, levels, step),
        out_shape=[parcel, jax.ShapeDtypeStruct(legendre.shape, BF16)],
        in_specs=[vmem] * 6 + [hbm],
        out_specs=[vmem] * 2,
        scratch_shapes=[
            pltpu.VMEM((groups, rows, LANES), BF16),
            pltpu.VMEM((rows, step), F32),
            pltpu.VMEM((rows, step), F32),
            pltpu.VMEM((rows, step), BF16),
            pltpu.VMEM((rows, step), BF16),
            pltpu.VMEM((groups, rows, LANES), F32),
            pltpu.VMEM((levels // 2, LANES, LANES), F32),
            pltpu.SemaphoreType.DMA,
        ],
        compiler_params=params,
        name="grid",
    )(*tables, got, pltpu.with_memory_space_constraint(legendre, pltpu.HBM))
    back = lax.all_to_all(tend, ("lev", "wave"), 0, 0, tiled=True)
    out = pl.pallas_call(
        functools.partial(backward_kernel, groups),
        out_shape=jax.ShapeDtypeStruct(spectral.shape, BF16),
        in_specs=[vmem, vmem, vmem],
        out_specs=vmem,
        compiler_params=params,
        name="backward",
    )(kept, leg, back)
    return jnp.transpose(out, (0, 1, 3, 2, 4))


def body(spectral, legendre, wavenumber):
    waves, levels = lax.axis_size("wave"), lax.axis_size("lev")
    lats = legendre.shape[1]
    group_lats = waves * levels * SUB
    groups = lats // (2 * group_lats)
    fits = (
        2 * groups * group_lats == lats
        and wavenumber.shape[0] == waves
        and spectral.shape[1] == 1
        and 2 * waves * SUB == LANES
        and levels % 2 == 0
        and 2 * groups * SUB <= LANES
        and group_lats % LANES == 0
    )
    if fits:
        return fast_body(groups, waves, levels, 2 * LANES, spectral, legendre, wavenumber)
    return general_body(spectral, legendre, wavenumber)


def circle_tables(latitude, band_index, wavenumber, lat_total, band_total, band_cap, wave_total):
    circle_length = 20 + 4 * jnp.minimum(latitude, lat_total - 1 - latitude)
    band_width = (circle_length + band_total - 1) // band_total
    offsets = jnp.arange(band_cap, dtype=jnp.int32)
    longitude_index = band_index[None, :, None] * band_width[:, None, None] + offsets[None, None, :]
    inside = (offsets[None, None, :] < band_width[:, None, None]) & (
        longitude_index < circle_length[:, None, None]
    )
    rows = latitude.shape[0]
    longitude_index = longitude_index.reshape(rows, -1)
    inside = inside.reshape(rows, -1)
    phase_index = (
        wavenumber[None, None, :] * longitude_index[:, :, None] % circle_length[:, None, None]
    )
    length_float = circle_length.astype(jnp.float32)
    angles = 2.0 * math.pi * phase_index.astype(jnp.float32) / length_float[:, None, None]
    shown = inside[:, :, None].astype(jnp.float32)
    trig_basis = jnp.stack([jnp.cos(angles) * shown, -jnp.sin(angles) * shown], axis=2)
    colatitude = (latitude.astype(jnp.float32) + 0.5) * (math.pi / lat_total)
    circle_weight = jnp.sin(colatitude) / jnp.sqrt(length_float)
    synth_table = (trig_basis / math.sqrt(wave_total)).astype(jnp.bfloat16)
    analysis_table = (trig_basis * circle_weight[:, None, None, None]).astype(jnp.bfloat16)
    return (synth_table, analysis_table, 2.0 * jnp.cos(colatitude))


def tendencies(grid_values, planetary):
    vorticity = grid_values[0]
    divergence = grid_values[1]
    absolute_vort = vorticity + planetary[None, :, None]
    column_div = jnp.sum(divergence, axis=0) / math.sqrt(divergence.shape[0])
    return jnp.stack(
        [-absolute_vort * divergence, absolute_vort * vorticity - divergence * column_div[None]]
    ).astype(jnp.bfloat16)


def general_body(spectral, legendre, wavenumber):
    wave_count = lax.axis_size("wave")
    lev_count = lax.axis_size("lev")
    wave_index = lax.axis_index("wave")
    lev_index = lax.axis_index("lev")
    lat_total = legendre.shape[1]
    degree_count = legendre.shape[2]
    set_span = lat_total // wave_count
    wave_total = wavenumber.shape[0]
    own_wave = lax.dynamic_slice_in_dim(wavenumber, wave_index, 1, 0)
    kept_degrees = (
        jnp.arange(degree_count, dtype=jnp.int32)[None, :] <= (degree_count - 1 - own_wave)[:, None]
    )
    masked_spec = jnp.where(kept_degrees, spectral, jnp.zeros_like(spectral))
    fourier = jnp.einsum(
        "flrsn,sjn->flrsj", masked_spec, legendre, preferred_element_type=jnp.float32
    ).astype(jnp.bfloat16)
    circle_max = 20 + 4 * (lat_total // 2 - 1)
    band_cap = (circle_max + lev_count - 1) // lev_count
    latitude = wave_index * set_span + jnp.arange(set_span, dtype=jnp.int32)
    band_index = jnp.reshape(lev_index, (1,))
    synth_table, analysis_table, planetary = circle_tables(
        latitude, band_index, wavenumber, lat_total, lev_count, band_cap, wave_total
    )
    set_fourier = lax.all_to_all(fourier, "wave", split_axis=4, concat_axis=3, tiled=True)
    grid_values = jnp.einsum(
        "flrsq,qprs->flqp",
        lax.all_gather(set_fourier, "lev", axis=1, tiled=True),
        synth_table,
        preferred_element_type=jnp.float32,
    )
    tendency = tendencies(grid_values, planetary)
    summed = lax.psum_scatter(
        jnp.einsum(
            "flqp,qprs->lfrsq", tendency, analysis_table, preferred_element_type=jnp.float32
        ),
        "lev",
        scatter_dimension=0,
        tiled=True,
    )
    returned = lax.all_to_all(
        summed.astype(jnp.bfloat16), "wave", split_axis=3, concat_axis=4, tiled=True
    )
    analysed = jnp.einsum(
        "lfrsj,sjn->flrsn", returned, legendre, preferred_element_type=jnp.float32
    )
    return jnp.where(kept_degrees, analysed, jnp.zeros_like(analysed)).astype(jnp.bfloat16)


def solution(mesh):
    in_specs = (P(None, "lev", None, "wave", None), P("wave", None, None), P())
    out_specs = P(None, "lev", None, "wave", None)
    return jax.shard_map(body, mesh=mesh, in_specs=in_specs, out_specs=out_specs, check_vma=False)
```

```python
import functools
import math

import jax
import jax.numpy as jnp
from jax import lax
from jax.experimental import pallas as pl
from jax.experimental.pallas import tpu as pltpu
from jax.sharding import PartitionSpec as P

SUB = 8
LANES = 128
QUARTERS = 4
FIRST = 5
NT = (((1,), (1,)), ((), ()))
NN = (((1,), (0,)), ((), ()))
F32 = jnp.float32
BF16 = jnp.bfloat16


def dot(a, b, dims):
    return lax.dot_general(a, b, dims, preferred_element_type=F32)


def iota(shape, dim):
    return lax.broadcasted_iota(jnp.int32, shape, dim)


def one_hot(mask):
    return jnp.where(mask, 1.0, 0.0).astype(BF16)


def cos_sin_turns(turns):
    quadrant = jnp.floor(turns * 4.0 + 0.5)
    u = (turns - quadrant * 0.25) * (2.0 * math.pi)
    u2 = u * u
    sine = u * (1.0 + u2 * (-1 / 6 + u2 * (1 / 120 + u2 * (-1 / 5040 + u2 * (1 / 362880)))))
    cosine = 1.0 + u2 * (-0.5 + u2 * (1 / 24 + u2 * (-1 / 720 + u2 * (1 / 40320))))
    quadrant = quadrant.astype(jnp.int32) & 3
    odd = (quadrant & 1) == 1
    c = jnp.where(odd, sine, cosine)
    s = jnp.where(odd, cosine, sine)
    c = jnp.where((quadrant == 1) | (quadrant == 2), -c, c)
    s = jnp.where(quadrant >= 2, -s, s)
    return c, s


def cos_sin_phase(wavenumber, point, circle):
    inverse = 1.0 / circle
    product = wavenumber * point
    whole = jnp.floor(product * inverse + 0.5)
    return cos_sin_turns((product - whole * circle) * inverse)


def quarter_turns(wavenumber, band):
    k = (wavenumber * band) & 3
    c = jnp.where(k == 0, 1.0, jnp.where(k == 2, -1.0, 0.0))
    s = jnp.where(k == 1, 1.0, jnp.where(k == 3, -1.0, 0.0))
    return c, s


def plain_part(group, south):
    return (group % 2 == 0) != south


def block_place(block, groups):
    south = block >= groups
    return (2 * groups - 1 - block if south else block), south


def reverse_matrix(n):
    return one_hot(iota((n, n), 0) + iota((n, n), 1) == n - 1)


def forward_kernel(
    groups, waves, levels, lats, wn_hbm, spec_hbm, leg_hbm,
    out_ref, kept_ref, leg, synth, analysis, planet, turns, backs, wn, spec, sems,
):
    block = leg.shape[1]
    first = [
        pltpu.make_async_copy(wn_hbm, wn, sems.at[2 * groups]),
        pltpu.make_async_copy(spec_hbm, spec, sems.at[2 * groups + 1]),
    ]
    copies = [
        pltpu.make_async_copy(
            leg_hbm.at[0, pl.ds(k * block, 2 * block)].reshape(2, block, leg.shape[2]),
            leg.at[pl.ds(k, 2)],
            sems.at[k],
        )
        for k in range(0, 2 * groups, 2)
    ]
    for copy in first + copies:
        copy.start()
    for copy in first:
        copy.wait()
    degrees = leg.shape[2]
    kept = iota((SUB, degrees), 1) <= degrees - 1 - wn[lax.axis_index("wave")]
    kept_ref[...] = jnp.where(kept, 1.0, 0.0)
    rows = [spec[f, 0, 0].astype(F32) for f in range(2)]
    rows = jnp.concatenate(rows + [jnp.zeros((SUB - 4, degrees), F32)], axis=0)
    rows = jnp.where(kept, rows, 0.0)
    rows = rows.astype(BF16)
    pieces = [[], []]
    device = this_device(waves)
    numbers = [wn[w] for w in range(waves)]
    counts = chunk_counts(groups, block, synth.shape[2])
    turn_tables(waves, numbers, turns, backs)
    analysis[sum(counts)] = jnp.zeros(analysis.shape[1:], BF16)
    for k in range(2 * groups):
        group, south = block_place(k, groups)
        if k % 2 == 0:
            g = groups - 1 - k // 2
            group_tables(
                g, sum(counts[:g]), counts[g], waves, block, lats, numbers, device,
                synth, analysis, planet,
            )
            copies[k // 2].wait()
        pieces[0 if plain_part(group, south) else 1].append((group, dot(rows, leg[k], NT)))
    pieces = [[v for _, v in sorted(p, key=lambda x: x[0])] for p in pieces]
    blank = jnp.zeros((SUB, block), F32)
    n = LANES // SUB
    plain = jnp.concatenate(pieces[0] + [blank] * (n - groups), axis=0)
    turned = jnp.concatenate([blank] * groups + pieces[1] + [blank] * (n - 2 * groups), axis=0)
    placed = jnp.transpose(plain) + dot(reverse_matrix(block), turned.astype(BF16), NT)
    out_ref[...] = placed.astype(BF16).reshape(out_ref.shape)


def backward_kernel(groups, kept_ref, leg, got_ref, out_ref):
    block, degrees = leg.shape[1:]
    got = got_ref[...].reshape(block, LANES)
    shape = (groups * SUB, LANES)
    row, lane = iota(shape, 0), iota(shape, 1)
    group, field, part = row // SUB, (row % SUB) // 2, row % 2
    source = group * SUB + part * 4 + field * 2
    used = row % SUB < 4
    odd = group % 2
    plain = dot(one_hot(used & (lane == source + odd)), got, NT).astype(BF16)
    turned = dot(one_hot(used & (lane == source + 1 - odd)), got, NT).astype(BF16)
    turned = dot(turned, reverse_matrix(block), NN).astype(BF16)
    total = jnp.zeros((SUB, degrees), F32)
    order = sorted(range(2 * groups), key=lambda k: not plain_part(*block_place(k, groups)))
    for k in order:
        g, south = block_place(k, groups)
        rows = plain if plain_part(g, south) else turned
        total = total + dot(rows[g * SUB : (g + 1) * SUB], leg[k], NN)
    total = (total * kept_ref[...]).astype(BF16)
    for f in range(2):
        out_ref[f, 0, 0] = total[f * 2 : f * 2 + 2]


def chunk_counts(groups, block, step):
    return [-(-(FIRST + block * (g + 1) - 1) // step) for g in range(groups)]


def latitude(group, block, order):
    return group * block + (order if group % 2 == 0 else block - 1 - order)


def step_counts(groups, block, step, device, largest):
    counts = []
    for g in range(groups):
        ends = [latitude(g, block, device * SUB + q) for q in (0, SUB - 1)]
        counts.append((FIRST + largest(*ends) + step - 1) // step)
    return counts


def this_device(waves):
    return lax.axis_index("lev") * waves + lax.axis_index("wave")


def turn_tables(waves, numbers, turns, backs):
    half = waves * SUB

    def slot_number(lanes):
        value = jnp.zeros(lanes.shape, jnp.int32)
        for s in range(waves):
            value = jnp.where(lanes == s, numbers[s], value)
        return value

    shape = turns.shape[1:]
    turns[0], turns[1] = quarter_turns(
        slot_number((iota(shape, 1) // SUB) % waves), iota(shape, 0) // 2
    )
    shape = backs.shape[1:]
    lane = iota(shape, 1)
    back_c, back_s = quarter_turns(slot_number((lane // SUB) % waves), iota(shape, 0) // 2)
    backs[0], backs[1] = back_c, jnp.where(lane < half, back_s, -back_s)


def group_tables(g, slot, count, waves, block, lats, numbers, device, synth, analysis, planet):
    half = waves * SUB
    step = synth.shape[2]
    shape = (SUB, LANES)
    lat = latitude(g, block, device * SUB + iota(shape, 0)).astype(F32)
    quarter = lat + FIRST
    circle = QUARTERS * quarter
    polar_c, polar_s = cos_sin_turns((lat + 0.5) * (0.5 / lats))
    scale = 1.0 / math.sqrt(waves)
    weight = polar_s / jnp.sqrt(circle) * (1.0 / scale)
    sign = jnp.where(iota(shape, 0) % 2 == 0, 2.0, -2.0)
    for q in range(SUB):
        value = jnp.broadcast_to(polar_c[q : q + 1], shape) * sign
        for part in range(step // LANES):
            planet[g, q * SUB : (q + 1) * SUB, part * LANES : (part + 1) * LANES] = value

    point = iota(shape, 1)
    inside = quarter.astype(jnp.int32)
    for s in range(0, waves, 2):
        pair, turn = [], []
        for k in range(2):
            c, n = cos_sin_phase(numbers[s + k].astype(F32), point.astype(F32), circle)
            mid_c = jnp.broadcast_to(c[:, LANES // 2 : LANES // 2 + 1], shape)
            mid_s = jnp.broadcast_to(n[:, LANES // 2 : LANES // 2 + 1], shape)
            turn.append((mid_c * mid_c - mid_s * mid_s, 2.0 * mid_c * mid_s))
            pair.append((c * scale, n * -scale))
        for a in range(count * (step // LANES)):
            at = slot + a * LANES // step
            lanes = pl.ds(a * LANES % step, LANES)
            for part in range(2):
                rows = pl.ds(part * half + s * SUB, 2 * SUB)
                basis = [v[part] for v in pair]
                synth[at, rows, lanes] = jnp.concatenate(basis, axis=0).astype(BF16)
                basis = [v * weight for v in basis]
                if (a + 1) * LANES > FIRST + g * block:
                    basis = [jnp.where(point + a * LANES < inside, v, 0.0) for v in basis]
                analysis[at, rows, lanes] = jnp.concatenate(basis, axis=0).astype(BF16)
            pair = [
                (c * tc + n * ts, n * tc - c * ts) for (c, n), (tc, ts) in zip(pair, turn)
            ]


def grid_kernel(
    groups, waves, levels, step, synth, analysis, planet, turns, backs, got_ref, out_ref,
    coef, grid_a, grid_b, tend_a, tend_b, total, kept,
):
    block = waves * levels * SUB
    half = waves * SUB
    device = this_device(waves)
    row, lane = iota((SUB, LANES), 0), iota((SUB, LANES), 1)
    first = lane < half
    which = lane % SUB

    got = got_ref[...].reshape(block, LANES)
    shape = (groups * 4 * SUB, LANES)
    row_of, lane_of = iota(shape, 0), iota(shape, 1)
    group, pair, south = row_of // (4 * SUB), (row_of // SUB) % 4, row_of % 2
    source = (group + south) % 2 * (groups * SUB) + group * SUB + pair
    fourier = dot(one_hot(lane_of == source), got, NT)
    turn_c, turn_s = turns[0], turns[1]

    for g in range(groups):
        for f in range(2):
            base = (g * 4 + f * 2) * SUB
            real, imag = fourier[base : base + SUB], fourier[base + SUB : base + 2 * SUB]
            turned_r = real * turn_c - imag * turn_s
            turned_i = real * turn_s + imag * turn_c
            for l in range(levels):
                cut = slice((l // 2) * LANES, (l // 2 + 1) * LANES)
                a, b = turned_r[:, cut], turned_i[:, cut]
                if l % 2 == 0:
                    b = pltpu.roll(b, half, 1)
                else:
                    a = pltpu.roll(a, half, 1)
                both = jnp.where(first, a, b)
                for q in range(0, SUB, 2):
                    place = ((f * levels + l) * SUB + q) * SUB
                    two = jnp.concatenate(
                        [jnp.where(which == q + k, both, 0.0) for k in range(2)], axis=0
                    )
                    coef[g, place : place + 2 * SUB, :] = two.astype(BF16)

    most = chunk_counts(groups, block, step)
    ends, skips = [], []
    end = 0
    for g, count in enumerate(step_counts(groups, block, step, device, jnp.maximum)):
        end = end + count
        ends.append(end)
        skips.append(most[g] - count)
    devices = waves * levels
    steps = max(sum(step_counts(groups, block, step, d, max)) for d in range(devices))

    def place_of(i):
        group, slot = jnp.int32(0), i
        for g in range(groups - 1):
            past = i >= ends[g]
            group = group + jnp.where(past, 1, 0)
            slot = slot + jnp.where(past, skips[g], 0)
        return group, slot

    total[...] = jnp.zeros_like(total)
    rows = levels * SUB * SUB

    def synthesis(i, values):
        group, slot = place_of(jnp.minimum(i, end - 1))
        values[...] = dot(coef[group], synth[slot], NN)

    def tendencies_of(i, values, tend):
        group, _ = place_of(jnp.minimum(i, end - 1))
        for r in range(0, SUB * SUB, 2 * SUB):
            at = [pl.ds(l * SUB * SUB + r, 2 * SUB) for l in range(levels)]
            below = [pl.ds(rows + l * SUB * SUB + r, 2 * SUB) for l in range(levels)]
            div = [values[b, :] for b in below]
            column = div[0]
            for l in range(1, levels):
                column = column + div[l]
            column = column * (1.0 / math.sqrt(levels))
            turning = planet[group, pl.ds(r, 2 * SUB), :]
            for l in range(levels):
                vort = values[at[l], :]
                absolute = vort + turning
                tend[at[l], :] = (-absolute * div[l]).astype(BF16)
                tend[below[l], :] = (absolute * vort - div[l] * column).astype(BF16)

    def analysis_of(i, tend):
        group, slot = place_of(jnp.minimum(i, end - 1))
        slot = jnp.where(i < end, slot, sum(most))
        total[group] += dot(tend[...], analysis[slot], NT)

    grids, tends = (grid_a, grid_b), (tend_a, tend_b)

    @pl.loop(0, jnp.minimum(end, 1))
    def _(_):
        for i in range(steps + 2):
            if i < steps:
                synthesis(i, grids[i % 2])
            if 1 <= i <= steps:
                tendencies_of(i - 1, grids[(i - 1) % 2], tends[(i - 1) % 2])
            if i >= 2:
                analysis_of(i - 2, tends[i % 2])

    back_c, back_s = backs[0], backs[1]
    kept[...] = jnp.zeros_like(kept)
    for g in range(groups):
        sums = []
        for f in range(2):
            for l in range(levels):
                base = (f * levels + l) * SUB * SUB
                value = jnp.zeros((SUB, LANES), F32)
                for q in range(SUB):
                    part = total[g, base + q * SUB : base + (q + 1) * SUB, :]
                    value = jnp.where(which == q, part, value)
                value = value * back_c + pltpu.roll(value, half, 1) * back_s
                value = value + pltpu.roll(value, 4, 0)
                sums.append(value + pltpu.roll(value, 2, 0))
        lined = []
        for l in range(levels):
            both = jnp.where(row % 4 < 2, sums[l], sums[levels + l])
            lined.append(jnp.where(row < 4, both, pltpu.roll(both, half, 1)))
        for p in range(levels // 2):
            kept[p, g * SUB : (g + 1) * SUB, :] = jnp.where(
                first, lined[2 * p], pltpu.roll(lined[2 * p + 1], half, 1)
            )
    for p in range(levels // 2):
        moved = jnp.transpose(kept[p]).astype(BF16)
        out_ref[p * 2 * waves : (p + 1) * 2 * waves] = moved.reshape(2 * waves, SUB, LANES)


def fast_body(groups, waves, levels, step, spectral, legendre, wavenumber):
    lats, degrees = legendre.shape[1:]
    devices = waves * levels
    block = devices * SUB
    vmem = pl.BlockSpec(memory_space=pltpu.VMEM)
    hbm = pl.BlockSpec(memory_space=pltpu.HBM)
    params = pltpu.CompilerParams(vmem_limit_bytes=24 * 1024 * 1024)
    parcel = jax.ShapeDtypeStruct((devices, SUB, LANES), BF16)
    spectral = jnp.transpose(spectral, (0, 1, 3, 2, 4))
    slots = sum(chunk_counts(groups, block, step))
    sent, kept, leg, *tables = pl.pallas_call(
        functools.partial(forward_kernel, groups, waves, levels, lats),
        out_shape=[
            parcel,
            jax.ShapeDtypeStruct((SUB, degrees), F32),
            jax.ShapeDtypeStruct((2 * groups, block, degrees), BF16),
            jax.ShapeDtypeStruct((slots, LANES, step), BF16),
            jax.ShapeDtypeStruct((slots + 1, LANES, step), BF16),
            jax.ShapeDtypeStruct((groups, SUB * SUB, step), F32),
            jax.ShapeDtypeStruct((2, SUB, block), F32),
            jax.ShapeDtypeStruct((2, SUB, LANES), F32),
        ],
        in_specs=[hbm, hbm, hbm],
        out_specs=[vmem] * 8,
        scratch_shapes=[
            pltpu.SMEM(wavenumber.shape, jnp.int32),
            pltpu.VMEM(spectral.shape, BF16),
            pltpu.SemaphoreType.DMA((2 * groups + 2,)),
        ],
        compiler_params=params,
        name="forward",
    )(*(pltpu.with_memory_space_constraint(x, pltpu.HBM) for x in (wavenumber, spectral, legendre)))
    got = lax.all_to_all(sent, ("lev", "wave"), 0, 0, tiled=True)
    rows = 2 * levels * SUB * SUB
    tend = pl.pallas_call(
        functools.partial(grid_kernel, groups, waves, levels, step),
        out_shape=parcel,
        in_specs=[vmem] * 6,
        out_specs=vmem,
        scratch_shapes=[
            pltpu.VMEM((groups, rows, LANES), BF16),
            pltpu.VMEM((rows, step), F32),
            pltpu.VMEM((rows, step), F32),
            pltpu.VMEM((rows, step), BF16),
            pltpu.VMEM((rows, step), BF16),
            pltpu.VMEM((groups, rows, LANES), F32),
            pltpu.VMEM((levels // 2, LANES, LANES), F32),
        ],
        compiler_params=params,
        name="grid",
    )(*tables, got)
    back = lax.all_to_all(tend, ("lev", "wave"), 0, 0, tiled=True)
    out = pl.pallas_call(
        functools.partial(backward_kernel, groups),
        out_shape=jax.ShapeDtypeStruct(spectral.shape, BF16),
        in_specs=[vmem, vmem, vmem],
        out_specs=vmem,
        compiler_params=params,
        name="backward",
    )(kept, leg, back)
    return jnp.transpose(out, (0, 1, 3, 2, 4))


def body(spectral, legendre, wavenumber):
    waves, levels = lax.axis_size("wave"), lax.axis_size("lev")
    lats = legendre.shape[1]
    group_lats = waves * levels * SUB
    groups = lats // (2 * group_lats)
    fits = (
        2 * groups * group_lats == lats
        and wavenumber.shape[0] == waves
        and spectral.shape[1] == 1
        and 2 * waves * SUB == LANES
        and levels % 2 == 0
        and 2 * groups * SUB <= LANES
        and group_lats % LANES == 0
    )
    if fits:
        return fast_body(groups, waves, levels, 2 * LANES, spectral, legendre, wavenumber)
    return general_body(spectral, legendre, wavenumber)


def circle_tables(latitude, band_index, wavenumber, lat_total, band_total, band_cap, wave_total):
    circle_length = 20 + 4 * jnp.minimum(latitude, lat_total - 1 - latitude)
    band_width = (circle_length + band_total - 1) // band_total
    offsets = jnp.arange(band_cap, dtype=jnp.int32)
    longitude_index = band_index[None, :, None] * band_width[:, None, None] + offsets[None, None, :]
    inside = (offsets[None, None, :] < band_width[:, None, None]) & (
        longitude_index < circle_length[:, None, None]
    )
    rows = latitude.shape[0]
    longitude_index = longitude_index.reshape(rows, -1)
    inside = inside.reshape(rows, -1)
    phase_index = (
        wavenumber[None, None, :] * longitude_index[:, :, None] % circle_length[:, None, None]
    )
    length_float = circle_length.astype(jnp.float32)
    angles = 2.0 * math.pi * phase_index.astype(jnp.float32) / length_float[:, None, None]
    shown = inside[:, :, None].astype(jnp.float32)
    trig_basis = jnp.stack([jnp.cos(angles) * shown, -jnp.sin(angles) * shown], axis=2)
    colatitude = (latitude.astype(jnp.float32) + 0.5) * (math.pi / lat_total)
    circle_weight = jnp.sin(colatitude) / jnp.sqrt(length_float)
    synth_table = (trig_basis / math.sqrt(wave_total)).astype(jnp.bfloat16)
    analysis_table = (trig_basis * circle_weight[:, None, None, None]).astype(jnp.bfloat16)
    return (synth_table, analysis_table, 2.0 * jnp.cos(colatitude))


def tendencies(grid_values, planetary):
    vorticity = grid_values[0]
    divergence = grid_values[1]
    absolute_vort = vorticity + planetary[None, :, None]
    column_div = jnp.sum(divergence, axis=0) / math.sqrt(divergence.shape[0])
    return jnp.stack(
        [-absolute_vort * divergence, absolute_vort * vorticity - divergence * column_div[None]]
    ).astype(jnp.bfloat16)


def general_body(spectral, legendre, wavenumber):
    wave_count = lax.axis_size("wave")
    lev_count = lax.axis_size("lev")
    wave_index = lax.axis_index("wave")
    lev_index = lax.axis_index("lev")
    lat_total = legendre.shape[1]
    degree_count = legendre.shape[2]
    set_span = lat_total // wave_count
    wave_total = wavenumber.shape[0]
    own_wave = lax.dynamic_slice_in_dim(wavenumber, wave_index, 1, 0)
    kept_degrees = (
        jnp.arange(degree_count, dtype=jnp.int32)[None, :] <= (degree_count - 1 - own_wave)[:, None]
    )
    masked_spec = jnp.where(kept_degrees, spectral, jnp.zeros_like(spectral))
    fourier = jnp.einsum(
        "flrsn,sjn->flrsj", masked_spec, legendre, preferred_element_type=jnp.float32
    ).astype(jnp.bfloat16)
    circle_max = 20 + 4 * (lat_total // 2 - 1)
    band_cap = (circle_max + lev_count - 1) // lev_count
    latitude = wave_index * set_span + jnp.arange(set_span, dtype=jnp.int32)
    band_index = jnp.reshape(lev_index, (1,))
    synth_table, analysis_table, planetary = circle_tables(
        latitude, band_index, wavenumber, lat_total, lev_count, band_cap, wave_total
    )
    set_fourier = lax.all_to_all(fourier, "wave", split_axis=4, concat_axis=3, tiled=True)
    grid_values = jnp.einsum(
        "flrsq,qprs->flqp",
        lax.all_gather(set_fourier, "lev", axis=1, tiled=True),
        synth_table,
        preferred_element_type=jnp.float32,
    )
    tendency = tendencies(grid_values, planetary)
    summed = lax.psum_scatter(
        jnp.einsum(
            "flqp,qprs->lfrsq", tendency, analysis_table, preferred_element_type=jnp.float32
        ),
        "lev",
        scatter_dimension=0,
        tiled=True,
    )
    returned = lax.all_to_all(
        summed.astype(jnp.bfloat16), "wave", split_axis=3, concat_axis=4, tiled=True
    )
    analysed = jnp.einsum(
        "lfrsj,sjn->flrsn", returned, legendre, preferred_element_type=jnp.float32
    )
    return jnp.where(kept_degrees, analysed, jnp.zeros_like(analysed)).astype(jnp.bfloat16)


def solution(mesh):
    in_specs = (P(None, "lev", None, "wave", None), P("wave", None, None), P())
    out_specs = P(None, "lev", None, "wave", None)
    return jax.shard_map(body, mesh=mesh, in_specs=in_specs, out_specs=out_specs, check_vma=False)
```

```python
import functools
import math

import jax
import jax.numpy as jnp
from jax import lax
from jax.experimental import pallas as pl
from jax.experimental.pallas import tpu as pltpu
from jax.sharding import PartitionSpec as P

SUB = 8
LANES = 128
QUARTERS = 4
FIRST = 5
NT = (((1,), (1,)), ((), ()))
NN = (((1,), (0,)), ((), ()))
F32 = jnp.float32
BF16 = jnp.bfloat16


def dot(a, b, dims):
    return lax.dot_general(a, b, dims, preferred_element_type=F32)


def iota(shape, dim):
    return lax.broadcasted_iota(jnp.int32, shape, dim)


def one_hot(mask):
    return jnp.where(mask, 1.0, 0.0).astype(BF16)


def cos_sin_turns(turns):
    quadrant = jnp.floor(turns * 4.0 + 0.5)
    u = (turns - quadrant * 0.25) * (2.0 * math.pi)
    u2 = u * u
    sine = u * (1.0 + u2 * (-1 / 6 + u2 * (1 / 120 + u2 * (-1 / 5040 + u2 * (1 / 362880)))))
    cosine = 1.0 + u2 * (-0.5 + u2 * (1 / 24 + u2 * (-1 / 720 + u2 * (1 / 40320))))
    quadrant = quadrant.astype(jnp.int32) & 3
    odd = (quadrant & 1) == 1
    c = jnp.where(odd, sine, cosine)
    s = jnp.where(odd, cosine, sine)
    c = jnp.where((quadrant == 1) | (quadrant == 2), -c, c)
    s = jnp.where(quadrant >= 2, -s, s)
    return c, s


def cos_sin_phase(wavenumber, point, circle):
    inverse = 1.0 / circle
    product = wavenumber * point
    whole = jnp.floor(product * inverse + 0.5)
    return cos_sin_turns((product - whole * circle) * inverse)


def quarter_turns(wavenumber, band):
    k = (wavenumber * band) & 3
    c = jnp.where(k == 0, 1.0, jnp.where(k == 2, -1.0, 0.0))
    s = jnp.where(k == 1, 1.0, jnp.where(k == 3, -1.0, 0.0))
    return c, s


def plain_part(group, south):
    return (group % 2 == 0) != south


def block_place(block, groups):
    south = block >= groups
    return (2 * groups - 1 - block if south else block), south


def reverse_matrix(n):
    return one_hot(iota((n, n), 0) + iota((n, n), 1) == n - 1)


def forward_kernel(
    groups, waves, levels, lats, wn_hbm, spec_hbm, leg_hbm,
    out_ref, kept_ref, leg, synth, analysis, planet, turns, backs, wn, spec, sems,
):
    block = leg.shape[1]
    first = [
        pltpu.make_async_copy(wn_hbm, wn, sems.at[4 * groups]),
        pltpu.make_async_copy(spec_hbm, spec, sems.at[4 * groups + 1]),
    ]
    chunks = []
    for k in range(0, 2 * groups, 2):
        runs = [pieces_of(k + h, groups, block) for h in range(2)]
        if len(runs[0]) == len(runs[1]) == 1:
            source = leg_hbm.at[0, pl.ds(k * block, 2 * block)].reshape(2, block, leg.shape[2])
            places = [(source, leg.at[pl.ds(k, 2)])]
        else:
            places = [
                (
                    leg_hbm.at[0, pl.ds((k + h) * block + source, rows)],
                    leg.at[k + h, pl.ds(target, rows)],
                )
                for h in range(2)
                for source, target, rows in runs[h]
            ]
        chunks.append(
            [
                pltpu.make_async_copy(*place, sems.at[2 * k + n])
                for n, place in enumerate(places)
            ]
        )
    for copy in first + sum(chunks, []):
        copy.start()
    for copy in first:
        copy.wait()
    degrees = leg.shape[2]
    kept = iota((SUB, degrees), 1) <= degrees - 1 - wn[lax.axis_index("wave")]
    kept_ref[...] = jnp.where(kept, 1.0, 0.0)
    rows = [spec[f, 0, 0].astype(F32) for f in range(2)]
    rows = jnp.concatenate(rows + [jnp.zeros((SUB - 4, degrees), F32)], axis=0)
    rows = jnp.where(kept, rows, 0.0)
    rows = rows.astype(BF16)
    reverse = reverse_matrix(block)
    pieces = [[], []]
    device = this_device(waves)
    numbers = [wn[w] for w in range(waves)]
    counts = chunk_counts(groups, block, synth.shape[2])
    turn_tables(waves, numbers, turns, backs)
    analysis[sum(counts)] = jnp.zeros(analysis.shape[1:], BF16)
    for k in range(2 * groups):
        group, south = block_place(k, groups)
        if k % 2 == 0:
            g = groups - 1 - k // 2
            group_tables(
                g, sum(counts[:g]), counts[g], waves, block, lats, numbers, device,
                synth, analysis, planet,
            )
            for copy in chunks[k // 2]:
                copy.wait()
        pieces[0 if plain_part(group, south) else 1].append((group, dot(rows, leg[k], NT)))
    pieces = [[v for _, v in sorted(p, key=lambda x: x[0])] for p in pieces]
    blank = jnp.zeros((SUB, block), F32)
    n = LANES // SUB
    plain = jnp.concatenate(pieces[0] + [blank] * (n - groups), axis=0)
    turned = jnp.concatenate([blank] * groups + pieces[1] + [blank] * (n - 2 * groups), axis=0)
    placed = jnp.transpose(plain) + dot(reverse, turned.astype(BF16), NT)
    out_ref[...] = placed.astype(BF16).reshape(out_ref.shape)


def backward_kernel(groups, kept_ref, leg, got_ref, out_ref):
    block, degrees = leg.shape[1:]
    got = got_ref[...].reshape(block, LANES)
    shape = (groups * SUB, LANES)
    row, lane = iota(shape, 0), iota(shape, 1)
    group, field, part = row // SUB, (row % SUB) // 2, row % 2
    source = group * SUB + part * 4 + field * 2
    used = row % SUB < 4
    odd = group % 2
    plain = dot(one_hot(used & (lane == source + odd)), got, NT).astype(BF16)
    turned = dot(one_hot(used & (lane == source + 1 - odd)), got, NT).astype(BF16)
    turned = dot(turned, reverse_matrix(block), NN).astype(BF16)
    total = jnp.zeros((SUB, degrees), F32)
    order = sorted(range(2 * groups), key=lambda k: not plain_part(*block_place(k, groups)))
    for k in order:
        g, south = block_place(k, groups)
        rows = plain if plain_part(g, south) else turned
        total = total + dot(rows[g * SUB : (g + 1) * SUB], leg[k], NN)
    total = (total * kept_ref[...]).astype(BF16)
    for f in range(2):
        out_ref[f, 0, 0] = total[f * 2 : f * 2 + 2]


def chunk_counts(groups, block, step):
    return [-(-(FIRST + block * (g + 1) - 1) // step) for g in range(groups)]


def shift_of(group, block):
    return group // 2 * (block // 4) % block


def latitude(group, block, order):
    turned = (order + shift_of(group, block)) % block
    return group * block + (turned if group % 2 == 0 else block - 1 - turned)


def pieces_of(block_index, groups, block):
    group, south = block_place(block_index, groups)
    by = shift_of(group, block)
    by = (-by if plain_part(group, south) else by) % block
    if by == 0:
        return [(0, 0, block)]
    return [(0, by, block - by), (block - by, 0, by)]


def step_counts(groups, block, step, device, largest):
    counts = []
    for g in range(groups):
        ends = [latitude(g, block, device * SUB + q) for q in (0, SUB - 1)]
        counts.append((FIRST + largest(*ends) + step - 1) // step)
    return counts


def this_device(waves):
    return lax.axis_index("lev") * waves + lax.axis_index("wave")


def turn_tables(waves, numbers, turns, backs):
    half = waves * SUB

    def slot_number(lanes):
        value = jnp.zeros(lanes.shape, jnp.int32)
        for s in range(waves):
            value = jnp.where(lanes == s, numbers[s], value)
        return value

    shape = turns.shape[1:]
    turns[0], turns[1] = quarter_turns(
        slot_number((iota(shape, 1) // SUB) % waves), iota(shape, 0) // 2
    )
    shape = backs.shape[1:]
    lane = iota(shape, 1)
    back_c, back_s = quarter_turns(slot_number((lane // SUB) % waves), iota(shape, 0) // 2)
    backs[0], backs[1] = back_c, jnp.where(lane < half, back_s, -back_s)


def group_tables(g, slot, count, waves, block, lats, numbers, device, synth, analysis, planet):
    half = waves * SUB
    step = synth.shape[2]
    shape = (SUB, LANES)
    lat = latitude(g, block, device * SUB + iota(shape, 0)).astype(F32)
    quarter = lat + FIRST
    circle = QUARTERS * quarter
    polar_c, polar_s = cos_sin_turns((lat + 0.5) * (0.5 / lats))
    scale = 1.0 / math.sqrt(waves)
    weight = polar_s / jnp.sqrt(circle) * (1.0 / scale)
    sign = jnp.where(iota(shape, 0) % 2 == 0, 2.0, -2.0)
    for q in range(SUB):
        value = jnp.broadcast_to(polar_c[q : q + 1], shape) * sign
        for part in range(step // LANES):
            planet[g, q * SUB : (q + 1) * SUB, part * LANES : (part + 1) * LANES] = value

    point = iota(shape, 1)
    inside = quarter.astype(jnp.int32)
    for s in range(0, waves, 2):
        pair, turn = [], []
        for k in range(2):
            c, n = cos_sin_phase(numbers[s + k].astype(F32), point.astype(F32), circle)
            mid_c = jnp.broadcast_to(c[:, LANES // 2 : LANES // 2 + 1], shape)
            mid_s = jnp.broadcast_to(n[:, LANES // 2 : LANES // 2 + 1], shape)
            turn.append((mid_c * mid_c - mid_s * mid_s, 2.0 * mid_c * mid_s))
            pair.append((c * scale, n * -scale))
        for a in range(count * (step // LANES)):
            at = slot + a * LANES // step
            lanes = pl.ds(a * LANES % step, LANES)
            for part in range(2):
                rows = pl.ds(part * half + s * SUB, 2 * SUB)
                basis = [v[part] for v in pair]
                synth[at, rows, lanes] = jnp.concatenate(basis, axis=0).astype(BF16)
                basis = [v * weight for v in basis]
                if (a + 1) * LANES > FIRST + g * block:
                    basis = [jnp.where(point + a * LANES < inside, v, 0.0) for v in basis]
                analysis[at, rows, lanes] = jnp.concatenate(basis, axis=0).astype(BF16)
            pair = [
                (c * tc + n * ts, n * tc - c * ts) for (c, n), (tc, ts) in zip(pair, turn)
            ]


def grid_kernel(
    groups, waves, levels, step, synth, analysis, planet, turns, backs, got_ref, out_ref,
    coef, grid_a, grid_b, tend_a, tend_b, total, kept,
):
    block = waves * levels * SUB
    half = waves * SUB
    device = this_device(waves)
    row, lane = iota((SUB, LANES), 0), iota((SUB, LANES), 1)
    first = lane < half
    which = lane % SUB

    got = got_ref[...].reshape(block, LANES)
    shape = (groups * 4 * SUB, LANES)
    row_of, lane_of = iota(shape, 0), iota(shape, 1)
    group, pair, south = row_of // (4 * SUB), (row_of // SUB) % 4, row_of % 2
    source = (group + south) % 2 * (groups * SUB) + group * SUB + pair
    fourier = dot(one_hot(lane_of == source), got, NT)
    turn_c, turn_s = turns[0], turns[1]

    for g in range(groups):
        for f in range(2):
            base = (g * 4 + f * 2) * SUB
            real, imag = fourier[base : base + SUB], fourier[base + SUB : base + 2 * SUB]
            turned_r = real * turn_c - imag * turn_s
            turned_i = real * turn_s + imag * turn_c
            for l in range(levels):
                cut = slice((l // 2) * LANES, (l // 2 + 1) * LANES)
                a, b = turned_r[:, cut], turned_i[:, cut]
                if l % 2 == 0:
                    b = pltpu.roll(b, half, 1)
                else:
                    a = pltpu.roll(a, half, 1)
                both = jnp.where(first, a, b)
                for q in range(0, SUB, 2):
                    place = ((f * levels + l) * SUB + q) * SUB
                    two = jnp.concatenate(
                        [jnp.where(which == q + k, both, 0.0) for k in range(2)], axis=0
                    )
                    coef[g, place : place + 2 * SUB, :] = two.astype(BF16)

    most = chunk_counts(groups, block, step)
    ends, skips = [], []
    end = 0
    for g, count in enumerate(step_counts(groups, block, step, device, jnp.maximum)):
        end = end + count
        ends.append(end)
        skips.append(most[g] - count)
    devices = waves * levels
    steps = max(sum(step_counts(groups, block, step, d, max)) for d in range(devices))

    def place_of(i):
        group, slot = jnp.int32(0), i
        for g in range(groups - 1):
            past = i >= ends[g]
            group = group + jnp.where(past, 1, 0)
            slot = slot + jnp.where(past, skips[g], 0)
        return group, slot

    rows = levels * SUB * SUB

    def synthesis(i, values):
        group, slot = place_of(jnp.minimum(i, end - 1))
        values[...] = dot(coef[group], synth[slot], NN)

    def tendencies_of(i, values, tend):
        group, _ = place_of(jnp.minimum(i, end - 1))
        for r in range(0, SUB * SUB, 2 * SUB):
            at = [pl.ds(l * SUB * SUB + r, 2 * SUB) for l in range(levels)]
            below = [pl.ds(rows + l * SUB * SUB + r, 2 * SUB) for l in range(levels)]
            div = [values[b, :] for b in below]
            column = div[0]
            for l in range(1, levels):
                column = column + div[l]
            column = column * (1.0 / math.sqrt(levels))
            turning = planet[group, pl.ds(r, 2 * SUB), :]
            for l in range(levels):
                vort = values[at[l], :]
                absolute = vort + turning
                tend[at[l], :] = (-absolute * div[l]).astype(BF16)
                tend[below[l], :] = (absolute * vort - div[l] * column).astype(BF16)

    def analysis_of(i, tend):
        group, slot = place_of(jnp.minimum(i, end - 1))
        slot = jnp.where(i < end, slot, sum(most))
        fresh = i == 0
        for begin in ends[:-1]:
            fresh = fresh | (i == begin)
        total[group] = jnp.where(fresh, 0.0, total[group]) + dot(tend[...], analysis[slot], NT)

    grids, tends = (grid_a, grid_b), (tend_a, tend_b)

    @pl.loop(0, jnp.minimum(end, 1))
    def _(_):
        for i in range(steps + 2):
            if i < steps:
                synthesis(i, grids[i % 2])
            if 1 <= i <= steps:
                tendencies_of(i - 1, grids[(i - 1) % 2], tends[(i - 1) % 2])
            if i >= 2:
                analysis_of(i - 2, tends[i % 2])

    back_c, back_s = backs[0], backs[1]
    kept[...] = jnp.zeros_like(kept)
    for g in range(groups):
        sums = []
        for f in range(2):
            for l in range(levels):
                base = (f * levels + l) * SUB * SUB
                value = jnp.zeros((SUB, LANES), F32)
                for q in range(SUB):
                    part = total[g, base + q * SUB : base + (q + 1) * SUB, :]
                    value = jnp.where(which == q, part, value)
                value = value * back_c + pltpu.roll(value, half, 1) * back_s
                value = value + pltpu.roll(value, 4, 0)
                sums.append(value + pltpu.roll(value, 2, 0))
        lined = []
        for l in range(levels):
            both = jnp.where(row % 4 < 2, sums[l], sums[levels + l])
            lined.append(jnp.where(row < 4, both, pltpu.roll(both, half, 1)))
        for p in range(levels // 2):
            kept[p, g * SUB : (g + 1) * SUB, :] = jnp.where(
                first, lined[2 * p], pltpu.roll(lined[2 * p + 1], half, 1)
            )
    for p in range(levels // 2):
        moved = jnp.transpose(kept[p]).astype(BF16)
        out_ref[p * 2 * waves : (p + 1) * 2 * waves] = moved.reshape(2 * waves, SUB, LANES)


def fast_body(groups, waves, levels, step, spectral, legendre, wavenumber):
    lats, degrees = legendre.shape[1:]
    devices = waves * levels
    block = devices * SUB
    vmem = pl.BlockSpec(memory_space=pltpu.VMEM)
    hbm = pl.BlockSpec(memory_space=pltpu.HBM)
    params = pltpu.CompilerParams(vmem_limit_bytes=24 * 1024 * 1024)
    parcel = jax.ShapeDtypeStruct((devices, SUB, LANES), BF16)
    spectral = jnp.transpose(spectral, (0, 1, 3, 2, 4))
    slots = sum(chunk_counts(groups, block, step))
    sent, kept, leg, *tables = pl.pallas_call(
        functools.partial(forward_kernel, groups, waves, levels, lats),
        out_shape=[
            parcel,
            jax.ShapeDtypeStruct((SUB, degrees), F32),
            jax.ShapeDtypeStruct((2 * groups, block, degrees), BF16),
            jax.ShapeDtypeStruct((slots, LANES, step), BF16),
            jax.ShapeDtypeStruct((slots + 1, LANES, step), BF16),
            jax.ShapeDtypeStruct((groups, SUB * SUB, step), F32),
            jax.ShapeDtypeStruct((2, SUB, block), F32),
            jax.ShapeDtypeStruct((2, SUB, LANES), F32),
        ],
        in_specs=[hbm, hbm, hbm],
        out_specs=[vmem] * 8,
        scratch_shapes=[
            pltpu.SMEM(wavenumber.shape, jnp.int32),
            pltpu.VMEM(spectral.shape, BF16),
            pltpu.SemaphoreType.DMA((4 * groups + 2,)),
        ],
        compiler_params=params,
        name="forward",
    )(*(pltpu.with_memory_space_constraint(x, pltpu.HBM) for x in (wavenumber, spectral, legendre)))
    got = lax.all_to_all(sent, ("lev", "wave"), 0, 0, tiled=True)
    rows = 2 * levels * SUB * SUB
    tend = pl.pallas_call(
        functools.partial(grid_kernel, groups, waves, levels, step),
        out_shape=parcel,
        in_specs=[vmem] * 6,
        out_specs=vmem,
        scratch_shapes=[
            pltpu.VMEM((groups, rows, LANES), BF16),
            pltpu.VMEM((rows, step), F32),
            pltpu.VMEM((rows, step), F32),
            pltpu.VMEM((rows, step), BF16),
            pltpu.VMEM((rows, step), BF16),
            pltpu.VMEM((groups, rows, LANES), F32),
            pltpu.VMEM((levels // 2, LANES, LANES), F32),
        ],
        compiler_params=params,
        name="grid",
    )(*tables, got)
    back = lax.all_to_all(tend, ("lev", "wave"), 0, 0, tiled=True)
    out = pl.pallas_call(
        functools.partial(backward_kernel, groups),
        out_shape=jax.ShapeDtypeStruct(spectral.shape, BF16),
        in_specs=[vmem, vmem, vmem],
        out_specs=vmem,
        compiler_params=params,
        name="backward",
    )(kept, leg, back)
    return jnp.transpose(out, (0, 1, 3, 2, 4))


def body(spectral, legendre, wavenumber):
    waves, levels = lax.axis_size("wave"), lax.axis_size("lev")
    lats = legendre.shape[1]
    group_lats = waves * levels * SUB
    groups = lats // (2 * group_lats)
    fits = (
        2 * groups * group_lats == lats
        and wavenumber.shape[0] == waves
        and spectral.shape[1] == 1
        and 2 * waves * SUB == LANES
        and levels % 2 == 0
        and 2 * groups * SUB <= LANES
        and group_lats % LANES == 0
    )
    if fits:
        return fast_body(groups, waves, levels, 2 * LANES, spectral, legendre, wavenumber)
    return general_body(spectral, legendre, wavenumber)


def circle_tables(latitude, band_index, wavenumber, lat_total, band_total, band_cap, wave_total):
    circle_length = 20 + 4 * jnp.minimum(latitude, lat_total - 1 - latitude)
    band_width = (circle_length + band_total - 1) // band_total
    offsets = jnp.arange(band_cap, dtype=jnp.int32)
    longitude_index = band_index[None, :, None] * band_width[:, None, None] + offsets[None, None, :]
    inside = (offsets[None, None, :] < band_width[:, None, None]) & (
        longitude_index < circle_length[:, None, None]
    )
    rows = latitude.shape[0]
    longitude_index = longitude_index.reshape(rows, -1)
    inside = inside.reshape(rows, -1)
    phase_index = (
        wavenumber[None, None, :] * longitude_index[:, :, None] % circle_length[:, None, None]
    )
    length_float = circle_length.astype(jnp.float32)
    angles = 2.0 * math.pi * phase_index.astype(jnp.float32) / length_float[:, None, None]
    shown = inside[:, :, None].astype(jnp.float32)
    trig_basis = jnp.stack([jnp.cos(angles) * shown, -jnp.sin(angles) * shown], axis=2)
    colatitude = (latitude.astype(jnp.float32) + 0.5) * (math.pi / lat_total)
    circle_weight = jnp.sin(colatitude) / jnp.sqrt(length_float)
    synth_table = (trig_basis / math.sqrt(wave_total)).astype(jnp.bfloat16)
    analysis_table = (trig_basis * circle_weight[:, None, None, None]).astype(jnp.bfloat16)
    return (synth_table, analysis_table, 2.0 * jnp.cos(colatitude))


def tendencies(grid_values, planetary):
    vorticity = grid_values[0]
    divergence = grid_values[1]
    absolute_vort = vorticity + planetary[None, :, None]
    column_div = jnp.sum(divergence, axis=0) / math.sqrt(divergence.shape[0])
    return jnp.stack(
        [-absolute_vort * divergence, absolute_vort * vorticity - divergence * column_div[None]]
    ).astype(jnp.bfloat16)


def general_body(spectral, legendre, wavenumber):
    wave_count = lax.axis_size("wave")
    lev_count = lax.axis_size("lev")
    wave_index = lax.axis_index("wave")
    lev_index = lax.axis_index("lev")
    lat_total = legendre.shape[1]
    degree_count = legendre.shape[2]
    set_span = lat_total // wave_count
    wave_total = wavenumber.shape[0]
    own_wave = lax.dynamic_slice_in_dim(wavenumber, wave_index, 1, 0)
    kept_degrees = (
        jnp.arange(degree_count, dtype=jnp.int32)[None, :] <= (degree_count - 1 - own_wave)[:, None]
    )
    masked_spec = jnp.where(kept_degrees, spectral, jnp.zeros_like(spectral))
    fourier = jnp.einsum(
        "flrsn,sjn->flrsj", masked_spec, legendre, preferred_element_type=jnp.float32
    ).astype(jnp.bfloat16)
    circle_max = 20 + 4 * (lat_total // 2 - 1)
    band_cap = (circle_max + lev_count - 1) // lev_count
    latitude = wave_index * set_span + jnp.arange(set_span, dtype=jnp.int32)
    band_index = jnp.reshape(lev_index, (1,))
    synth_table, analysis_table, planetary = circle_tables(
        latitude, band_index, wavenumber, lat_total, lev_count, band_cap, wave_total
    )
    set_fourier = lax.all_to_all(fourier, "wave", split_axis=4, concat_axis=3, tiled=True)
    grid_values = jnp.einsum(
        "flrsq,qprs->flqp",
        lax.all_gather(set_fourier, "lev", axis=1, tiled=True),
        synth_table,
        preferred_element_type=jnp.float32,
    )
    tendency = tendencies(grid_values, planetary)
    summed = lax.psum_scatter(
        jnp.einsum(
            "flqp,qprs->lfrsq", tendency, analysis_table, preferred_element_type=jnp.float32
        ),
        "lev",
        scatter_dimension=0,
        tiled=True,
    )
    returned = lax.all_to_all(
        summed.astype(jnp.bfloat16), "wave", split_axis=3, concat_axis=4, tiled=True
    )
    analysed = jnp.einsum(
        "lfrsj,sjn->flrsn", returned, legendre, preferred_element_type=jnp.float32
    )
    return jnp.where(kept_degrees, analysed, jnp.zeros_like(analysed)).astype(jnp.bfloat16)


def solution(mesh):
    in_specs = (P(None, "lev", None, "wave", None), P("wave", None, None), P())
    out_specs = P(None, "lev", None, "wave", None)
    return jax.shard_map(body, mesh=mesh, in_specs=in_specs, out_specs=out_specs, check_vma=False)
```

```python
import functools
import math

import jax
import jax.numpy as jnp
from jax import lax
from jax.experimental import pallas as pl
from jax.experimental.pallas import tpu as pltpu
from jax.sharding import PartitionSpec as P

SUB = 8
LANES = 128
QUARTERS = 4
FIRST = 5
NT = (((1,), (1,)), ((), ()))
NN = (((1,), (0,)), ((), ()))
F32 = jnp.float32
BF16 = jnp.bfloat16


def dot(a, b, dims):
    return lax.dot_general(a, b, dims, preferred_element_type=F32)


def iota(shape, dim):
    return lax.broadcasted_iota(jnp.int32, shape, dim)


def one_hot(mask):
    return jnp.where(mask, 1.0, 0.0).astype(BF16)


def cos_sin_turns(turns):
    quadrant = jnp.floor(turns * 4.0 + 0.5)
    u = (turns - quadrant * 0.25) * (2.0 * math.pi)
    u2 = u * u
    sine = u * (1.0 + u2 * (-1 / 6 + u2 * (1 / 120 + u2 * (-1 / 5040 + u2 * (1 / 362880)))))
    cosine = 1.0 + u2 * (-0.5 + u2 * (1 / 24 + u2 * (-1 / 720 + u2 * (1 / 40320))))
    quadrant = quadrant.astype(jnp.int32) & 3
    odd = (quadrant & 1) == 1
    c = jnp.where(odd, sine, cosine)
    s = jnp.where(odd, cosine, sine)
    c = jnp.where((quadrant == 1) | (quadrant == 2), -c, c)
    s = jnp.where(quadrant >= 2, -s, s)
    return c, s


def cos_sin_phase(wavenumber, point, circle):
    inverse = 1.0 / circle
    product = wavenumber * point
    whole = jnp.floor(product * inverse + 0.5)
    return cos_sin_turns((product - whole * circle) * inverse)


def quarter_turns(wavenumber, band):
    k = (wavenumber * band) & 3
    c = jnp.where(k == 0, 1.0, jnp.where(k == 2, -1.0, 0.0))
    s = jnp.where(k == 1, 1.0, jnp.where(k == 3, -1.0, 0.0))
    return c, s


def plain_part(group, south):
    return (group % 2 == 0) != south


def block_place(block, groups):
    south = block >= groups
    return (2 * groups - 1 - block if south else block), south


def reverse_matrix(n):
    return one_hot(iota((n, n), 0) + iota((n, n), 1) == n - 1)


def forward_kernel(
    groups, waves, levels, lats, wn_hbm, spec_hbm, leg_hbm,
    out_ref, kept_ref, leg, synth, analysis, planet, turns, backs, wn, spec, sems,
):
    block = leg.shape[1]
    first = [
        pltpu.make_async_copy(wn_hbm, wn, sems.at[4 * groups]),
        pltpu.make_async_copy(spec_hbm, spec, sems.at[4 * groups + 1]),
    ]
    chunks = []
    for k in range(0, 2 * groups, 2):
        runs = [pieces_of(k + h, groups, block) for h in range(2)]
        if len(runs[0]) == len(runs[1]) == 1:
            source = leg_hbm.at[0, pl.ds(k * block, 2 * block)].reshape(2, block, leg.shape[2])
            places = [(source, leg.at[pl.ds(k, 2)])]
        else:
            places = [
                (
                    leg_hbm.at[0, pl.ds((k + h) * block + source, rows)],
                    leg.at[k + h, pl.ds(target, rows)],
                )
                for h in range(2)
                for source, target, rows in runs[h]
            ]
        chunks.append(
            [
                pltpu.make_async_copy(*place, sems.at[2 * k + n])
                for n, place in enumerate(places)
            ]
        )
    for copy in first + sum(chunks, []):
        copy.start()
    for copy in first:
        copy.wait()
    degrees = leg.shape[2]
    kept = iota((SUB, degrees), 1) <= degrees - 1 - wn[lax.axis_index("wave")]
    kept_ref[...] = jnp.where(kept, 1.0, 0.0)
    rows = [spec[f, 0, 0].astype(F32) for f in range(2)]
    rows = jnp.concatenate(rows + [jnp.zeros((SUB - 4, degrees), F32)], axis=0)
    rows = jnp.where(kept, rows, 0.0)
    rows = rows.astype(BF16)
    reverse = reverse_matrix(block)
    pieces = [[], []]
    device = this_device(waves)
    numbers = [wn[w] for w in range(waves)]
    counts = chunk_counts(groups, block, synth.shape[2])
    turn_tables(waves, numbers, turns, backs)
    analysis[sum(counts)] = jnp.zeros(analysis.shape[1:], BF16)
    for k in range(2 * groups):
        group, south = block_place(k, groups)
        if k % 2 == 0:
            g = groups - 1 - k // 2
            group_tables(
                g, sum(counts[:g]), counts[g], waves, block, lats, numbers, device,
                synth, analysis, planet,
            )
            for copy in chunks[k // 2]:
                copy.wait()
        pieces[0 if plain_part(group, south) else 1].append((group, dot(rows, leg[k], NT)))
    pieces = [[v for _, v in sorted(p, key=lambda x: x[0])] for p in pieces]
    blank = jnp.zeros((SUB, block), F32)
    n = LANES // SUB
    plain = jnp.concatenate(pieces[0] + [blank] * (n - groups), axis=0)
    turned = jnp.concatenate([blank] * groups + pieces[1] + [blank] * (n - 2 * groups), axis=0)
    placed = jnp.transpose(plain) + dot(reverse, turned.astype(BF16), NT)
    out_ref[...] = placed.astype(BF16).reshape(out_ref.shape)


def backward_kernel(groups, kept_ref, leg, got_ref, out_ref):
    block, degrees = leg.shape[1:]
    got = jnp.transpose(got_ref[...].reshape(block, LANES).astype(F32))[: groups * SUB]
    plain = got.astype(BF16)
    turned = dot(plain, reverse_matrix(block), NN).astype(BF16)
    sums = [jnp.zeros((SUB, degrees), F32)] * 2
    order = sorted(range(2 * groups), key=lambda k: not plain_part(*block_place(k, groups)))
    for k in order:
        g, south = block_place(k, groups)
        rows = plain if plain_part(g, south) else turned
        sums[south] = sums[south] + dot(rows[g * SUB : (g + 1) * SUB], leg[k], NN)
    for f in range(2):
        for r in range(2):
            row = r * 4 + f * 2
            total = sums[0][row : row + 1] + sums[1][row + 1 : row + 2]
            out_ref[f, 0, 0, r : r + 1] = (total * kept_ref[:1]).astype(BF16)


def chunk_counts(groups, block, step):
    return [-(-(FIRST + block * (g + 1) - 1) // step) for g in range(groups)]


def shift_of(group, block):
    return group // 2 * (block // 4) % block


def latitude(group, block, order):
    turned = (order + shift_of(group, block)) % block
    return group * block + (turned if group % 2 == 0 else block - 1 - turned)


def pieces_of(block_index, groups, block):
    group, south = block_place(block_index, groups)
    by = shift_of(group, block)
    by = (-by if plain_part(group, south) else by) % block
    if by == 0:
        return [(0, 0, block)]
    return [(0, by, block - by), (block - by, 0, by)]


def step_counts(groups, block, step, device, largest):
    counts = []
    for g in range(groups):
        ends = [latitude(g, block, device * SUB + q) for q in (0, SUB - 1)]
        counts.append((FIRST + largest(*ends) + step - 1) // step)
    return counts


def this_device(waves):
    return lax.axis_index("lev") * waves + lax.axis_index("wave")


def turn_tables(waves, numbers, turns, backs):
    half = waves * SUB

    def slot_number(lanes):
        value = jnp.zeros(lanes.shape, jnp.int32)
        for s in range(waves):
            value = jnp.where(lanes == s, numbers[s], value)
        return value

    shape = turns.shape[1:]
    turns[0], turns[1] = quarter_turns(
        slot_number((iota(shape, 1) // SUB) % waves), iota(shape, 0) // 2
    )
    shape = backs.shape[1:]
    lane = iota(shape, 1)
    back_c, back_s = quarter_turns(slot_number((lane // SUB) % waves), iota(shape, 0) // 2)
    backs[0], backs[1] = back_c, jnp.where(lane < half, back_s, -back_s)


def group_tables(g, slot, count, waves, block, lats, numbers, device, synth, analysis, planet):
    half = waves * SUB
    step = synth.shape[2]
    shape = (SUB, LANES)
    lat = latitude(g, block, device * SUB + iota(shape, 0)).astype(F32)
    quarter = lat + FIRST
    circle = QUARTERS * quarter
    polar_c, polar_s = cos_sin_turns((lat + 0.5) * (0.5 / lats))
    scale = 1.0 / math.sqrt(waves)
    weight = polar_s / jnp.sqrt(circle) * (1.0 / scale)
    sign = jnp.where(iota(shape, 0) % 2 == 0, 2.0, -2.0)
    for q in range(SUB):
        value = jnp.broadcast_to(polar_c[q : q + 1], shape) * sign
        for part in range(step // LANES):
            planet[g, q * SUB : (q + 1) * SUB, part * LANES : (part + 1) * LANES] = value

    point = iota(shape, 1)
    inside = quarter.astype(jnp.int32)
    for s in range(0, waves, 2):
        pair, turn = [], []
        for k in range(2):
            c, n = cos_sin_phase(numbers[s + k].astype(F32), point.astype(F32), circle)
            mid_c = jnp.broadcast_to(c[:, LANES // 2 : LANES // 2 + 1], shape)
            mid_s = jnp.broadcast_to(n[:, LANES // 2 : LANES // 2 + 1], shape)
            turn.append((mid_c * mid_c - mid_s * mid_s, 2.0 * mid_c * mid_s))
            pair.append((c * scale, n * -scale))
        for a in range(count * (step // LANES)):
            at = slot + a * LANES // step
            lanes = pl.ds(a * LANES % step, LANES)
            for part in range(2):
                rows = pl.ds(part * half + s * SUB, 2 * SUB)
                basis = [v[part] for v in pair]
                synth[at, rows, lanes] = jnp.concatenate(basis, axis=0).astype(BF16)
                basis = [v * weight for v in basis]
                if (a + 1) * LANES > FIRST + g * block:
                    basis = [jnp.where(point + a * LANES < inside, v, 0.0) for v in basis]
                analysis[at, rows, lanes] = jnp.concatenate(basis, axis=0).astype(BF16)
            pair = [
                (c * tc + n * ts, n * tc - c * ts) for (c, n), (tc, ts) in zip(pair, turn)
            ]


def grid_kernel(
    groups, waves, levels, step, synth, analysis, planet, turns, backs, got_ref, out_ref,
    coef, grid_a, grid_b, tend_a, tend_b, total, kept,
):
    block = waves * levels * SUB
    half = waves * SUB
    device = this_device(waves)
    row, lane = iota((SUB, LANES), 0), iota((SUB, LANES), 1)
    first = lane < half
    which = lane % SUB

    got = jnp.transpose(got_ref[...].reshape(block, LANES).astype(F32))
    turn_c, turn_s = turns[0], turns[1]
    north = iota((SUB, block), 0) % 2 == 0

    def spread(group, pair):
        rows = [p * groups * SUB + group * SUB + pair for p in (group % 2, 1 - group % 2)]
        here, there = (jnp.broadcast_to(got[r : r + 1], (SUB, block)) for r in rows)
        return jnp.where(north, here, there)


    for g in range(groups):
        for f in range(2):
            real, imag = spread(g, f * 2), spread(g, f * 2 + 1)
            turned_r = real * turn_c - imag * turn_s
            turned_i = real * turn_s + imag * turn_c
            for l in range(levels):
                cut = slice((l // 2) * LANES, (l // 2 + 1) * LANES)
                a, b = turned_r[:, cut], turned_i[:, cut]
                if l % 2 == 0:
                    b = pltpu.roll(b, half, 1)
                else:
                    a = pltpu.roll(a, half, 1)
                both = jnp.where(first, a, b)
                for q in range(0, SUB, 2):
                    place = ((f * levels + l) * SUB + q) * SUB
                    two = jnp.concatenate(
                        [jnp.where(which == q + k, both, 0.0) for k in range(2)], axis=0
                    )
                    coef[g, place : place + 2 * SUB, :] = two.astype(BF16)

    most = chunk_counts(groups, block, step)
    ends, skips = [], []
    end = 0
    for g, count in enumerate(step_counts(groups, block, step, device, jnp.maximum)):
        end = end + count
        ends.append(end)
        skips.append(most[g] - count)
    devices = waves * levels
    steps = max(sum(step_counts(groups, block, step, d, max)) for d in range(devices))

    def place_of(i):
        group, slot = jnp.int32(0), i
        for g in range(groups - 1):
            past = i >= ends[g]
            group = group + jnp.where(past, 1, 0)
            slot = slot + jnp.where(past, skips[g], 0)
        return group, slot

    rows = levels * SUB * SUB

    def synthesis(i, values):
        group, slot = place_of(jnp.minimum(i, end - 1))
        values[...] = dot(coef[group], synth[slot], NN)

    def tendencies_of(i, values, tend):
        group, _ = place_of(jnp.minimum(i, end - 1))
        for r in range(0, SUB * SUB, 2 * SUB):
            at = [pl.ds(l * SUB * SUB + r, 2 * SUB) for l in range(levels)]
            below = [pl.ds(rows + l * SUB * SUB + r, 2 * SUB) for l in range(levels)]
            div = [values[b, :] for b in below]
            column = div[0]
            for l in range(1, levels):
                column = column + div[l]
            column = column * (1.0 / math.sqrt(levels))
            turning = planet[group, pl.ds(r, 2 * SUB), :]
            for l in range(levels):
                vort = values[at[l], :]
                absolute = vort + turning
                tend[at[l], :] = (-absolute * div[l]).astype(BF16)
                tend[below[l], :] = (absolute * vort - div[l] * column).astype(BF16)

    def analysis_of(i, tend):
        group, slot = place_of(jnp.minimum(i, end - 1))
        slot = jnp.where(i < end, slot, sum(most))
        fresh = i == 0
        for begin in ends[:-1]:
            fresh = fresh | (i == begin)
        total[group] = jnp.where(fresh, 0.0, total[group]) + dot(tend[...], analysis[slot], NT)

    grids, tends = (grid_a, grid_b), (tend_a, tend_b)

    @pl.loop(0, jnp.minimum(end, 1))
    def _(_):
        for i in range(steps + 2):
            if i < steps:
                synthesis(i, grids[i % 2])
            if 1 <= i <= steps:
                tendencies_of(i - 1, grids[(i - 1) % 2], tends[(i - 1) % 2])
            if i >= 2:
                analysis_of(i - 2, tends[i % 2])

    back_c, back_s = backs[0], backs[1]
    kept[...] = jnp.zeros_like(kept)
    for g in range(groups):
        sums = []
        for f in range(2):
            for l in range(levels):
                base = (f * levels + l) * SUB * SUB
                value = jnp.zeros((SUB, LANES), F32)
                for q in range(SUB):
                    part = total[g, base + q * SUB : base + (q + 1) * SUB, :]
                    value = jnp.where(which == q, part, value)
                value = value * back_c + pltpu.roll(value, half, 1) * back_s
                value = value + pltpu.roll(value, 4, 0)
                sums.append(value + pltpu.roll(value, 2, 0))
        lined = []
        for l in range(levels):
            both = jnp.where(row % 4 < 2, sums[l], sums[levels + l])
            swapped = pltpu.roll(both, half, 1)
            lined.append(jnp.where((row < 4) == (l % 2 == 0), both, swapped))
        for p in range(levels // 2):
            kept[p, g * SUB : (g + 1) * SUB, :] = jnp.where(first, lined[2 * p], lined[2 * p + 1])
    for p in range(levels // 2):
        moved = jnp.transpose(kept[p]).astype(BF16)
        out_ref[p * 2 * waves : (p + 1) * 2 * waves] = moved.reshape(2 * waves, SUB, LANES)


def fast_body(groups, waves, levels, step, spectral, legendre, wavenumber):
    lats, degrees = legendre.shape[1:]
    devices = waves * levels
    block = devices * SUB
    vmem = pl.BlockSpec(memory_space=pltpu.VMEM)
    hbm = pl.BlockSpec(memory_space=pltpu.HBM)
    params = pltpu.CompilerParams(vmem_limit_bytes=24 * 1024 * 1024)
    parcel = jax.ShapeDtypeStruct((devices, SUB, LANES), BF16)
    spectral = jnp.transpose(spectral, (0, 1, 3, 2, 4))
    slots = sum(chunk_counts(groups, block, step))
    sent, kept, leg, *tables = pl.pallas_call(
        functools.partial(forward_kernel, groups, waves, levels, lats),
        out_shape=[
            parcel,
            jax.ShapeDtypeStruct((SUB, degrees), F32),
            jax.ShapeDtypeStruct((2 * groups, block, degrees), BF16),
            jax.ShapeDtypeStruct((slots, LANES, step), BF16),
            jax.ShapeDtypeStruct((slots + 1, LANES, step), BF16),
            jax.ShapeDtypeStruct((groups, SUB * SUB, step), F32),
            jax.ShapeDtypeStruct((2, SUB, block), F32),
            jax.ShapeDtypeStruct((2, SUB, LANES), F32),
        ],
        in_specs=[hbm, hbm, hbm],
        out_specs=[vmem] * 8,
        scratch_shapes=[
            pltpu.SMEM(wavenumber.shape, jnp.int32),
            pltpu.VMEM(spectral.shape, BF16),
            pltpu.SemaphoreType.DMA((4 * groups + 2,)),
        ],
        compiler_params=params,
        name="forward",
    )(*(pltpu.with_memory_space_constraint(x, pltpu.HBM) for x in (wavenumber, spectral, legendre)))
    got = lax.all_to_all(sent, ("lev", "wave"), 0, 0, tiled=True)
    rows = 2 * levels * SUB * SUB
    tend = pl.pallas_call(
        functools.partial(grid_kernel, groups, waves, levels, step),
        out_shape=parcel,
        in_specs=[vmem] * 6,
        out_specs=vmem,
        scratch_shapes=[
            pltpu.VMEM((groups, rows, LANES), BF16),
            pltpu.VMEM((rows, step), F32),
            pltpu.VMEM((rows, step), F32),
            pltpu.VMEM((rows, step), BF16),
            pltpu.VMEM((rows, step), BF16),
            pltpu.VMEM((groups, rows, LANES), F32),
            pltpu.VMEM((levels // 2, LANES, LANES), F32),
        ],
        compiler_params=params,
        name="grid",
    )(*tables, got)
    back = lax.all_to_all(tend, ("lev", "wave"), 0, 0, tiled=True)
    out = pl.pallas_call(
        functools.partial(backward_kernel, groups),
        out_shape=jax.ShapeDtypeStruct(spectral.shape, BF16),
        in_specs=[vmem, vmem, vmem],
        out_specs=vmem,
        compiler_params=params,
        name="backward",
    )(kept, leg, back)
    return jnp.transpose(out, (0, 1, 3, 2, 4))


def body(spectral, legendre, wavenumber):
    waves, levels = lax.axis_size("wave"), lax.axis_size("lev")
    lats = legendre.shape[1]
    group_lats = waves * levels * SUB
    groups = lats // (2 * group_lats)
    fits = (
        2 * groups * group_lats == lats
        and wavenumber.shape[0] == waves
        and spectral.shape[1] == 1
        and 2 * waves * SUB == LANES
        and levels % 2 == 0
        and 2 * groups * SUB <= LANES
        and group_lats % LANES == 0
    )
    if fits:
        return fast_body(groups, waves, levels, 2 * LANES, spectral, legendre, wavenumber)
    return general_body(spectral, legendre, wavenumber)


def circle_tables(latitude, band_index, wavenumber, lat_total, band_total, band_cap, wave_total):
    circle_length = 20 + 4 * jnp.minimum(latitude, lat_total - 1 - latitude)
    band_width = (circle_length + band_total - 1) // band_total
    offsets = jnp.arange(band_cap, dtype=jnp.int32)
    longitude_index = band_index[None, :, None] * band_width[:, None, None] + offsets[None, None, :]
    inside = (offsets[None, None, :] < band_width[:, None, None]) & (
        longitude_index < circle_length[:, None, None]
    )
    rows = latitude.shape[0]
    longitude_index = longitude_index.reshape(rows, -1)
    inside = inside.reshape(rows, -1)
    phase_index = (
        wavenumber[None, None, :] * longitude_index[:, :, None] % circle_length[:, None, None]
    )
    length_float = circle_length.astype(jnp.float32)
    angles = 2.0 * math.pi * phase_index.astype(jnp.float32) / length_float[:, None, None]
    shown = inside[:, :, None].astype(jnp.float32)
    trig_basis = jnp.stack([jnp.cos(angles) * shown, -jnp.sin(angles) * shown], axis=2)
    colatitude = (latitude.astype(jnp.float32) + 0.5) * (math.pi / lat_total)
    circle_weight = jnp.sin(colatitude) / jnp.sqrt(length_float)
    synth_table = (trig_basis / math.sqrt(wave_total)).astype(jnp.bfloat16)
    analysis_table = (trig_basis * circle_weight[:, None, None, None]).astype(jnp.bfloat16)
    return (synth_table, analysis_table, 2.0 * jnp.cos(colatitude))


def tendencies(grid_values, planetary):
    vorticity = grid_values[0]
    divergence = grid_values[1]
    absolute_vort = vorticity + planetary[None, :, None]
    column_div = jnp.sum(divergence, axis=0) / math.sqrt(divergence.shape[0])
    return jnp.stack(
        [-absolute_vort * divergence, absolute_vort * vorticity - divergence * column_div[None]]
    ).astype(jnp.bfloat16)


def general_body(spectral, legendre, wavenumber):
    wave_count = lax.axis_size("wave")
    lev_count = lax.axis_size("lev")
    wave_index = lax.axis_index("wave")
    lev_index = lax.axis_index("lev")
    lat_total = legendre.shape[1]
    degree_count = legendre.shape[2]
    set_span = lat_total // wave_count
    wave_total = wavenumber.shape[0]
    own_wave = lax.dynamic_slice_in_dim(wavenumber, wave_index, 1, 0)
    kept_degrees = (
        jnp.arange(degree_count, dtype=jnp.int32)[None, :] <= (degree_count - 1 - own_wave)[:, None]
    )
    masked_spec = jnp.where(kept_degrees, spectral, jnp.zeros_like(spectral))
    fourier = jnp.einsum(
        "flrsn,sjn->flrsj", masked_spec, legendre, preferred_element_type=jnp.float32
    ).astype(jnp.bfloat16)
    circle_max = 20 + 4 * (lat_total // 2 - 1)
    band_cap = (circle_max + lev_count - 1) // lev_count
    latitude = wave_index * set_span + jnp.arange(set_span, dtype=jnp.int32)
    band_index = jnp.reshape(lev_index, (1,))
    synth_table, analysis_table, planetary = circle_tables(
        latitude, band_index, wavenumber, lat_total, lev_count, band_cap, wave_total
    )
    set_fourier = lax.all_to_all(fourier, "wave", split_axis=4, concat_axis=3, tiled=True)
    grid_values = jnp.einsum(
        "flrsq,qprs->flqp",
        lax.all_gather(set_fourier, "lev", axis=1, tiled=True),
        synth_table,
        preferred_element_type=jnp.float32,
    )
    tendency = tendencies(grid_values, planetary)
    summed = lax.psum_scatter(
        jnp.einsum(
            "flqp,qprs->lfrsq", tendency, analysis_table, preferred_element_type=jnp.float32
        ),
        "lev",
        scatter_dimension=0,
        tiled=True,
    )
    returned = lax.all_to_all(
        summed.astype(jnp.bfloat16), "wave", split_axis=3, concat_axis=4, tiled=True
    )
    analysed = jnp.einsum(
        "lfrsj,sjn->flrsn", returned, legendre, preferred_element_type=jnp.float32
    )
    return jnp.where(kept_degrees, analysed, jnp.zeros_like(analysed)).astype(jnp.bfloat16)


def solution(mesh):
    in_specs = (P(None, "lev", None, "wave", None), P("wave", None, None), P())
    out_specs = P(None, "lev", None, "wave", None)
    return jax.shard_map(body, mesh=mesh, in_specs=in_specs, out_specs=out_specs, check_vma=False)
```

```python
import functools
import math

import jax
import jax.numpy as jnp
from jax import lax
from jax.experimental import pallas as pl
from jax.experimental.pallas import tpu as pltpu
from jax.sharding import PartitionSpec as P

SUB = 8
LANES = 128
WIDTH = 256
QUARTERS = 4
FIRST = 5
NT = (((1,), (1,)), ((), ()))
NN = (((1,), (0,)), ((), ()))
F32 = jnp.float32
BF16 = jnp.bfloat16


def dot(a, b, dims):
    return lax.dot_general(a, b, dims, preferred_element_type=F32)


def iota(shape, dim):
    return lax.broadcasted_iota(jnp.int32, shape, dim)


def one_hot(mask):
    return jnp.where(mask, 1.0, 0.0).astype(BF16)


def cos_sin_turns(turns):
    quadrant = jnp.floor(turns * 4.0 + 0.5)
    u = (turns - quadrant * 0.25) * (2.0 * math.pi)
    u2 = u * u
    sine = u * (1.0 + u2 * (-1 / 6 + u2 * (1 / 120 + u2 * (-1 / 5040 + u2 * (1 / 362880)))))
    cosine = 1.0 + u2 * (-0.5 + u2 * (1 / 24 + u2 * (-1 / 720 + u2 * (1 / 40320))))
    quadrant = quadrant.astype(jnp.int32) & 3
    odd = (quadrant & 1) == 1
    c = jnp.where(odd, sine, cosine)
    s = jnp.where(odd, cosine, sine)
    c = jnp.where((quadrant == 1) | (quadrant == 2), -c, c)
    s = jnp.where(quadrant >= 2, -s, s)
    return c, s


def cos_sin_phase(wavenumber, point, circle):
    inverse = 1.0 / circle
    product = wavenumber * point
    whole = jnp.floor(product * inverse + 0.5)
    return cos_sin_turns((product - whole * circle) * inverse)


def quarter_turns(wavenumber, band):
    k = (wavenumber * band) & 3
    c = jnp.where(k == 0, 1.0, jnp.where(k == 2, -1.0, 0.0))
    s = jnp.where(k == 1, 1.0, jnp.where(k == 3, -1.0, 0.0))
    return c, s


def plain_part(group, south):
    return (group % 2 == 0) != south


def block_place(block, groups):
    south = block >= groups
    return (2 * groups - 1 - block if south else block), south


def reverse_matrix(n):
    return one_hot(iota((n, n), 0) + iota((n, n), 1) == n - 1)


def forward_kernel(
    groups, waves, levels, lats, wn_hbm, spec_hbm, leg_hbm,
    out_ref, kept_ref, leg, synth, analysis, planet, turns, backs, wn, spec, sems,
):
    block = leg.shape[1]
    first = [
        pltpu.make_async_copy(wn_hbm, wn, sems.at[4 * groups]),
        pltpu.make_async_copy(spec_hbm, spec, sems.at[4 * groups + 1]),
    ]
    chunks = []
    for k in range(0, 2 * groups, 2):
        runs = [pieces_of(k + h, groups, block) for h in range(2)]
        if len(runs[0]) == len(runs[1]) == 1:
            source = leg_hbm.at[0, pl.ds(k * block, 2 * block)].reshape(2, block, leg.shape[2])
            places = [(source, leg.at[pl.ds(k, 2)])]
        else:
            places = [
                (
                    leg_hbm.at[0, pl.ds((k + h) * block + source, rows)],
                    leg.at[k + h, pl.ds(target, rows)],
                )
                for h in range(2)
                for source, target, rows in runs[h]
            ]
        chunks.append(
            [
                pltpu.make_async_copy(*place, sems.at[2 * k + n])
                for n, place in enumerate(places)
            ]
        )
    for copy in first + sum(chunks, []):
        copy.start()
    for copy in first:
        copy.wait()
    degrees = leg.shape[2]
    kept = iota((SUB, degrees), 1) <= degrees - 1 - wn[lax.axis_index("wave")]
    kept_ref[...] = jnp.where(kept, 1.0, 0.0)
    rows = [spec[f, 0, 0].astype(F32) for f in range(2)]
    rows = jnp.concatenate(rows + [jnp.zeros((SUB - 4, degrees), F32)], axis=0)
    rows = jnp.where(kept, rows, 0.0)
    rows = rows.astype(BF16)
    reverse = reverse_matrix(block)
    pieces = [[], []]
    device = this_device(waves)
    numbers = [wn[w] for w in range(waves)]
    counts = chunk_counts(groups, block, synth.shape[2])
    turn_tables(waves, numbers, turns, backs)
    analysis[sum(counts)] = jnp.zeros(analysis.shape[1:], BF16)
    for k in range(2 * groups):
        group, south = block_place(k, groups)
        if k % 2 == 0:
            g = groups - 1 - k // 2
            group_tables(
                g, sum(counts[:g]), counts[g], waves, block, lats, numbers, device,
                synth, analysis, planet,
            )
            for copy in chunks[k // 2]:
                copy.wait()
        pieces[0 if plain_part(group, south) else 1].append((group, dot(rows, leg[k], NT)))
    pieces = [[v for _, v in sorted(p, key=lambda x: x[0])] for p in pieces]
    blank = jnp.zeros((SUB, block), F32)
    n = LANES // SUB
    plain = jnp.concatenate(pieces[0] + [blank] * (n - groups), axis=0)
    turned = jnp.concatenate([blank] * groups + pieces[1] + [blank] * (n - 2 * groups), axis=0)
    placed = jnp.transpose(plain) + dot(reverse, turned.astype(BF16), NT)
    out_ref[...] = placed.astype(BF16).reshape(out_ref.shape)


def backward_kernel(groups, kept_ref, leg, got_ref, out_ref):
    block, degrees = leg.shape[1:]
    got = jnp.transpose(got_ref[...].reshape(block, LANES).astype(F32))[: groups * SUB]
    plain = got.astype(BF16)
    turned = dot(plain, reverse_matrix(block), NN).astype(BF16)
    order = sorted(range(2 * groups), key=lambda k: not plain_part(*block_place(k, groups)))

    def add_up(width):
        sums = [jnp.zeros((SUB, width), F32)] * 2
        for k in order:
            g, south = block_place(k, groups)
            rows = plain if plain_part(g, south) else turned
            sums[south] = sums[south] + dot(
                rows[g * SUB : (g + 1) * SUB], leg[k, :, :width], NN
            )
        for f in range(2):
            for r in range(2):
                row = r * 4 + f * 2
                total = sums[0][row : row + 1] + sums[1][row + 1 : row + 2]
                total = (total * kept_ref[:1, :width]).astype(BF16)
                if width < degrees:
                    rest = jnp.zeros((1, degrees - width), BF16)
                    total = jnp.concatenate([total, rest], axis=1)
                out_ref[f, 0, 0, r : r + 1] = total

    held = jnp.sum(kept_ref[:1]).astype(jnp.int32)
    for width in range(WIDTH, degrees + 1, WIDTH):
        pl.when((held > width - WIDTH) & (held <= width))(functools.partial(add_up, width))


def chunk_counts(groups, block, step):
    return [-(-(FIRST + block * (g + 1) - 1) // step) for g in range(groups)]


def shift_of(group, block):
    return group // 2 * (block // 4) % block


def latitude(group, block, order):
    turned = (order + shift_of(group, block)) % block
    return group * block + (turned if group % 2 == 0 else block - 1 - turned)


def pieces_of(block_index, groups, block):
    group, south = block_place(block_index, groups)
    by = shift_of(group, block)
    by = (-by if plain_part(group, south) else by) % block
    if by == 0:
        return [(0, 0, block)]
    return [(0, by, block - by), (block - by, 0, by)]


def step_counts(groups, block, step, device, largest):
    counts = []
    for g in range(groups):
        ends = [latitude(g, block, device * SUB + q) for q in (0, SUB - 1)]
        counts.append((FIRST + largest(*ends) + step - 1) // step)
    return counts


def this_device(waves):
    return lax.axis_index("lev") * waves + lax.axis_index("wave")


def turn_tables(waves, numbers, turns, backs):
    half = waves * SUB

    def slot_number(lanes):
        value = jnp.zeros(lanes.shape, jnp.int32)
        for s in range(waves):
            value = jnp.where(lanes == s, numbers[s], value)
        return value

    shape = turns.shape[1:]
    turns[0], turns[1] = quarter_turns(
        slot_number((iota(shape, 1) // SUB) % waves), iota(shape, 0) // 2
    )
    shape = backs.shape[1:]
    lane = iota(shape, 1)
    back_c, back_s = quarter_turns(slot_number((lane // SUB) % waves), iota(shape, 0) // 2)
    backs[0], backs[1] = back_c, jnp.where(lane < half, back_s, -back_s)


def group_tables(g, slot, count, waves, block, lats, numbers, device, synth, analysis, planet):
    half = waves * SUB
    step = synth.shape[2]
    shape = (SUB, LANES)
    lat = latitude(g, block, device * SUB + iota(shape, 0)).astype(F32)
    quarter = lat + FIRST
    circle = QUARTERS * quarter
    polar_c, polar_s = cos_sin_turns((lat + 0.5) * (0.5 / lats))
    scale = 1.0 / math.sqrt(waves)
    weight = polar_s / jnp.sqrt(circle) * (1.0 / scale)
    sign = jnp.where(iota(shape, 0) % 2 == 0, 2.0, -2.0)
    for q in range(SUB):
        value = jnp.broadcast_to(polar_c[q : q + 1], shape) * sign
        for part in range(step // LANES):
            planet[g, q * SUB : (q + 1) * SUB, part * LANES : (part + 1) * LANES] = value

    point = iota(shape, 1)
    inside = quarter.astype(jnp.int32)
    for s in range(0, waves, 2):
        pair, turn = [], []
        for k in range(2):
            c, n = cos_sin_phase(numbers[s + k].astype(F32), point.astype(F32), circle)
            mid_c = jnp.broadcast_to(c[:, LANES // 2 : LANES // 2 + 1], shape)
            mid_s = jnp.broadcast_to(n[:, LANES // 2 : LANES // 2 + 1], shape)
            turn.append((mid_c * mid_c - mid_s * mid_s, 2.0 * mid_c * mid_s))
            pair.append((c * scale, n * -scale))
        for a in range(count * (step // LANES)):
            at = slot + a * LANES // step
            lanes = pl.ds(a * LANES % step, LANES)
            for part in range(2):
                rows = pl.ds(part * half + s * SUB, 2 * SUB)
                basis = [v[part] for v in pair]
                synth[at, rows, lanes] = jnp.concatenate(basis, axis=0).astype(BF16)
                basis = [v * weight for v in basis]
                if (a + 1) * LANES > FIRST + g * block:
                    basis = [jnp.where(point + a * LANES < inside, v, 0.0) for v in basis]
                analysis[at, rows, lanes] = jnp.concatenate(basis, axis=0).astype(BF16)
            pair = [
                (c * tc + n * ts, n * tc - c * ts) for (c, n), (tc, ts) in zip(pair, turn)
            ]


def grid_kernel(
    groups, waves, levels, step, synth, analysis, planet, turns, backs, got_ref, out_ref,
    coef, grid_a, grid_b, tend_a, tend_b, total, kept,
):
    block = waves * levels * SUB
    half = waves * SUB
    device = this_device(waves)
    row, lane = iota((SUB, LANES), 0), iota((SUB, LANES), 1)
    first = lane < half
    which = lane % SUB

    got = jnp.transpose(got_ref[...].reshape(block, LANES).astype(F32))
    turn_c, turn_s = turns[0], turns[1]
    north = iota((SUB, block), 0) % 2 == 0

    def spread(group, pair):
        rows = [p * groups * SUB + group * SUB + pair for p in (group % 2, 1 - group % 2)]
        here, there = (jnp.broadcast_to(got[r : r + 1], (SUB, block)) for r in rows)
        return jnp.where(north, here, there)


    for g in range(groups):
        for f in range(2):
            real, imag = spread(g, f * 2), spread(g, f * 2 + 1)
            turned_r = real * turn_c - imag * turn_s
            turned_i = real * turn_s + imag * turn_c
            for l in range(levels):
                cut = slice((l // 2) * LANES, (l // 2 + 1) * LANES)
                a, b = turned_r[:, cut], turned_i[:, cut]
                if l % 2 == 0:
                    b = pltpu.roll(b, half, 1)
                else:
                    a = pltpu.roll(a, half, 1)
                both = jnp.where(first, a, b)
                for q in range(0, SUB, 2):
                    place = ((f * levels + l) * SUB + q) * SUB
                    two = jnp.concatenate(
                        [jnp.where(which == q + k, both, 0.0) for k in range(2)], axis=0
                    )
                    coef[g, place : place + 2 * SUB, :] = two.astype(BF16)

    most = chunk_counts(groups, block, step)
    ends, skips = [], []
    end = 0
    for g, count in enumerate(step_counts(groups, block, step, device, jnp.maximum)):
        end = end + count
        ends.append(end)
        skips.append(most[g] - count)
    devices = waves * levels
    steps = max(sum(step_counts(groups, block, step, d, max)) for d in range(devices))

    def place_of(i):
        group, slot = jnp.int32(0), i
        for g in range(groups - 1):
            past = i >= ends[g]
            group = group + jnp.where(past, 1, 0)
            slot = slot + jnp.where(past, skips[g], 0)
        return group, slot

    rows = levels * SUB * SUB

    def synthesis(i, values):
        group, slot = place_of(jnp.minimum(i, end - 1))
        values[...] = dot(coef[group], synth[slot], NN)

    def tendencies_of(i, values, tend):
        group, _ = place_of(jnp.minimum(i, end - 1))
        for r in range(0, SUB * SUB, 2 * SUB):
            at = [pl.ds(l * SUB * SUB + r, 2 * SUB) for l in range(levels)]
            below = [pl.ds(rows + l * SUB * SUB + r, 2 * SUB) for l in range(levels)]
            div = [values[b, :] for b in below]
            column = div[0]
            for l in range(1, levels):
                column = column + div[l]
            column = column * (1.0 / math.sqrt(levels))
            turning = planet[group, pl.ds(r, 2 * SUB), :]
            for l in range(levels):
                vort = values[at[l], :]
                absolute = vort + turning
                tend[at[l], :] = (-absolute * div[l]).astype(BF16)
                tend[below[l], :] = (absolute * vort - div[l] * column).astype(BF16)

    def analysis_of(i, tend):
        group, slot = place_of(jnp.minimum(i, end - 1))
        slot = jnp.where(i < end, slot, sum(most))
        fresh = i == 0
        for begin in ends[:-1]:
            fresh = fresh | (i == begin)
        total[group] = jnp.where(fresh, 0.0, total[group]) + dot(tend[...], analysis[slot], NT)

    grids, tends = (grid_a, grid_b), (tend_a, tend_b)

    @pl.loop(0, jnp.minimum(end, 1))
    def _(_):
        for i in range(steps + 2):
            if i < steps:
                synthesis(i, grids[i % 2])
            if 1 <= i <= steps:
                tendencies_of(i - 1, grids[(i - 1) % 2], tends[(i - 1) % 2])
            if i >= 2:
                analysis_of(i - 2, tends[i % 2])

    back_c, back_s = backs[0], backs[1]
    kept[...] = jnp.zeros_like(kept)
    for g in range(groups):
        sums = []
        for f in range(2):
            for l in range(levels):
                base = (f * levels + l) * SUB * SUB
                value = jnp.zeros((SUB, LANES), F32)
                for q in range(SUB):
                    part = total[g, base + q * SUB : base + (q + 1) * SUB, :]
                    value = jnp.where(which == q, part, value)
                value = value * back_c + pltpu.roll(value, half, 1) * back_s
                value = value + pltpu.roll(value, 4, 0)
                sums.append(value + pltpu.roll(value, 2, 0))
        lined = []
        for l in range(levels):
            both = jnp.where(row % 4 < 2, sums[l], sums[levels + l])
            swapped = pltpu.roll(both, half, 1)
            lined.append(jnp.where((row < 4) == (l % 2 == 0), both, swapped))
        for p in range(levels // 2):
            kept[p, g * SUB : (g + 1) * SUB, :] = jnp.where(first, lined[2 * p], lined[2 * p + 1])
    for p in range(levels // 2):
        moved = jnp.transpose(kept[p]).astype(BF16)
        out_ref[p * 2 * waves : (p + 1) * 2 * waves] = moved.reshape(2 * waves, SUB, LANES)


def fast_body(groups, waves, levels, step, spectral, legendre, wavenumber):
    lats, degrees = legendre.shape[1:]
    devices = waves * levels
    block = devices * SUB
    vmem = pl.BlockSpec(memory_space=pltpu.VMEM)
    hbm = pl.BlockSpec(memory_space=pltpu.HBM)
    params = pltpu.CompilerParams(vmem_limit_bytes=24 * 1024 * 1024)
    parcel = jax.ShapeDtypeStruct((devices, SUB, LANES), BF16)
    spectral = jnp.transpose(spectral, (0, 1, 3, 2, 4))
    slots = sum(chunk_counts(groups, block, step))
    sent, kept, leg, *tables = pl.pallas_call(
        functools.partial(forward_kernel, groups, waves, levels, lats),
        out_shape=[
            parcel,
            jax.ShapeDtypeStruct((SUB, degrees), F32),
            jax.ShapeDtypeStruct((2 * groups, block, degrees), BF16),
            jax.ShapeDtypeStruct((slots, LANES, step), BF16),
            jax.ShapeDtypeStruct((slots + 1, LANES, step), BF16),
            jax.ShapeDtypeStruct((groups, SUB * SUB, step), F32),
            jax.ShapeDtypeStruct((2, SUB, block), F32),
            jax.ShapeDtypeStruct((2, SUB, LANES), F32),
        ],
        in_specs=[hbm, hbm, hbm],
        out_specs=[vmem] * 8,
        scratch_shapes=[
            pltpu.SMEM(wavenumber.shape, jnp.int32),
            pltpu.VMEM(spectral.shape, BF16),
            pltpu.SemaphoreType.DMA((4 * groups + 2,)),
        ],
        compiler_params=params,
        name="forward",
    )(*(pltpu.with_memory_space_constraint(x, pltpu.HBM) for x in (wavenumber, spectral, legendre)))
    got = lax.all_to_all(sent, ("lev", "wave"), 0, 0, tiled=True)
    rows = 2 * levels * SUB * SUB
    tend = pl.pallas_call(
        functools.partial(grid_kernel, groups, waves, levels, step),
        out_shape=parcel,
        in_specs=[vmem] * 6,
        out_specs=vmem,
        scratch_shapes=[
            pltpu.VMEM((groups, rows, LANES), BF16),
            pltpu.VMEM((rows, step), F32),
            pltpu.VMEM((rows, step), F32),
            pltpu.VMEM((rows, step), BF16),
            pltpu.VMEM((rows, step), BF16),
            pltpu.VMEM((groups, rows, LANES), F32),
            pltpu.VMEM((levels // 2, LANES, LANES), F32),
        ],
        compiler_params=params,
        name="grid",
    )(*tables, got)
    back = lax.all_to_all(tend, ("lev", "wave"), 0, 0, tiled=True)
    out = pl.pallas_call(
        functools.partial(backward_kernel, groups),
        out_shape=jax.ShapeDtypeStruct(spectral.shape, BF16),
        in_specs=[vmem, vmem, vmem],
        out_specs=vmem,
        compiler_params=params,
        name="backward",
    )(kept, leg, back)
    return jnp.transpose(out, (0, 1, 3, 2, 4))


def body(spectral, legendre, wavenumber):
    waves, levels = lax.axis_size("wave"), lax.axis_size("lev")
    lats = legendre.shape[1]
    group_lats = waves * levels * SUB
    groups = lats // (2 * group_lats)
    fits = (
        2 * groups * group_lats == lats
        and wavenumber.shape[0] == waves
        and spectral.shape[1] == 1
        and 2 * waves * SUB == LANES
        and levels % 2 == 0
        and 2 * groups * SUB <= LANES
        and group_lats % LANES == 0
        and legendre.shape[2] % WIDTH == 0
    )
    if fits:
        return fast_body(groups, waves, levels, 2 * LANES, spectral, legendre, wavenumber)
    return general_body(spectral, legendre, wavenumber)


def circle_tables(latitude, band_index, wavenumber, lat_total, band_total, band_cap, wave_total):
    circle_length = 20 + 4 * jnp.minimum(latitude, lat_total - 1 - latitude)
    band_width = (circle_length + band_total - 1) // band_total
    offsets = jnp.arange(band_cap, dtype=jnp.int32)
    longitude_index = band_index[None, :, None] * band_width[:, None, None] + offsets[None, None, :]
    inside = (offsets[None, None, :] < band_width[:, None, None]) & (
        longitude_index < circle_length[:, None, None]
    )
    rows = latitude.shape[0]
    longitude_index = longitude_index.reshape(rows, -1)
    inside = inside.reshape(rows, -1)
    phase_index = (
        wavenumber[None, None, :] * longitude_index[:, :, None] % circle_length[:, None, None]
    )
    length_float = circle_length.astype(jnp.float32)
    angles = 2.0 * math.pi * phase_index.astype(jnp.float32) / length_float[:, None, None]
    shown = inside[:, :, None].astype(jnp.float32)
    trig_basis = jnp.stack([jnp.cos(angles) * shown, -jnp.sin(angles) * shown], axis=2)
    colatitude = (latitude.astype(jnp.float32) + 0.5) * (math.pi / lat_total)
    circle_weight = jnp.sin(colatitude) / jnp.sqrt(length_float)
    synth_table = (trig_basis / math.sqrt(wave_total)).astype(jnp.bfloat16)
    analysis_table = (trig_basis * circle_weight[:, None, None, None]).astype(jnp.bfloat16)
    return (synth_table, analysis_table, 2.0 * jnp.cos(colatitude))


def tendencies(grid_values, planetary):
    vorticity = grid_values[0]
    divergence = grid_values[1]
    absolute_vort = vorticity + planetary[None, :, None]
    column_div = jnp.sum(divergence, axis=0) / math.sqrt(divergence.shape[0])
    return jnp.stack(
        [-absolute_vort * divergence, absolute_vort * vorticity - divergence * column_div[None]]
    ).astype(jnp.bfloat16)


def general_body(spectral, legendre, wavenumber):
    wave_count = lax.axis_size("wave")
    lev_count = lax.axis_size("lev")
    wave_index = lax.axis_index("wave")
    lev_index = lax.axis_index("lev")
    lat_total = legendre.shape[1]
    degree_count = legendre.shape[2]
    set_span = lat_total // wave_count
    wave_total = wavenumber.shape[0]
    own_wave = lax.dynamic_slice_in_dim(wavenumber, wave_index, 1, 0)
    kept_degrees = (
        jnp.arange(degree_count, dtype=jnp.int32)[None, :] <= (degree_count - 1 - own_wave)[:, None]
    )
    masked_spec = jnp.where(kept_degrees, spectral, jnp.zeros_like(spectral))
    fourier = jnp.einsum(
        "flrsn,sjn->flrsj", masked_spec, legendre, preferred_element_type=jnp.float32
    ).astype(jnp.bfloat16)
    circle_max = 20 + 4 * (lat_total // 2 - 1)
    band_cap = (circle_max + lev_count - 1) // lev_count
    latitude = wave_index * set_span + jnp.arange(set_span, dtype=jnp.int32)
    band_index = jnp.reshape(lev_index, (1,))
    synth_table, analysis_table, planetary = circle_tables(
        latitude, band_index, wavenumber, lat_total, lev_count, band_cap, wave_total
    )
    set_fourier = lax.all_to_all(fourier, "wave", split_axis=4, concat_axis=3, tiled=True)
    grid_values = jnp.einsum(
        "flrsq,qprs->flqp",
        lax.all_gather(set_fourier, "lev", axis=1, tiled=True),
        synth_table,
        preferred_element_type=jnp.float32,
    )
    tendency = tendencies(grid_values, planetary)
    summed = lax.psum_scatter(
        jnp.einsum(
            "flqp,qprs->lfrsq", tendency, analysis_table, preferred_element_type=jnp.float32
        ),
        "lev",
        scatter_dimension=0,
        tiled=True,
    )
    returned = lax.all_to_all(
        summed.astype(jnp.bfloat16), "wave", split_axis=3, concat_axis=4, tiled=True
    )
    analysed = jnp.einsum(
        "lfrsj,sjn->flrsn", returned, legendre, preferred_element_type=jnp.float32
    )
    return jnp.where(kept_degrees, analysed, jnp.zeros_like(analysed)).astype(jnp.bfloat16)


def solution(mesh):
    in_specs = (P(None, "lev", None, "wave", None), P("wave", None, None), P())
    out_specs = P(None, "lev", None, "wave", None)
    return jax.shard_map(body, mesh=mesh, in_specs=in_specs, out_specs=out_specs, check_vma=False)
```

```python
import functools
import math

import jax
import jax.numpy as jnp
from jax import lax
from jax.experimental import pallas as pl
from jax.experimental.pallas import tpu as pltpu
from jax.sharding import PartitionSpec as P

SUB = 8
LANES = 128
AHEAD = 2
WIDTH = 256
QUARTERS = 4
FIRST = 5
NT = (((1,), (1,)), ((), ()))
NN = (((1,), (0,)), ((), ()))
F32 = jnp.float32
BF16 = jnp.bfloat16


def dot(a, b, dims):
    return lax.dot_general(a, b, dims, preferred_element_type=F32)


def iota(shape, dim):
    return lax.broadcasted_iota(jnp.int32, shape, dim)


def one_hot(mask):
    return jnp.where(mask, 1.0, 0.0).astype(BF16)


def cos_sin_turns(turns):
    quadrant = jnp.floor(turns * 4.0 + 0.5)
    u = (turns - quadrant * 0.25) * (2.0 * math.pi)
    u2 = u * u
    sine = u * (1.0 + u2 * (-1 / 6 + u2 * (1 / 120 + u2 * (-1 / 5040 + u2 * (1 / 362880)))))
    cosine = 1.0 + u2 * (-0.5 + u2 * (1 / 24 + u2 * (-1 / 720 + u2 * (1 / 40320))))
    quadrant = quadrant.astype(jnp.int32) & 3
    odd = (quadrant & 1) == 1
    c = jnp.where(odd, sine, cosine)
    s = jnp.where(odd, cosine, sine)
    c = jnp.where((quadrant == 1) | (quadrant == 2), -c, c)
    s = jnp.where(quadrant >= 2, -s, s)
    return c, s


def cos_sin_phase(wavenumber, point, circle):
    inverse = 1.0 / circle
    product = wavenumber * point
    whole = jnp.floor(product * inverse + 0.5)
    return cos_sin_turns((product - whole * circle) * inverse)


def quarter_turns(wavenumber, band):
    k = (wavenumber * band) & 3
    c = jnp.where(k == 0, 1.0, jnp.where(k == 2, -1.0, 0.0))
    s = jnp.where(k == 1, 1.0, jnp.where(k == 3, -1.0, 0.0))
    return c, s


def plain_part(group, south):
    return (group % 2 == 0) != south


def block_place(block, groups):
    south = block >= groups
    return (2 * groups - 1 - block if south else block), south


def reverse_matrix(n):
    return one_hot(iota((n, n), 0) + iota((n, n), 1) == n - 1)


def forward_kernel(
    groups, waves, levels, lats, wn_hbm, spec_hbm, leg_hbm,
    out_ref, kept_ref, leg, synth, analysis, planet, turns, backs, wn, spec, sems,
):
    block = leg.shape[1]
    first = [
        pltpu.make_async_copy(wn_hbm, wn, sems.at[4 * groups]),
        pltpu.make_async_copy(spec_hbm, spec, sems.at[4 * groups + 1]),
    ]
    def chunk_copies(k, width):
        runs = [pieces_of(k + h, groups, block) for h in range(2)]
        columns = pl.ds(0, width)
        if len(runs[0]) == len(runs[1]) == 1:
            source = leg_hbm.at[0, pl.ds(k * block, 2 * block)].reshape(2, block, leg.shape[2])
            places = [(source.at[:, :, columns], leg.at[pl.ds(k, 2), :, columns])]
        else:
            places = [
                (
                    leg_hbm.at[0, pl.ds((k + h) * block + source, rows), columns],
                    leg.at[k + h, pl.ds(target, rows), columns],
                )
                for h in range(2)
                for source, target, rows in runs[h]
            ]
        return [
            pltpu.make_async_copy(*place, sems.at[2 * k + n]) for n, place in enumerate(places)
        ]

    degrees = leg.shape[2]
    ahead = [chunk_copies(k, degrees) for k in range(0, 2 * groups, 2)[:AHEAD]]
    for copy in first + sum(ahead, []):
        copy.start()
    for copy in first:
        copy.wait()
    held = degrees - wn[lax.axis_index("wave")]
    kept = iota((SUB, degrees), 1) < held
    kept_ref[...] = jnp.where(kept, 1.0, 0.0)
    rows = [spec[f, 0, 0].astype(F32) for f in range(2)]
    rows = jnp.concatenate(rows + [jnp.zeros((SUB - 4, degrees), F32)], axis=0)
    rows = jnp.where(kept, rows, 0.0)
    rows = rows.astype(BF16)
    reverse = reverse_matrix(block)
    device = this_device(waves)
    numbers = [wn[w] for w in range(waves)]
    counts = chunk_counts(groups, block, synth.shape[2])
    turn_tables(waves, numbers, turns, backs)
    analysis[sum(counts)] = jnp.zeros(analysis.shape[1:], BF16)

    def add_up(width):
        late = [chunk_copies(k, width) for k in range(0, 2 * groups, 2)[AHEAD:]]
        for copy in sum(late, []):
            copy.start()
        chunks = ahead + late
        pieces = [[], []]
        for k in range(2 * groups):
            group, south = block_place(k, groups)
            if k % 2 == 0:
                g = groups - 1 - k // 2
                group_tables(
                    g, sum(counts[:g]), counts[g], waves, block, lats, numbers, device,
                    synth, analysis, planet,
                )
                for copy in chunks[k // 2]:
                    copy.wait()
            pieces[0 if plain_part(group, south) else 1].append((group, dot(rows[:, :width], leg[k, :, :width], NT)))
        pieces = [[v for _, v in sorted(p, key=lambda x: x[0])] for p in pieces]
        blank = jnp.zeros((SUB, block), F32)
        n = LANES // SUB
        plain = jnp.concatenate(pieces[0] + [blank] * (n - groups), axis=0)
        turned = jnp.concatenate([blank] * groups + pieces[1] + [blank] * (n - 2 * groups), axis=0)
        placed = jnp.transpose(plain) + dot(reverse, turned.astype(BF16), NT)
        out_ref[...] = placed.astype(BF16).reshape(out_ref.shape)

    for width in range(WIDTH, degrees + 1, WIDTH):
        pl.when((held > width - WIDTH) & (held <= width))(functools.partial(add_up, width))


def backward_kernel(groups, kept_ref, leg, got_ref, out_ref):
    block, degrees = leg.shape[1:]
    got = jnp.transpose(got_ref[...].reshape(block, LANES).astype(F32))[: groups * SUB]
    plain = got.astype(BF16)
    turned = dot(plain, reverse_matrix(block), NN).astype(BF16)
    order = sorted(range(2 * groups), key=lambda k: not plain_part(*block_place(k, groups)))

    def add_up(width):
        sums = [jnp.zeros((SUB, width), F32)] * 2
        for k in order:
            g, south = block_place(k, groups)
            rows = plain if plain_part(g, south) else turned
            sums[south] = sums[south] + dot(
                rows[g * SUB : (g + 1) * SUB], leg[k, :, :width], NN
            )
        for f in range(2):
            for r in range(2):
                row = r * 4 + f * 2
                total = sums[0][row : row + 1] + sums[1][row + 1 : row + 2]
                total = (total * kept_ref[:1, :width]).astype(BF16)
                if width < degrees:
                    rest = jnp.zeros((1, degrees - width), BF16)
                    total = jnp.concatenate([total, rest], axis=1)
                out_ref[f, 0, 0, r : r + 1] = total

    held = jnp.sum(kept_ref[:1]).astype(jnp.int32)
    for width in range(WIDTH, degrees + 1, WIDTH):
        pl.when((held > width - WIDTH) & (held <= width))(functools.partial(add_up, width))


def chunk_counts(groups, block, step):
    return [-(-(FIRST + block * (g + 1) - 1) // step) for g in range(groups)]


def shift_of(group, block):
    return group // 2 * (block // 4) % block


def latitude(group, block, order):
    turned = (order + shift_of(group, block)) % block
    return group * block + (turned if group % 2 == 0 else block - 1 - turned)


def pieces_of(block_index, groups, block):
    group, south = block_place(block_index, groups)
    by = shift_of(group, block)
    by = (-by if plain_part(group, south) else by) % block
    if by == 0:
        return [(0, 0, block)]
    return [(0, by, block - by), (block - by, 0, by)]


def step_counts(groups, block, step, device, largest):
    counts = []
    for g in range(groups):
        ends = [latitude(g, block, device * SUB + q) for q in (0, SUB - 1)]
        counts.append((FIRST + largest(*ends) + step - 1) // step)
    return counts


def this_device(waves):
    return lax.axis_index("lev") * waves + lax.axis_index("wave")


def turn_tables(waves, numbers, turns, backs):
    half = waves * SUB

    def slot_number(lanes):
        value = jnp.zeros(lanes.shape, jnp.int32)
        for s in range(waves):
            value = jnp.where(lanes == s, numbers[s], value)
        return value

    shape = turns.shape[1:]
    turns[0], turns[1] = quarter_turns(
        slot_number((iota(shape, 1) // SUB) % waves), iota(shape, 0) // 2
    )
    shape = backs.shape[1:]
    lane = iota(shape, 1)
    back_c, back_s = quarter_turns(slot_number((lane // SUB) % waves), iota(shape, 0) // 2)
    backs[0], backs[1] = back_c, jnp.where(lane < half, back_s, -back_s)


def group_tables(g, slot, count, waves, block, lats, numbers, device, synth, analysis, planet):
    half = waves * SUB
    step = synth.shape[2]
    shape = (SUB, LANES)
    lat = latitude(g, block, device * SUB + iota(shape, 0)).astype(F32)
    quarter = lat + FIRST
    circle = QUARTERS * quarter
    polar_c, polar_s = cos_sin_turns((lat + 0.5) * (0.5 / lats))
    scale = 1.0 / math.sqrt(waves)
    weight = polar_s / jnp.sqrt(circle) * (1.0 / scale)
    sign = jnp.where(iota(shape, 0) % 2 == 0, 2.0, -2.0)
    for q in range(SUB):
        value = jnp.broadcast_to(polar_c[q : q + 1], shape) * sign
        for part in range(step // LANES):
            planet[g, q * SUB : (q + 1) * SUB, part * LANES : (part + 1) * LANES] = value

    point = iota(shape, 1)
    inside = quarter.astype(jnp.int32)
    for s in range(0, waves, 2):
        pair, turn = [], []
        for k in range(2):
            c, n = cos_sin_phase(numbers[s + k].astype(F32), point.astype(F32), circle)
            mid_c = jnp.broadcast_to(c[:, LANES // 2 : LANES // 2 + 1], shape)
            mid_s = jnp.broadcast_to(n[:, LANES // 2 : LANES // 2 + 1], shape)
            turn.append((mid_c * mid_c - mid_s * mid_s, 2.0 * mid_c * mid_s))
            pair.append((c * scale, n * -scale))
        for a in range(count * (step // LANES)):
            at = slot + a * LANES // step
            lanes = pl.ds(a * LANES % step, LANES)
            for part in range(2):
                rows = pl.ds(part * half + s * SUB, 2 * SUB)
                basis = [v[part] for v in pair]
                synth[at, rows, lanes] = jnp.concatenate(basis, axis=0).astype(BF16)
                basis = [v * weight for v in basis]
                if (a + 1) * LANES > FIRST + g * block:
                    basis = [jnp.where(point + a * LANES < inside, v, 0.0) for v in basis]
                analysis[at, rows, lanes] = jnp.concatenate(basis, axis=0).astype(BF16)
            pair = [
                (c * tc + n * ts, n * tc - c * ts) for (c, n), (tc, ts) in zip(pair, turn)
            ]


def grid_kernel(
    groups, waves, levels, step, synth, analysis, planet, turns, backs, got_ref, out_ref,
    coef, grid_a, grid_b, tend_a, tend_b, total, kept,
):
    block = waves * levels * SUB
    half = waves * SUB
    device = this_device(waves)
    row, lane = iota((SUB, LANES), 0), iota((SUB, LANES), 1)
    first = lane < half
    which = lane % SUB

    got = jnp.transpose(got_ref[...].reshape(block, LANES).astype(F32))
    turn_c, turn_s = turns[0], turns[1]
    north = iota((SUB, block), 0) % 2 == 0

    def spread(group, pair):
        rows = [p * groups * SUB + group * SUB + pair for p in (group % 2, 1 - group % 2)]
        here, there = (jnp.broadcast_to(got[r : r + 1], (SUB, block)) for r in rows)
        return jnp.where(north, here, there)


    for g in range(groups):
        for f in range(2):
            real, imag = spread(g, f * 2), spread(g, f * 2 + 1)
            turned_r = real * turn_c - imag * turn_s
            turned_i = real * turn_s + imag * turn_c
            for l in range(levels):
                cut = slice((l // 2) * LANES, (l // 2 + 1) * LANES)
                a, b = turned_r[:, cut], turned_i[:, cut]
                if l % 2 == 0:
                    b = pltpu.roll(b, half, 1)
                else:
                    a = pltpu.roll(a, half, 1)
                both = jnp.where(first, a, b)
                for q in range(0, SUB, 2):
                    place = ((f * levels + l) * SUB + q) * SUB
                    two = jnp.concatenate(
                        [jnp.where(which == q + k, both, 0.0) for k in range(2)], axis=0
                    )
                    coef[g, place : place + 2 * SUB, :] = two.astype(BF16)

    most = chunk_counts(groups, block, step)
    ends, skips = [], []
    end = 0
    for g, count in enumerate(step_counts(groups, block, step, device, jnp.maximum)):
        end = end + count
        ends.append(end)
        skips.append(most[g] - count)
    devices = waves * levels
    steps = max(sum(step_counts(groups, block, step, d, max)) for d in range(devices))

    def place_of(i):
        group, slot = jnp.int32(0), i
        for g in range(groups - 1):
            past = i >= ends[g]
            group = group + jnp.where(past, 1, 0)
            slot = slot + jnp.where(past, skips[g], 0)
        return group, slot

    rows = levels * SUB * SUB

    def synthesis(i, values):
        group, slot = place_of(jnp.minimum(i, end - 1))
        values[...] = dot(coef[group], synth[slot], NN)

    def tendencies_of(i, values, tend):
        group, _ = place_of(jnp.minimum(i, end - 1))
        for r in range(0, SUB * SUB, 2 * SUB):
            at = [pl.ds(l * SUB * SUB + r, 2 * SUB) for l in range(levels)]
            below = [pl.ds(rows + l * SUB * SUB + r, 2 * SUB) for l in range(levels)]
            div = [values[b, :] for b in below]
            column = div[0]
            for l in range(1, levels):
                column = column + div[l]
            column = column * (1.0 / math.sqrt(levels))
            turning = planet[group, pl.ds(r, 2 * SUB), :]
            for l in range(levels):
                vort = values[at[l], :]
                absolute = vort + turning
                tend[at[l], :] = (-absolute * div[l]).astype(BF16)
                tend[below[l], :] = (absolute * vort - div[l] * column).astype(BF16)

    def analysis_of(i, tend):
        group, slot = place_of(jnp.minimum(i, end - 1))
        slot = jnp.where(i < end, slot, sum(most))
        fresh = i == 0
        for begin in ends[:-1]:
            fresh = fresh | (i == begin)
        total[group] = jnp.where(fresh, 0.0, total[group]) + dot(tend[...], analysis[slot], NT)

    grids, tends = (grid_a, grid_b), (tend_a, tend_b)

    @pl.loop(0, jnp.minimum(end, 1))
    def _(_):
        for i in range(steps + 2):
            if i < steps:
                synthesis(i, grids[i % 2])
            if 1 <= i <= steps:
                tendencies_of(i - 1, grids[(i - 1) % 2], tends[(i - 1) % 2])
            if i >= 2:
                analysis_of(i - 2, tends[i % 2])

    back_c, back_s = backs[0], backs[1]
    kept[...] = jnp.zeros_like(kept)
    for g in range(groups):
        sums = []
        for f in range(2):
            for l in range(levels):
                base = (f * levels + l) * SUB * SUB
                value = jnp.zeros((SUB, LANES), F32)
                for q in range(SUB):
                    part = total[g, base + q * SUB : base + (q + 1) * SUB, :]
                    value = jnp.where(which == q, part, value)
                value = value * back_c + pltpu.roll(value, half, 1) * back_s
                value = value + pltpu.roll(value, 4, 0)
                sums.append(value + pltpu.roll(value, 2, 0))
        lined = []
        for l in range(levels):
            both = jnp.where(row % 4 < 2, sums[l], sums[levels + l])
            swapped = pltpu.roll(both, half, 1)
            lined.append(jnp.where((row < 4) == (l % 2 == 0), both, swapped))
        for p in range(levels // 2):
            kept[p, g * SUB : (g + 1) * SUB, :] = jnp.where(first, lined[2 * p], lined[2 * p + 1])
    for p in range(levels // 2):
        moved = jnp.transpose(kept[p]).astype(BF16)
        out_ref[p * 2 * waves : (p + 1) * 2 * waves] = moved.reshape(2 * waves, SUB, LANES)


def fast_body(groups, waves, levels, step, spectral, legendre, wavenumber):
    lats, degrees = legendre.shape[1:]
    devices = waves * levels
    block = devices * SUB
    vmem = pl.BlockSpec(memory_space=pltpu.VMEM)
    hbm = pl.BlockSpec(memory_space=pltpu.HBM)
    params = pltpu.CompilerParams(vmem_limit_bytes=24 * 1024 * 1024)
    parcel = jax.ShapeDtypeStruct((devices, SUB, LANES), BF16)
    spectral = jnp.transpose(spectral, (0, 1, 3, 2, 4))
    slots = sum(chunk_counts(groups, block, step))
    sent, kept, leg, *tables = pl.pallas_call(
        functools.partial(forward_kernel, groups, waves, levels, lats),
        out_shape=[
            parcel,
            jax.ShapeDtypeStruct((SUB, degrees), F32),
            jax.ShapeDtypeStruct((2 * groups, block, degrees), BF16),
            jax.ShapeDtypeStruct((slots, LANES, step), BF16),
            jax.ShapeDtypeStruct((slots + 1, LANES, step), BF16),
            jax.ShapeDtypeStruct((groups, SUB * SUB, step), F32),
            jax.ShapeDtypeStruct((2, SUB, block), F32),
            jax.ShapeDtypeStruct((2, SUB, LANES), F32),
        ],
        in_specs=[hbm, hbm, hbm],
        out_specs=[vmem] * 8,
        scratch_shapes=[
            pltpu.SMEM(wavenumber.shape, jnp.int32),
            pltpu.VMEM(spectral.shape, BF16),
            pltpu.SemaphoreType.DMA((4 * groups + 2,)),
        ],
        compiler_params=params,
        name="forward",
    )(*(pltpu.with_memory_space_constraint(x, pltpu.HBM) for x in (wavenumber, spectral, legendre)))
    got = lax.all_to_all(sent, ("lev", "wave"), 0, 0, tiled=True)
    rows = 2 * levels * SUB * SUB
    tend = pl.pallas_call(
        functools.partial(grid_kernel, groups, waves, levels, step),
        out_shape=parcel,
        in_specs=[vmem] * 6,
        out_specs=vmem,
        scratch_shapes=[
            pltpu.VMEM((groups, rows, LANES), BF16),
            pltpu.VMEM((rows, step), F32),
            pltpu.VMEM((rows, step), F32),
            pltpu.VMEM((rows, step), BF16),
            pltpu.VMEM((rows, step), BF16),
            pltpu.VMEM((groups, rows, LANES), F32),
            pltpu.VMEM((levels // 2, LANES, LANES), F32),
        ],
        compiler_params=params,
        name="grid",
    )(*tables, got)
    back = lax.all_to_all(tend, ("lev", "wave"), 0, 0, tiled=True)
    out = pl.pallas_call(
        functools.partial(backward_kernel, groups),
        out_shape=jax.ShapeDtypeStruct(spectral.shape, BF16),
        in_specs=[vmem, vmem, vmem],
        out_specs=vmem,
        compiler_params=params,
        name="backward",
    )(kept, leg, back)
    return jnp.transpose(out, (0, 1, 3, 2, 4))


def body(spectral, legendre, wavenumber):
    waves, levels = lax.axis_size("wave"), lax.axis_size("lev")
    lats = legendre.shape[1]
    group_lats = waves * levels * SUB
    groups = lats // (2 * group_lats)
    fits = (
        2 * groups * group_lats == lats
        and wavenumber.shape[0] == waves
        and spectral.shape[1] == 1
        and 2 * waves * SUB == LANES
        and levels % 2 == 0
        and 2 * groups * SUB <= LANES
        and group_lats % LANES == 0
        and legendre.shape[2] % WIDTH == 0
    )
    if fits:
        return fast_body(groups, waves, levels, 2 * LANES, spectral, legendre, wavenumber)
    return general_body(spectral, legendre, wavenumber)


def circle_tables(latitude, band_index, wavenumber, lat_total, band_total, band_cap, wave_total):
    circle_length = 20 + 4 * jnp.minimum(latitude, lat_total - 1 - latitude)
    band_width = (circle_length + band_total - 1) // band_total
    offsets = jnp.arange(band_cap, dtype=jnp.int32)
    longitude_index = band_index[None, :, None] * band_width[:, None, None] + offsets[None, None, :]
    inside = (offsets[None, None, :] < band_width[:, None, None]) & (
        longitude_index < circle_length[:, None, None]
    )
    rows = latitude.shape[0]
    longitude_index = longitude_index.reshape(rows, -1)
    inside = inside.reshape(rows, -1)
    phase_index = (
        wavenumber[None, None, :] * longitude_index[:, :, None] % circle_length[:, None, None]
    )
    length_float = circle_length.astype(jnp.float32)
    angles = 2.0 * math.pi * phase_index.astype(jnp.float32) / length_float[:, None, None]
    shown = inside[:, :, None].astype(jnp.float32)
    trig_basis = jnp.stack([jnp.cos(angles) * shown, -jnp.sin(angles) * shown], axis=2)
    colatitude = (latitude.astype(jnp.float32) + 0.5) * (math.pi / lat_total)
    circle_weight = jnp.sin(colatitude) / jnp.sqrt(length_float)
    synth_table = (trig_basis / math.sqrt(wave_total)).astype(jnp.bfloat16)
    analysis_table = (trig_basis * circle_weight[:, None, None, None]).astype(jnp.bfloat16)
    return (synth_table, analysis_table, 2.0 * jnp.cos(colatitude))


def tendencies(grid_values, planetary):
    vorticity = grid_values[0]
    divergence = grid_values[1]
    absolute_vort = vorticity + planetary[None, :, None]
    column_div = jnp.sum(divergence, axis=0) / math.sqrt(divergence.shape[0])
    return jnp.stack(
        [-absolute_vort * divergence, absolute_vort * vorticity - divergence * column_div[None]]
    ).astype(jnp.bfloat16)


def general_body(spectral, legendre, wavenumber):
    wave_count = lax.axis_size("wave")
    lev_count = lax.axis_size("lev")
    wave_index = lax.axis_index("wave")
    lev_index = lax.axis_index("lev")
    lat_total = legendre.shape[1]
    degree_count = legendre.shape[2]
    set_span = lat_total // wave_count
    wave_total = wavenumber.shape[0]
    own_wave = lax.dynamic_slice_in_dim(wavenumber, wave_index, 1, 0)
    kept_degrees = (
        jnp.arange(degree_count, dtype=jnp.int32)[None, :] <= (degree_count - 1 - own_wave)[:, None]
    )
    masked_spec = jnp.where(kept_degrees, spectral, jnp.zeros_like(spectral))
    fourier = jnp.einsum(
        "flrsn,sjn->flrsj", masked_spec, legendre, preferred_element_type=jnp.float32
    ).astype(jnp.bfloat16)
    circle_max = 20 + 4 * (lat_total // 2 - 1)
    band_cap = (circle_max + lev_count - 1) // lev_count
    latitude = wave_index * set_span + jnp.arange(set_span, dtype=jnp.int32)
    band_index = jnp.reshape(lev_index, (1,))
    synth_table, analysis_table, planetary = circle_tables(
        latitude, band_index, wavenumber, lat_total, lev_count, band_cap, wave_total
    )
    set_fourier = lax.all_to_all(fourier, "wave", split_axis=4, concat_axis=3, tiled=True)
    grid_values = jnp.einsum(
        "flrsq,qprs->flqp",
        lax.all_gather(set_fourier, "lev", axis=1, tiled=True),
        synth_table,
        preferred_element_type=jnp.float32,
    )
    tendency = tendencies(grid_values, planetary)
    summed = lax.psum_scatter(
        jnp.einsum(
            "flqp,qprs->lfrsq", tendency, analysis_table, preferred_element_type=jnp.float32
        ),
        "lev",
        scatter_dimension=0,
        tiled=True,
    )
    returned = lax.all_to_all(
        summed.astype(jnp.bfloat16), "wave", split_axis=3, concat_axis=4, tiled=True
    )
    analysed = jnp.einsum(
        "lfrsj,sjn->flrsn", returned, legendre, preferred_element_type=jnp.float32
    )
    return jnp.where(kept_degrees, analysed, jnp.zeros_like(analysed)).astype(jnp.bfloat16)


def solution(mesh):
    in_specs = (P(None, "lev", None, "wave", None), P("wave", None, None), P())
    out_specs = P(None, "lev", None, "wave", None)
    return jax.shard_map(body, mesh=mesh, in_specs=in_specs, out_specs=out_specs, check_vma=False)
```
